512 devices in a mesh: dom: 128 (over z, y, core), feat: 4 (over x).
Axes of the slice: x: 4, y: 4, z: 16, core: 2. Of those that a mesh axis runs over, the one named last changes fastest.
Arguments:
- features: bfloat16 [65536, 768], P('dom', 'feat'), may hold values from -6 to 6
- w_self: bfloat16 [768, 1024], P(None, 'feat'), may hold values from -0.21875 to 0.21875
- w_neigh: bfloat16 [768, 1024], P(None, 'feat'), may hold values from -0.21875 to 0.21875
- out_bias: float32 [1024], P('feat'), may hold values from -3 to 3
- degrees: int32 [65536], P('dom'), may hold values from 1 to 16
- tile_index: int32 [128, 12, 2], P('dom'), may hold values from 0 to 3
- tile_mask: int32 [128, 12, 128, 128], P('dom'), may hold values 0 or 1
- cut_source: int32 [128, 128, 24], P('dom'), may hold values from 0 to 511
- cut_target: int32 [128, 128, 24], P('dom'), may hold values from -1 to 511, as said below
- hub_local: int32 [128, 4], P('dom'), may hold values from 0 to 511, as said below
- hub_source: int32 [128, 512], P('dom'), may hold values from 0 to 511
- hub_target: int32 [128, 512], P('dom'), may hold values from 0 to 511
- mirror_source: int32 [128, 512], P('dom'), may hold values from 0 to 511
- mirror_target: int32 [128, 512], P('dom'), may hold values from 0 to 511, as said below
Outputs:
- hidden: bfloat16 [65536, 1024], P('dom', 'feat')
The draws below stay inside these ranges and needn't reach their ends.
Inputs may be any that keep to these rules, and one draw needn't show every extreme that they name: `hub_local`: within each partition the 4 rows are distinct. `cut_target`: slots holding -1 come after the live ones of each pair; for every receiving partition some sending partition fills all 24 slots. `mirror_target`: of one partition's edges, at most 8 go into hubs of any one master partition, and for every partition some master receives exactly 8 of them.
All inputs are finite; a program needn't handle non-finite values. No bound on the sum of `tile_mask` on one device may be relied on, other than what follows from the above.
Results may differ from the reference program's by a relative error of at most 0.0044.
Values may be sent and summed in bfloat16 or wider, within the bound.
A program may use at most 64 MiB of HBM per device.

```python
import jax
import jax.numpy as jnp
from jax import lax

D = 768
H = 1024
NODE_DEV = 512
TILE = 128
TILES = 12
CAP = 24
HUB_DEV = 4
HUB_EDGES = 512
MIRROR_EDGES = 512
PARTS_SIZE = 128
NODES = 65536
BLOCKS = 4
HUBS = 512
MIRROR_CAP = 8


def draw_cut_target(key, part):
    key = jax.random.fold_in(key, 11)
    key_level, key_count, key_full, key_nodes = jax.random.split(key, 4)
    level = jax.random.randint(key_level, (PARTS_SIZE, 1), 1, 5)
    count = jax.random.randint(key_count, (PARTS_SIZE, PARTS_SIZE), 0, CAP * level // 4 + 1)
    full_peer = jax.random.randint(key_full, (PARTS_SIZE, 1), 0, PARTS_SIZE)
    peers = jnp.arange(PARTS_SIZE)[None, :]
    count = jnp.where(peers == full_peer, CAP, count)
    nodes = jax.random.randint(key_nodes, (PARTS_SIZE, PARTS_SIZE, CAP), 0, NODE_DEV)
    slots = jnp.arange(CAP)[None, None, :]
    return jnp.where(slots < count[:, :, None], nodes, -1).astype(jnp.int32)


def draw_hub_local(key, part):
    key = jax.random.fold_in(key, 23)
    keys = jax.random.split(key, PARTS_SIZE)
    picks = jax.vmap(lambda one_key: jax.random.permutation(one_key, NODE_DEV)[:HUB_DEV])(keys)
    return picks.astype(jnp.int32)


def mirror_row(one_key):
    key_full, key_order, key_shuffle, key_hub = jax.random.split(one_key, 4)
    total_slots = PARTS_SIZE * MIRROR_CAP
    full_master = jax.random.randint(key_full, (), 0, PARTS_SIZE)
    order = jax.random.permutation(key_order, total_slots).astype(jnp.int32)
    slot_master = (jnp.arange(total_slots, dtype=jnp.int32) // MIRROR_CAP).astype(jnp.int32)
    scores = order + jnp.where(slot_master == full_master, 0, total_slots).astype(jnp.int32)
    chosen = jnp.argsort(scores, stable=True)[:MIRROR_EDGES].astype(jnp.int32)
    chosen = jax.random.permutation(key_shuffle, chosen)
    masters = chosen // MIRROR_CAP
    within = jax.random.randint(key_hub, (MIRROR_EDGES,), 0, HUB_DEV)
    return (masters * HUB_DEV + within).astype(jnp.int32)


def draw_mirror_target(key, part):
    key = jax.random.fold_in(key, 37)
    keys = jax.random.split(key, PARTS_SIZE)
    return jax.vmap(mirror_row)(keys).astype(jnp.int32)


def plant(values, own_key, least, high):
    longest = values.shape.index(max(values.shape))
    spots = []
    for shift in (0, 1):
        where = [jax.random.randint(jax.random.fold_in(own_key, axis), (), 0, length) for axis, length in enumerate(values.shape)]
        where[longest] = (where[longest] + shift) % values.shape[longest]
        spots.append(tuple(where))
    return values.at[spots[0]].set(least).at[spots[1]].set(high)


def level_of(stream_key, extent, cuts, smallest, high):
    factor_of, own = 1.0, jax.random.fold_in(stream_key, 6)
    for dim, parts in cuts:
        draws = jnp.exp(jax.random.uniform(jax.random.fold_in(own, dim), (parts,), jnp.float32, smallest / len(cuts), high / len(cuts)))
        factor_of = factor_of * jnp.repeat(draws, extent[dim] // parts).reshape([-1 if axis == dim else 1 for axis in range(len(extent))])
    return factor_of


def bell_draw(own_key, shape, deviation, reach, shards=(), kind=jnp.bfloat16):
    drawn = deviation * jax.random.normal(own_key, shape, jnp.float32)
    if shards:
        drawn = drawn * level_of(own_key, shape, shards, -0.22, 0.18)
    return jnp.clip(drawn, -reach, reach).astype(kind)


def setup_inputs(seed: int = 0) -> dict:
    arg_keys = jax.random.split(jax.random.key(seed), 15)
    return {
        "features": bell_draw(arg_keys[0], (NODES, D), 1.0, 6.0, ((0, 128), (1, 4))),
        "w_self": bell_draw(arg_keys[1], (D, H), D ** -0.5, 0.21875, ((1, 4),)),
        "w_neigh": bell_draw(arg_keys[2], (D, H), D ** -0.5, 0.21875, ((1, 4),)),
        "out_bias": bell_draw(arg_keys[3], (H,), 0.5, 3.0, ((0, 4),), jnp.float32),
        "degrees": plant(jax.random.randint(arg_keys[4], (NODES,), 1, 17), jax.random.fold_in(arg_keys[4], 1), 1, 16).astype(jnp.int32),
        "tile_index": plant(jax.random.randint(arg_keys[5], (PARTS_SIZE, TILES, 2), 0, BLOCKS), jax.random.fold_in(arg_keys[5], 1), 0, BLOCKS - 1).astype(jnp.int32),
        "tile_mask": plant((jax.random.randint(arg_keys[6], (PARTS_SIZE, TILES, TILE, TILE), 0, 16) < 1).astype(jnp.int32), jax.random.fold_in(arg_keys[6], 1), 0, 1),
        "cut_source": plant(jax.random.randint(arg_keys[7], (PARTS_SIZE, PARTS_SIZE, CAP), 0, NODE_DEV), jax.random.fold_in(arg_keys[7], 1), 0, NODE_DEV - 1).astype(jnp.int32),
        "cut_target": draw_cut_target(jax.random.fold_in(arg_keys[14], 71), 0),
        "hub_local": draw_hub_local(jax.random.fold_in(arg_keys[14], 71), 0),
        "hub_source": plant(jax.random.randint(arg_keys[10], (PARTS_SIZE, HUB_EDGES), 0, HUBS), jax.random.fold_in(arg_keys[10], 1), 0, HUBS - 1).astype(jnp.int32),
        "hub_target": plant(jax.random.randint(arg_keys[11], (PARTS_SIZE, HUB_EDGES), 0, NODE_DEV), jax.random.fold_in(arg_keys[11], 1), 0, NODE_DEV - 1).astype(jnp.int32),
        "mirror_source": plant(jax.random.randint(arg_keys[12], (PARTS_SIZE, MIRROR_EDGES), 0, NODE_DEV), jax.random.fold_in(arg_keys[12], 1), 0, NODE_DEV - 1).astype(jnp.int32),
        "mirror_target": draw_mirror_target(jax.random.fold_in(arg_keys[14], 71), 0),
    }


def reference(features, w_self, w_neigh, out_bias, degrees, tile_index, tile_mask, cut_source, cut_target, hub_local, hub_source, hub_target, mirror_source, mirror_target):
    part_ids = jnp.arange(PARTS_SIZE, dtype=jnp.int32)
    hub_rows = (part_ids[:, None] * NODE_DEV + hub_local).astype(jnp.int32).reshape(-1)
    hub_table = jnp.take(features, hub_rows, axis=0).astype(jnp.float32)
    mirror_rows = (part_ids[:, None] * NODE_DEV + mirror_source).astype(jnp.int32).reshape(-1)
    mirror_vals = jnp.take(features, mirror_rows, axis=0).astype(jnp.float32)
    mirror_sum = jax.ops.segment_sum(mirror_vals, mirror_target.reshape(-1), HUBS)

    def one_part(part):
        start = (part * NODE_DEV).astype(jnp.int32)
        own = lax.dynamic_slice_in_dim(features, start, NODE_DEV, 0)
        blocks = own.reshape(BLOCKS, TILE, D).astype(jnp.float32)
        index_here = tile_index[part]
        picked = jnp.take(blocks, index_here[:, 1], axis=0)
        masks = tile_mask[part].astype(jnp.float32)
        products = jnp.einsum("tuv,tvc->tuc", masks, picked, precision=lax.Precision.HIGHEST)
        owners = (index_here[:, 0][:, None] == jnp.arange(BLOCKS, dtype=jnp.int32)[None, :]).astype(jnp.float32)
        local_sum = jnp.einsum("tb,tuc->buc", owners, products, precision=lax.Precision.HIGHEST).reshape(NODE_DEV, D)
        sources = jnp.take(cut_source, part, axis=1)
        source_rows = (part_ids[:, None] * NODE_DEV + sources).astype(jnp.int32).reshape(-1)
        arrived = jnp.take(features, source_rows, axis=0).astype(jnp.float32)
        targets = cut_target[part].reshape(-1)
        slots = jnp.where(targets < 0, NODE_DEV, targets).astype(jnp.int32)
        cut_sum = jax.ops.segment_sum(arrived, slots, NODE_DEV + 1)[:NODE_DEV]
        hub_vals = jnp.take(hub_table, hub_source[part], axis=0)
        hub_sum = jax.ops.segment_sum(hub_vals, hub_target[part], NODE_DEV)
        mine = lax.dynamic_slice_in_dim(mirror_sum, (part * HUB_DEV).astype(jnp.int32), HUB_DEV, 0)
        master = jnp.zeros((NODE_DEV, D), jnp.float32).at[hub_local[part]].add(mine)
        degree_here = lax.dynamic_slice_in_dim(degrees, start, NODE_DEV, 0).astype(jnp.float32)
        mean_rows = ((local_sum + cut_sum + hub_sum + master) / degree_here[:, None]).astype(jnp.bfloat16)
        total = jnp.dot(own, w_self, preferred_element_type=jnp.float32) + jnp.dot(mean_rows, w_neigh, preferred_element_type=jnp.float32)
        return jax.nn.relu(total + out_bias[None, :]).astype(jnp.bfloat16)

    result = lax.map(one_part, part_ids)
    return result.reshape(NODES, H)
```

```python
import jax
import jax.numpy as jnp
from jax import lax
from jax.sharding import PartitionSpec as P


def on_device(features, w_self, w_neigh, out_bias, degrees, tile_index, tile_mask, cut_source, cut_target,
              hub_local, hub_source, hub_target, mirror_source, mirror_target):
    bf16, f32 = jnp.bfloat16, jnp.float32
    nodes, columns = features.shape
    parts, cap = cut_source.shape[1:]
    tile = tile_mask.shape[2]
    blocks = nodes // tile
    hub_dev = hub_local.shape[1]
    hubs = parts * hub_dev
    node_ids = jnp.arange(nodes, dtype=jnp.int32)
    hub_ids = jnp.arange(hubs, dtype=jnp.int32)
    dot = lambda a, b: jnp.dot(a, b, preferred_element_type=f32)

    take_cut = (cut_source[0].reshape(-1)[:, None] == node_ids[None, :]).astype(bf16)
    outgoing = dot(take_cut, features).astype(bf16).reshape(parts, cap, columns)
    own_hubs = dot((hub_local[0][:, None] == node_ids[None, :]).astype(bf16), features).astype(bf16)
    mirror_to = (hub_ids[:, None] == mirror_target[0][None, :]).astype(bf16)
    mirror_from = (mirror_source[0][:, None] == node_ids[None, :]).astype(bf16)
    partial = dot(dot(mirror_to, mirror_from).astype(bf16), features).astype(bf16).reshape(parts, hub_dev, columns)
    message = jnp.concatenate(
        [outgoing, jnp.broadcast_to(own_hubs[None], (parts, hub_dev, columns)), partial], axis=1)
    arrived = lax.all_to_all(message, "dom", split_axis=0, concat_axis=0, tiled=True)
    all_features = lax.all_gather(features, "feat", axis=1, tiled=True)
    carry = dot(all_features, w_self)

    cut_to = (node_ids[:, None, None] == cut_target[0][None]).astype(bf16)
    hub_to = dot((node_ids[:, None] == hub_target[0][None, :]).astype(bf16),
                 (hub_source[0][:, None] == hub_ids[None, :]).astype(bf16)).astype(bf16).reshape(nodes, parts, hub_dev)
    master_to = jnp.broadcast_to((node_ids[:, None] == hub_local[0][None, :]).astype(bf16)[:, None], hub_to.shape)
    place = jnp.concatenate([cut_to, hub_to, master_to], axis=2).reshape(nodes, -1)

    row_is = (tile_index[0, :, 0][:, None] == jnp.arange(blocks)[None, :]).astype(f32)
    col_is = (tile_index[0, :, 1][:, None] == jnp.arange(blocks)[None, :]).astype(f32)
    adjacency = jnp.einsum("tr,tc,tuv->rucv", row_is, col_is, tile_mask[0].astype(f32)).reshape(nodes, nodes)
    total = dot(adjacency.astype(bf16), features) + dot(place, arrived.reshape(-1, columns))
    mean_rows = (total / degrees.astype(f32)[:, None]).astype(bf16)
    out = carry + dot(lax.all_gather(mean_rows, "feat", axis=1, tiled=True), w_neigh)
    return jax.nn.relu(out + out_bias[None, :]).astype(bf16)


def solution(mesh):
    return jax.shard_map(
        on_device,
        mesh=mesh,
        in_specs=(P("dom", "feat"), P(None, "feat"), P(None, "feat"), P("feat"), P("dom"), P("dom"), P("dom"), P("dom"),
                  P("dom"), P("dom"), P("dom"), P("dom"), P("dom"), P("dom")),
        out_specs=P("dom", "feat"),
        check_vma=False,
    )
```

```python
import functools

import jax
import jax.numpy as jnp
from jax import lax
from jax.experimental import pallas as pl
from jax.experimental.pallas import tpu as pltpu
from jax.sharding import PartitionSpec as P

MESH = pl.DeviceIdType.MESH
BF16, F32, I32 = jnp.bfloat16, jnp.float32, jnp.int32
PLANE = 8
SLOTS = 32
ROWS = 816
PIECES, PIECE = 3, 272
CUT = 416
SHIFT = 256


def dot(a, b):
    return jnp.dot(a, b, preferred_element_type=F32)


def dot_nt(a, b):
    return lax.dot_general(a, b, (((1,), (1,)), ((), ())), preferred_element_type=F32)


def iota(shape, axis):
    return lax.broadcasted_iota(I32, shape, axis)


def hot(mask):
    return jnp.where(mask, 1.0, 0.0).astype(BF16)


def column(row):
    return jnp.transpose(jnp.broadcast_to(row, (128, 128)))


def kernel(rings, feats, item, feat, tidx, tgt, hub_at, hub_t, hub_s, deg, bias, mask_hbm, ws_hbm, wn_hbm, out,
           ring, ysend, yrecv, xf, xm, accp, accm, accl, msum, hub_hot, mask, ws, wn, wfold, carry,
           zs, zr, ys, yr, fs, fr, ms, mr, local):
    half = rings // 2
    dom, x = lax.axis_index("dom"), lax.axis_index("feat")
    z, me = dom // PLANE, dom % PLANE
    up, down = ((z + 1) % rings) * PLANE + me, ((z + rings - 1) % rings) * PLANE + me

    loads = [pltpu.make_async_copy(src, dst, local.at[i])
             for i, (src, dst) in enumerate(((mask_hbm, mask), (ws_hbm, ws), (wn_hbm, wn)))]
    for load in loads:
        load.start()

    barrier = pltpu.get_barrier_semaphore()
    for dev in (up, down):
        pl.semaphore_signal(barrier, inc=1, device_id=(dev, x), device_id_type=MESH)
    for o in range(1, PLANE):
        pl.semaphore_signal(barrier, inc=1, device_id=(z * PLANE + (me + o) % PLANE, x), device_id_type=MESH)
    for o in range(1, feats):
        pl.semaphore_signal(barrier, inc=1, device_id=(dom, (x + o) % feats), device_id_type=MESH)
    pl.semaphore_wait(barrier, 2 + PLANE - 1 + feats - 1)

    def zcopy(way, step, piece, src):
        slot = (z + rings - step) % rings if way == 0 else (z + step) % rings
        rows = pl.ds(piece * PIECE, PIECE)
        return pltpu.make_async_remote_copy(
            src_ref=src.at[rows] if src is not None else ring.at[slot, rows], dst_ref=ring.at[slot, rows],
            send_sem=zs.at[way, step, piece], recv_sem=zr.at[slot, piece],
            device_id=(up if way == 0 else down, x), device_id_type=MESH)

    def zlast(way):
        step = half - 1
        slot = (z + rings - step) % rings if way == 0 else (z + step) % rings
        rows = pl.ds(0, CUT) if way == 0 else pl.ds(CUT, ROWS - CUT)
        return pltpu.make_async_remote_copy(
            src_ref=ring.at[slot, rows], dst_ref=ring.at[slot, rows],
            send_sem=zs.at[way, step, 0], recv_sem=zr.at[slot, way],
            device_id=(up if way == 0 else down, x), device_id_type=MESH)

    def zarrived(way, step, piece):
        slot = (z + rings - step) % rings if way == 0 else (z + step) % rings
        rows = pl.ds(piece * PIECE, PIECE)
        pltpu.make_async_remote_copy(
            src_ref=ring.at[slot, rows], dst_ref=ring.at[slot, rows], send_sem=zs.at[way, 0, piece],
            recv_sem=zr.at[slot, piece], device_id=(up, x), device_id_type=MESH).wait_recv()

    def zlast_arrived(way):
        slot = (z + half) % rings
        rows = pl.ds(0, CUT) if way == 0 else pl.ds(CUT, ROWS - CUT)
        pltpu.make_async_remote_copy(
            src_ref=ring.at[slot, rows], dst_ref=ring.at[slot, rows], send_sem=zs.at[way, 0, 0],
            recv_sem=zr.at[slot, way], device_id=(up, x), device_id_type=MESH).wait_recv()

    def ycopy(step, o, rows):
        dest = (me + o) % PLANE
        return pltpu.make_async_remote_copy(
            src_ref=ysend.at[step, dest, pl.ds(0, rows)], dst_ref=yrecv.at[step, me, pl.ds(0, rows)],
            send_sem=ys.at[step, o - 1], recv_sem=yr.at[step, me],
            device_id=(z * PLANE + dest, x), device_id_type=MESH)

    def yarrived(step, rows):
        for o in range(1, PLANE):
            src = (me + o) % PLANE
            pltpu.make_async_remote_copy(
                src_ref=ysend.at[step, src, pl.ds(0, rows)], dst_ref=yrecv.at[step, src, pl.ds(0, rows)],
                send_sem=ys.at[step, o - 1], recv_sem=yr.at[step, src],
                device_id=(z * PLANE + src, x), device_id_type=MESH).wait_recv()

    def xcopy(buf, send, recv, o):
        return pltpu.make_async_remote_copy(
            src_ref=buf.at[x], dst_ref=buf.at[x], send_sem=send.at[o - 1], recv_sem=recv.at[x],
            device_id=(dom, (x + o) % feats), device_id_type=MESH)

    def xarrived(buf, send, recv, o):
        src = (x + o) % feats
        pltpu.make_async_remote_copy(
            src_ref=buf.at[src], dst_ref=buf.at[src], send_sem=send.at[o - 1], recv_sem=recv.at[src],
            device_id=(dom, src), device_id_type=MESH).wait_recv()

    def select(ref):
        ids = ref[768:800, :].astype(F32)
        row = iota((32, 128), 0)
        cols = [column(jnp.sum(jnp.where(row == 2 * z + i, ids, 0.0), axis=0, keepdims=True)) for i in (0, 1)]
        lane = iota((128, 128), 1).astype(F32) - SHIFT
        blocks = [jnp.concatenate([hot(c == lane + 128.0 * b) for c in cols], axis=0) for b in range(4)]
        edges = ref[800:816, :].astype(F32)
        hub = (iota((32, 128), 0) + z * 32 - SHIFT).astype(F32)
        node = (iota((512, 128), 0) - SHIFT).astype(F32)
        to = jnp.concatenate([hot(hub == edges[4 + c:5 + c, :]) for c in range(4)], axis=1)
        fro = jnp.concatenate([hot(node == edges[c:c + 1, :]) for c in range(4)], axis=1)
        count = dot_nt(to, fro).astype(BF16)
        fold = ref[512:768, :]
        got = []
        for i in (0, 1):
            left = jnp.concatenate(
                [jnp.concatenate(blocks[2 * i:2 * i + 2], axis=1), count[:, 256 * i:256 * i + 256]], axis=0)
            right = jnp.concatenate([ref[256 * i:256 * i + 256, :], fold], axis=1)
            part = dot(left, right)
            msum[i] += part[256:288, :]
            got.append(part[:256, :])
        return got

    low = iota((256, 128), 1) < 64

    def put(step, way, got):
        ysend[step, :, 64 * way:64 * way + 32, :] = (got[0][:, :128] + got[1][:, :128]).astype(BF16).reshape(
            PLANE, SLOTS, 128)
        if way == 0:
            tail = jnp.where(low, got[0][:, 128:] + pltpu.roll(got[1][:, 128:], 64, 1), 0.0)
        else:
            before = ysend[step, :, 32:64, :].reshape(256, 128).astype(F32)
            tail = jnp.where(low, before, got[1][:, 128:] + pltpu.roll(got[0][:, 128:], 64, 1))
        ysend[step, :, 32:64, :] = tail.astype(BF16).reshape(PLANE, SLOTS, 128)

    def send(step, rows):
        for o in (4, 5, 3, 2, 6, 1, 7):
            ycopy(step, o, rows).start()
        yrecv[step, me, 0:rows, :] = ysend[step, me, 0:rows, :]

    def place(step, way, last=False):
        zz = (z + rings - step) % rings if way == 0 else (z + step) % rings
        to = tgt[zz]
        if last:
            to = jnp.where((iota((1, 256), 1) % SLOTS) >= 28, hub_at[...], to)
        node = iota((512, 256), 0)
        pos = iota((256, 512), 0)
        slot = pos % SLOTS
        hub = jnp.where((slot >= 24) & (slot < 28), zz * 32 + (pos // SLOTS) * 4 + slot - 24, -1)
        where = dot_nt(hub_hot[...], hot(hub == hub_s[...]))
        where = (where + jnp.where(node == to, 1.0, 0.0)).astype(BF16)
        rows = jnp.concatenate([yrecv[step, :, 64 * way:64 * way + 32, :].reshape(256, 128),
                                yrecv[step, :, 32:64, :].reshape(256, 128)], axis=1)
        acc = accp if way == 0 else accm
        acc[...] += dot(where, rows)

    def product(buf, which):
        tops = bots = None
        for i in range(feats):
            fold = buf[i, 512:768, :]
            top = dot(jnp.concatenate([buf[i, 0:256, :], fold], axis=1), wfold[which, i, 0])
            bot = dot(jnp.concatenate([buf[i, 256:512, :], fold], axis=1), wfold[which, i, 1])
            tops, bots = (top, bot) if tops is None else (tops + top, bots + bot)
        return tops, bots

    for piece in range(PIECES):
        zcopy(0, 0, piece, item).start()
        zcopy(1, 0, piece, item).start()
    xf[x] = item[0:768, :]
    for o in range(1, feats):
        xcopy(xf, fs, fr, o).start()

    accp[...] = jnp.zeros_like(accp)
    accm[...] = jnp.zeros_like(accm)
    accl[...] = jnp.zeros_like(accl)
    msum[...] = jnp.zeros_like(msum)
    hub_hot[...] = hot(iota((512, 512), 0) == hub_t[...])

    ysend[0, :, 64:96, :] = jnp.zeros((PLANE, SLOTS, 128), BF16)
    put(0, 0, select(item))
    send(0, 96)

    for piece in range(PIECES):
        for way in (0, 1):
            zarrived(way, 1, piece)
            if half > 2:
                zcopy(way, 1, piece, None).start()
    if half == 2:
        zlast(0).start()
        zlast(1).start()

    for load in loads:
        load.wait()

    def tile(t, _):
        at = tidx[pl.ds(t, 1), :]
        is_at = [[(at[:, i:i + 1] == b).astype(F32) for b in range(4)] for i in (0, 1)]
        block = sum(feat[128 * b:128 * b + 128, :].astype(F32) * is_at[1][b] for b in range(4)).astype(BF16)
        part = dot(mask[t].astype(F32).astype(BF16), block)
        for b in range(4):
            accl[128 * b:128 * b + 128, 0:192] += part * is_at[0][b]
        return 0

    lax.fori_loop(0, 12, tile, 0)

    for which, w in enumerate((ws, wn)):
        for i in range(feats):
            a, b, zero = w[192 * i:192 * i + 128, :], w[192 * i + 128:192 * i + 192, :], jnp.zeros((64, 256), BF16)
            wfold[which, i, 0] = jnp.concatenate([a, b, zero], axis=0)
            wfold[which, i, 1] = jnp.concatenate([a, zero, b], axis=0)

    def step(k, _):
        for way in (0, 1):
            zarrived(way, k, 0)
            zcopy(way, k, 0, None).start()
        put(k - 1, 0, select(ring.at[(z + rings - k + 1) % rings]))
        for way in (0, 1):
            zarrived(way, k, 1)
            zcopy(way, k, 1, None).start()
        put(k - 1, 1, select(ring.at[(z + k - 1) % rings]))
        send(k - 1, 96)
        for way in (0, 1):
            zarrived(way, k, 2)
            zcopy(way, k, 2, None).start()
        yarrived(k - 2, 96)
        place(k - 2, 0)
        place(k - 2, 1)
        return 0

    lax.fori_loop(2, half - 1, step, 0)
    k = half - 1
    if half > 2:
        for way in (0, 1):
            zarrived(way, k, 0)
            zarrived(way, k, 1)
        zlast(0).start()
        for way in (0, 1):
            zarrived(way, k, 2)
        zlast(1).start()
        put(k - 1, 0, select(ring.at[(z + rings - k + 1) % rings]))
        put(k - 1, 1, select(ring.at[(z + k - 1) % rings]))
        send(k - 1, 96)
    put(k, 0, select(ring.at[(z + rings - k) % rings]))
    put(k, 1, select(ring.at[(z + k) % rings]))
    send(k, 96)
    if half > 2:
        yarrived(k - 2, 96)
        place(k - 2, 0)
        place(k - 2, 1)
    yarrived(k - 1, 96)
    place(k - 1, 0)
    place(k - 1, 1)
    for o in range(1, feats):
        xarrived(xf, fs, fr, o)
    top, bot = product(xf, 0)
    carry[0:256, :] = top + bias[...]
    carry[256:512, :] = bot + bias[...]

    zlast_arrived(0)
    zlast_arrived(1)
    got = select(ring.at[(z + half) % rings])
    row, col = iota((256, 32), 0), iota((256, 32), 1)
    spread = hot((row // SLOTS == col // 4) & (row % SLOTS == 28 + col % 4))
    got = [part + dot(spread, msum[i].astype(BF16)) for i, part in enumerate(got)]
    put(half, 0, got)
    send(half, 64)
    yarrived(k, 96)
    place(k, 0)
    place(k, 1)
    yarrived(half, 64)
    place(half, 0, last=True)

    degree = deg[...].astype(F32)
    degree = jnp.concatenate([column(degree[i:i + 1, :]) for i in range(4)], axis=0)
    lead = (accp[:, 0:128] + accm[:, 0:128] + accl[:, 0:128]) / degree
    rest = (accp[:, 128:256] + pltpu.roll(accm[:, 128:256], 64, 1) + accl[:, 128:256]) / degree
    xm[x, 0:512, :] = lead.astype(BF16)
    xm[x, 512:768, :] = jnp.where(low, rest[0:256, :], pltpu.roll(rest[256:512, :], 64, 1)).astype(BF16)
    for o in range(1, feats):
        xcopy(xm, ms, mr, o).start()
    for o in range(1, feats):
        xarrived(xm, ms, mr, o)
    top, bot = product(xm, 1)
    out[0:256, :] = jnp.maximum(carry[0:256, :] + top, 0.0).astype(BF16)
    out[256:512, :] = jnp.maximum(carry[256:512, :] + bot, 0.0).astype(BF16)

    for way in (0, 1):
        for s in range(half - 1):
            for piece in range(PIECES):
                zcopy(way, s, piece, item if s == 0 else None).wait_send()
        zlast(way).wait_send()
    for o in range(1, PLANE):
        for s in range(half):
            ycopy(s, o, 96).wait_send()
        ycopy(half, o, 64).wait_send()
    for o in range(1, feats):
        xcopy(xf, fs, fr, o).wait_send()
        xcopy(xm, ms, mr, o).wait_send()


def on_device(rings, feats, features, w_self, w_neigh, out_bias, degrees, tile_index, tile_mask, cut_source, cut_target,
              hub_local, hub_source, hub_target, mirror_source, mirror_target):
    parts = rings * PLANE
    half = rings // 2
    fold = jnp.concatenate([features[0:256, 128:], features[256:, 128:]], axis=1)
    ids = jnp.concatenate([cut_source[0], jnp.broadcast_to(hub_local, (parts, 4)), jnp.full((parts, 4), 640, I32)], axis=1)
    ids = jnp.concatenate([ids.reshape(-1, 128), jnp.full((32 - parts // 4, 128), 640, I32),
                           mirror_source.reshape(4, 128), mirror_target.reshape(4, 128), jnp.full((8, 128), 640, I32)], axis=0)
    item = jnp.concatenate([features[:, :128], fold, (ids - SHIFT).astype(BF16)], axis=0)
    tgt = jnp.concatenate([cut_target[0], jnp.full((parts, 8), -1, I32)], axis=1).reshape(rings, 1, 256)
    hub_at = jnp.tile(jnp.tile(hub_local, (1, 8)), (1, PLANE))
    vmem, anywhere = pl.BlockSpec(memory_space=pltpu.VMEM), pl.BlockSpec(memory_space=pl.ANY)
    return pl.pallas_call(
        functools.partial(kernel, rings, feats),
        out_shape=jax.ShapeDtypeStruct((512, 256), BF16),
        in_specs=[vmem] * 9 + [anywhere] * 3,
        out_specs=vmem,
        scratch_shapes=[
            pltpu.VMEM((rings, ROWS, 128), BF16),
            pltpu.VMEM((half + 1, PLANE, 96, 128), BF16),
            pltpu.VMEM((half + 1, PLANE, 96, 128), BF16),
            pltpu.VMEM((feats, 768, 128), BF16),
            pltpu.VMEM((feats, 768, 128), BF16),
            pltpu.VMEM((512, 256), F32),
            pltpu.VMEM((512, 256), F32),
            pltpu.VMEM((512, 256), F32),
            pltpu.VMEM((2, 32, 256), F32),
            pltpu.VMEM((512, 512), BF16),
            pltpu.VMEM((12, 128, 128), I32),
            pltpu.VMEM((192 * feats, 256), BF16),
            pltpu.VMEM((192 * feats, 256), BF16),
            pltpu.VMEM((2, feats, 2, 256, 256), BF16),
            pltpu.VMEM((512, 256), F32),
            pltpu.SemaphoreType.DMA((2, half, PIECES)),
            pltpu.SemaphoreType.DMA((rings, PIECES)),
            pltpu.SemaphoreType.DMA((half + 1, PLANE)),
            pltpu.SemaphoreType.DMA((half + 1, PLANE)),
            pltpu.SemaphoreType.DMA((4,)),
            pltpu.SemaphoreType.DMA((4,)),
            pltpu.SemaphoreType.DMA((4,)),
            pltpu.SemaphoreType.DMA((4,)),
            pltpu.SemaphoreType.DMA((3,)),
        ],
        compiler_params=pltpu.CompilerParams(
            collective_id=0, has_side_effects=True, vmem_limit_bytes=40 * 1024 * 1024),
        cost_estimate=pl.CostEstimate(flops=10**10, bytes_accessed=4 * 10**6, transcendentals=0),
    )(item, features, tile_index[0], tgt, hub_at, hub_target, hub_source, degrees.reshape(4, 128), out_bias.reshape(1, 256),
      tile_mask[0], w_self, w_neigh)


def solution(mesh):
    return jax.shard_map(
        functools.partial(on_device, mesh.shape["dom"] // PLANE, mesh.shape["feat"]),
        mesh=mesh,
        in_specs=(P("dom", "feat"), P(None, "feat"), P(None, "feat"), P("feat"), P("dom"), P("dom"), P("dom"), P("dom"),
                  P("dom"), P("dom"), P("dom"), P("dom"), P("dom"), P("dom")),
        out_specs=P("dom", "feat"),
        check_vma=False,
    )
```

```python
import functools

import jax
import jax.numpy as jnp
from jax import lax
from jax.experimental import pallas as pl
from jax.experimental.pallas import tpu as pltpu
from jax.sharding import PartitionSpec as P

MESH = pl.DeviceIdType.MESH
BF16, F32, I32 = jnp.bfloat16, jnp.float32, jnp.int32
PLANE = 8
SLOTS = 32
WIDTH = 192
PIECES, PIECE = 6, 32
IDS = 48
SHIFT = 256


def dot(a, b):
    return jnp.dot(a, b, preferred_element_type=F32)


def dot_nt(a, b):
    return lax.dot_general(a, b, (((1,), (1,)), ((), ())), preferred_element_type=F32)


def iota(shape, axis):
    return lax.broadcasted_iota(I32, shape, axis)


def hot(mask):
    return jnp.where(mask, 1.0, 0.0).astype(BF16)


def column(row):
    return jnp.transpose(jnp.broadcast_to(row, (128, 128)))


def dot_tn(a, b):
    return lax.dot_general(a, b, (((0,), (0,)), ((), ())), preferred_element_type=F32)


def kernel(rings, feats, ft_hbm, cs_hbm, ct_hbm, ti_hbm, hl_hbm, ht_hbm, hs_hbm, mf_hbm, mt_hbm, deg_hbm, bias_hbm,
           mask_hbm, ws_hbm, wn_hbm, out, ring, ringi, ysend, yrecv, xf, xm, accp, accm, accl, msum, hub_hot, wfold, carry,
           own, tgt, raw, ft, cs, ct, tidx, hub_local, hub_t, hub_s, mirror_f, mirror_t, deg, bias, mask, ws, wn,
           zs, zr, ys, yr, fs, fr, ms, mr, local):
    half = rings // 2
    dom, x = lax.axis_index("dom"), lax.axis_index("feat")
    z, me = dom // PLANE, dom % PLANE
    up, down = ((z + 1) % rings) * PLANE + me, ((z + rings - 1) % rings) * PLANE + me

    barrier = pltpu.get_barrier_semaphore()
    for dev in (up, down):
        pl.semaphore_signal(barrier, inc=1, device_id=(dev, x), device_id_type=MESH)
    for o in range(1, PLANE):
        pl.semaphore_signal(barrier, inc=1, device_id=(z * PLANE + (me + o) % PLANE, x), device_id_type=MESH)
    for o in range(1, feats):
        pl.semaphore_signal(barrier, inc=1, device_id=(dom, (x + o) % feats), device_id_type=MESH)

    loads = [pltpu.make_async_copy(src, dst, local.at[i]) for i, (src, dst) in enumerate((
        (cs_hbm, cs), (hl_hbm, hub_local), (mf_hbm, mirror_f), (mt_hbm, mirror_t), (ft_hbm, ft), (ct_hbm, ct), (ti_hbm, tidx),
        (ht_hbm, hub_t), (hs_hbm, hub_s), (deg_hbm, deg), (bias_hbm, bias), (mask_hbm, mask), (ws_hbm, ws), (wn_hbm, wn)))]
    for load in loads:
        load.start()

    def at(way, step):
        return (z + rings - step) % rings if way == 0 else (z + step) % rings

    def zcopy(way, step, piece):
        slot = at(way, step)
        if piece == PIECES:
            src, dst = own if isinstance(step, int) and step == 0 else ringi.at[slot], ringi.at[slot]
        else:
            rows = pl.ds(piece * PIECE, PIECE)
            src = ft_hbm.at[rows] if isinstance(step, int) and step == 0 else ring.at[slot, rows]
            dst = ring.at[slot, rows]
        return pltpu.make_async_remote_copy(
            src_ref=src, dst_ref=dst, send_sem=zs.at[way, step, piece], recv_sem=zr.at[slot, piece],
            device_id=(up if way == 0 else down, x), device_id_type=MESH)

    def zarrived(way, step, piece):
        slot = at(way, step)
        ref = ringi.at[slot] if piece == PIECES else ring.at[slot, pl.ds(piece * PIECE, PIECE)]
        pltpu.make_async_remote_copy(
            src_ref=ref, dst_ref=ref, send_sem=zs.at[way, 0, piece], recv_sem=zr.at[slot, piece],
            device_id=(up, x), device_id_type=MESH).wait_recv()

    order = (PIECES,) + tuple(range(PIECES))
    last = ((PIECES,) + tuple(range(PIECES // 2)), tuple(range(PIECES // 2, PIECES)))

    def forward(step, pieces):
        for piece in pieces:
            for way in (0, 1):
                zarrived(way, step, piece)
                zcopy(way, step, piece).start()

    def ycopy(step, o, rows):
        dest = (me + o) % PLANE
        return pltpu.make_async_remote_copy(
            src_ref=ysend.at[step, dest, pl.ds(0, rows)], dst_ref=yrecv.at[step, me, pl.ds(0, rows)],
            send_sem=ys.at[step, o - 1], recv_sem=yr.at[step, me],
            device_id=(z * PLANE + dest, x), device_id_type=MESH)

    def yarrived(step, rows):
        for o in range(1, PLANE):
            src = (me + o) % PLANE
            pltpu.make_async_remote_copy(
                src_ref=ysend.at[step, src, pl.ds(0, rows)], dst_ref=yrecv.at[step, src, pl.ds(0, rows)],
                send_sem=ys.at[step, o - 1], recv_sem=yr.at[step, src],
                device_id=(z * PLANE + src, x), device_id_type=MESH).wait_recv()

    def fcopy(o):
        return pltpu.make_async_remote_copy(
            src_ref=ft_hbm, dst_ref=xf.at[x], send_sem=fs.at[o - 1], recv_sem=fr.at[x],
            device_id=(dom, (x + o) % feats), device_id_type=MESH)

    def farrived(o):
        src = (x + o) % feats
        pltpu.make_async_remote_copy(
            src_ref=ft_hbm, dst_ref=xf.at[src], send_sem=fs.at[o - 1], recv_sem=fr.at[src],
            device_id=(dom, src), device_id_type=MESH).wait_recv()

    def mcopy(src, part, o, sem):
        rows = pl.ds(384 * part, 384)
        return pltpu.make_async_remote_copy(
            src_ref=xm.at[src, rows], dst_ref=xm.at[src, rows], send_sem=ms.at[sem], recv_sem=mr.at[src, part],
            device_id=(dom, (x + o + feats) % feats), device_id_type=MESH)

    def marrived(o, part):
        mcopy((x + o + feats) % feats, part, 1, 0).wait_recv()

    def select(ref, idref):
        ids = pltpu.roll(idref[0:32, :].astype(F32), (128 - PLANE * z) % 128, 1)
        lane = iota((32, 512), 1).astype(F32) - SHIFT
        pick = [hot(ids[:, d:d + 1] == lane) for d in range(PLANE)]
        edges = idref[32:48, :].astype(F32)
        hub = (iota((32, 128), 0) + z * 32 - SHIFT).astype(F32)
        node = (iota((512, 128), 0) - SHIFT).astype(F32)
        to = jnp.concatenate([hot(hub == edges[4 + c:5 + c, :]) for c in range(4)], axis=1)
        fro = jnp.concatenate([hot(node == edges[c:c + 1, :]) for c in range(4)], axis=1)
        got = dot_nt(jnp.concatenate(pick + [dot_nt(to, fro).astype(BF16)], axis=0), ref[...])
        msum[:, 0:WIDTH] += got[256:288, :]
        return got[0:256, :]

    def widen(tail):
        return jnp.concatenate([tail, jnp.zeros_like(tail)], axis=1)

    low = iota((256, 128), 1) < 64

    def put(step, way, got):
        ysend[step, :, 64 * way:64 * way + 32, :] = got[:, :128].astype(BF16).reshape(PLANE, SLOTS, 128)
        tail = widen(got[:, 128:])
        if way == 1:
            tail = ysend[step, :, 32:64, :].reshape(256, 128).astype(F32) + pltpu.roll(tail, 64, 1)
        ysend[step, :, 32:64, :] = tail.astype(BF16).reshape(PLANE, SLOTS, 128)

    def pick(step, way):
        slot = at(way, step)
        put(step, way, select(ring.at[slot], ringi.at[slot]))

    def send(step, rows):
        for o in (4, 5, 3, 2, 6, 1, 7):
            ycopy(step, o, rows).start()
        yrecv[step, me, 0:rows, :] = ysend[step, me, 0:rows, :]

    def place(step, way, last=False):
        zz = at(way, step)
        to = tgt[pl.ds(zz, 1), :]
        lane = iota((1, 256), 1) % SLOTS
        if last:
            for j in range(4):
                to = jnp.where(lane == 28 + j, hub_local[0:1, j:j + 1].astype(F32), to)
        pos = iota((256, 512), 0)
        slot = pos % SLOTS
        hub = jnp.where((slot >= 24) & (slot < 28), zz * 32 + (pos // SLOTS) * 4 + slot - 24, -1)
        where = dot_nt(hub_hot[...], hot(hub == hub_s[...]))
        where = (where + jnp.where(iota((512, 256), 0).astype(F32) == to, 1.0, 0.0)).astype(BF16)
        rows = jnp.concatenate([yrecv[step, :, 64 * way:64 * way + 32, :].reshape(256, 128),
                                yrecv[step, :, 32:64, :].reshape(256, 128)], axis=1)
        acc = accp if way == 0 else accm
        acc[...] += dot(where, rows)

    def product(i):
        fold = xm[i, 512:768, :]
        carry[0:256, :] += dot(jnp.concatenate([xm[i, 0:256, :], fold], axis=1), wfold[i, 0])
        carry[256:512, :] += dot(jnp.concatenate([xm[i, 256:512, :], fold], axis=1), wfold[i, 1])

    for load in loads[:4]:
        load.wait()
    raw[0:24, :] = (cs[...] - SHIFT).astype(F32)
    row = iota((8, 128), 0)
    hubs = jnp.full((8, 128), 640, I32)
    for j in range(4):
        hubs = jnp.where(row == j, hub_local[0:1, j:j + 1], hubs)
    raw[24:32, :] = (hubs - SHIFT).astype(F32)
    raw[32:36, :] = (mirror_f[...] - SHIFT).astype(F32)
    raw[36:40, :] = (mirror_t[...] - SHIFT).astype(F32)
    raw[40:48, :] = jnp.zeros((8, 128), F32)
    own[...] = raw[...].astype(BF16)

    pl.semaphore_wait(barrier, 2 + PLANE - 1 + feats - 1)
    for piece in order:
        for way in (0, 1):
            zcopy(way, 0, piece).start()
    for o in range(1, feats):
        fcopy(o).start()

    for load in loads[4:]:
        load.wait()
    accp[...] = jnp.zeros_like(accp)
    accm[...] = jnp.zeros_like(accm)
    accl[...] = jnp.zeros_like(accl)
    msum[...] = jnp.zeros_like(msum)

    ysend[0, :, 64:96, :] = jnp.zeros((PLANE, SLOTS, 128), BF16)
    put(0, 0, select(ft, own))
    send(0, 96)

    raw[0:24, :] = ct[...].astype(F32)
    raw[24:48, :] = jnp.full((24, 128), -1.0, F32)
    wide = jnp.transpose(jnp.concatenate([raw[0:32, :], jnp.full((96, 128), -1.0, F32)], axis=0))
    wide = wide[0:rings * PLANE, :].reshape(rings, PLANE, 128)
    lane = iota((rings, 128), 1)
    for part in (0, 1):
        whole = jnp.full((rings, 128), -1.0, F32)
        for d in range(4):
            one = wide[:, 4 * part + d, :]
            whole = jnp.where(lane // SLOTS == d, pltpu.roll(one, SLOTS * d, 1) if d else one, whole)
        tgt[:, 128 * part:128 * part + 128] = whole
    hub_hot[...] = hot(iota((512, 512), 0) == hub_t[...])

    if half > 2:
        forward(1, order)
    else:
        for piece in order:
            for way in (0, 1):
                zarrived(way, 1, piece)
        for way in (0, 1):
            for piece in last[way]:
                zcopy(way, 1, piece).start()

    for t in range(12):
        is_at = [[(tidx[i:i + 1, t:t + 1] == b).astype(F32) for b in range(4)] for i in (0, 1)]
        block = sum(ft[:, 128 * b:128 * b + 128].astype(F32) * is_at[1][b] for b in range(4)).astype(BF16)
        part = dot_nt(mask[t].astype(F32).astype(BF16), block)
        for b in range(4):
            accl[128 * b:128 * b + 128, 0:WIDTH] += part * is_at[0][b]

    for i in range(feats):
        a, b, zero = wn[192 * i:192 * i + 128, :], wn[192 * i + 128:192 * i + 192, :], jnp.zeros((64, 256), BF16)
        wfold[i, 0] = jnp.concatenate([a, b, zero], axis=0)
        wfold[i, 1] = jnp.concatenate([a, zero, b], axis=0)

    def own_columns():
        xf[x] = ft[...]
        for o in range(1, feats):
            farrived(o)
        carry[...] = jnp.zeros_like(carry) + bias[...]

        def one(i, _):
            carry[...] += dot_tn(xf[i], ws[pl.ds(pl.multiple_of(i * WIDTH, 64), WIDTH), :])
            return 0

        lax.fori_loop(0, feats, one, 0)

    def step(k, _):
        forward(k, order[:2])
        pick(k - 1, 0)
        forward(k, order[2:4])
        pick(k - 1, 1)
        forward(k, order[4:5])
        send(k - 1, 96)
        forward(k, order[5:6])
        yarrived(k - 2, 96)
        place(k - 2, 0)
        forward(k, order[6:7])
        place(k - 2, 1)

        @pl.when(k == half // 2)
        def _():
            own_columns()
        return 0

    k = half - 1
    if half > 2:
        lax.fori_loop(2, half - 1, step, 0)
        if half // 2 < 2 or half // 2 >= half - 1:
            own_columns()
        for piece in order:
            for way in (0, 1):
                zarrived(way, k, piece)
                if piece in last[way]:
                    zcopy(way, k, piece).start()
        pick(k - 1, 0)
        pick(k - 1, 1)
        send(k - 1, 96)
    else:
        own_columns()
    pick(k, 0)
    pick(k, 1)
    send(k, 96)
    if half > 2:
        yarrived(k - 2, 96)
        place(k - 2, 0)
        place(k - 2, 1)
    yarrived(k - 1, 96)
    place(k - 1, 0)
    place(k - 1, 1)

    for piece in order:
        zarrived(0, half, piece)
    slot = at(0, half)
    got = select(ring.at[slot], ringi.at[slot])
    row, col = iota((256, 32), 0), iota((256, 32), 1)
    spread = hot((row // SLOTS == col // 4) & (row % SLOTS == 28 + col % 4))
    put(half, 0, got + dot(spread, msum[:, 0:WIDTH].astype(BF16)))
    send(half, 64)
    yarrived(k, 96)
    place(k, 0)
    place(k, 1)
    yarrived(half, 64)
    place(half, 0, last=True)

    degree = deg[...].astype(F32)
    degree = jnp.concatenate([column(degree[i:i + 1, :]) for i in range(4)], axis=0)
    lead = (accp[:, 0:128] + accm[:, 0:128] + accl[:, 0:128]) / degree
    rest = (accp[:, 128:256] + pltpu.roll(accm[:, 128:256], 64, 1) + accl[:, 128:256]) / degree
    xm[x, 0:512, :] = lead.astype(BF16)
    xm[x, 512:768, :] = jnp.where(low, rest[0:256, :], pltpu.roll(rest[256:512, :], 64, 1)).astype(BF16)
    sent = []
    if feats == 4:
        sent = [mcopy(x, 0, 1, 0), mcopy(x, 1, -1, 1), mcopy(x, 1, 1, 2), mcopy(x, 0, -1, 3)]
        for copy in sent:
            copy.start()
        product(x)
        marrived(-1, 0)
        sent.append(mcopy((x + 3) % 4, 0, 1, 4))
        sent[4].start()
        marrived(1, 1)
        sent.append(mcopy((x + 1) % 4, 1, -1, 5))
        sent[5].start()
        marrived(-1, 1)
        product((x + 3) % 4)
        marrived(1, 0)
        product((x + 1) % 4)
        marrived(2, 0)
        marrived(2, 1)
        product((x + 2) % 4)
    else:
        sent = [mcopy(x, part, o, 2 * o + part - 2) for o in range(1, feats) for part in (0, 1)]
        for copy in sent:
            copy.start()
        product(x)
        for o in range(1, feats):
            marrived(o, 0)
            marrived(o, 1)
            product((x + o) % feats)
    out[...] = jnp.maximum(carry[...], 0.0).astype(BF16)

    for way in (0, 1):
        for s in range(half - 1):
            for piece in order:
                zcopy(way, s, piece).wait_send()
        for piece in last[way]:
            zcopy(way, half - 1, piece).wait_send()
    for o in range(1, PLANE):
        for s in range(half):
            ycopy(s, o, 96).wait_send()
        ycopy(half, o, 64).wait_send()
    for o in range(1, feats):
        fcopy(o).wait_send()
    for copy in sent:
        copy.wait_send()


def on_device(rings, feats, features, w_self, w_neigh, out_bias, degrees, tile_index, tile_mask, cut_source, cut_target,
              hub_local, hub_source, hub_target, mirror_source, mirror_target):
    half = rings // 2
    parts = rings * PLANE
    anywhere = pl.BlockSpec(memory_space=pl.ANY)
    args = (features.T, cut_source[0].T, cut_target[0].T, tile_index[0].T, hub_local, hub_target, hub_source,
            mirror_source.reshape(4, 128), mirror_target.reshape(4, 128), degrees.reshape(4, 128), out_bias.reshape(1, 256),
            tile_mask[0], w_self, w_neigh)
    if parts < 128:
        args = args[:1] + tuple(jnp.pad(a, ((0, 0), (0, 128 - parts))) for a in args[1:3]) + args[3:]
    return pl.pallas_call(
        functools.partial(kernel, rings, feats),
        out_shape=jax.ShapeDtypeStruct((512, 256), BF16),
        in_specs=[anywhere] * len(args),
        out_specs=pl.BlockSpec(memory_space=pltpu.VMEM),
        scratch_shapes=[
            pltpu.VMEM((rings, WIDTH, 512), BF16),
            pltpu.VMEM((rings, IDS, 128), BF16),
            pltpu.VMEM((half + 1, PLANE, 96, 128), BF16),
            pltpu.VMEM((half + 1, PLANE, 96, 128), BF16),
            pltpu.VMEM((feats, WIDTH, 512), BF16),
            pltpu.VMEM((feats, 768, 128), BF16),
            pltpu.VMEM((512, 256), F32),
            pltpu.VMEM((512, 256), F32),
            pltpu.VMEM((512, 256), F32),
            pltpu.VMEM((32, 256), F32),
            pltpu.VMEM((512, 512), BF16),
            pltpu.VMEM((feats, 2, 256, 256), BF16),
            pltpu.VMEM((512, 256), F32),
            pltpu.VMEM((IDS, 128), BF16),
            pltpu.VMEM((rings, 256), F32),
            pltpu.VMEM((IDS, 128), F32),
        ] + [pltpu.VMEM(a.shape, a.dtype) for a in args] + [
            pltpu.SemaphoreType.DMA((2, half, PIECES + 1)),
            pltpu.SemaphoreType.DMA((rings, PIECES + 1)),
            pltpu.SemaphoreType.DMA((half + 1, PLANE)),
            pltpu.SemaphoreType.DMA((half + 1, PLANE)),
            pltpu.SemaphoreType.DMA((4,)),
            pltpu.SemaphoreType.DMA((4,)),
            pltpu.SemaphoreType.DMA((6,)),
            pltpu.SemaphoreType.DMA((4, 2)),
            pltpu.SemaphoreType.DMA((len(args),)),
        ],
        compiler_params=pltpu.CompilerParams(
            collective_id=0, has_side_effects=True, vmem_limit_bytes=40 * 1024 * 1024),
        cost_estimate=pl.CostEstimate(flops=10**10, bytes_accessed=4 * 10**6, transcendentals=0),
    )(*args)


def solution(mesh):
    return jax.shard_map(
        functools.partial(on_device, mesh.shape["dom"] // PLANE, mesh.shape["feat"]),
        mesh=mesh,
        in_specs=(P("dom", "feat"), P(None, "feat"), P(None, "feat"), P("feat"), P("dom"), P("dom"), P("dom"), P("dom"),
                  P("dom"), P("dom"), P("dom"), P("dom"), P("dom"), P("dom")),
        out_specs=P("dom", "feat"),
        check_vma=False,
    )
```

```python
import functools

import jax
import jax.numpy as jnp
from jax import lax
from jax.experimental import pallas as pl
from jax.experimental.pallas import tpu as pltpu
from jax.sharding import PartitionSpec as P

MESH = pl.DeviceIdType.MESH
BF16, F32, I32 = jnp.bfloat16, jnp.float32, jnp.int32
PLANE = 8
SLOTS = 32
WIDTH = 192
PIECES, PIECE = 6, 32
IDS = 48
DIRECT = 2
SHIFT = 256


def dot(a, b):
    return jnp.dot(a, b, preferred_element_type=F32)


def dot_nt(a, b):
    return lax.dot_general(a, b, (((1,), (1,)), ((), ())), preferred_element_type=F32)


def iota(shape, axis):
    return lax.broadcasted_iota(I32, shape, axis)


def hot(mask):
    return jnp.where(mask, 1.0, 0.0).astype(BF16)


def column(row):
    return jnp.transpose(jnp.broadcast_to(row, (128, 128)))


def dot_tn(a, b):
    return lax.dot_general(a, b, (((0,), (0,)), ((), ())), preferred_element_type=F32)


def kernel(rings, feats, ft_hbm, cs_hbm, ct_hbm, ti_hbm, hl_hbm, ht_hbm, hs_hbm, mf_hbm, mt_hbm, deg_hbm, bias_hbm,
           mask_hbm, ws_hbm, wn_hbm, out, ring, ringi, ysend, yrecv, lsend, lrecv, xf, xm, accp, accm, accl, msum, hub_hot, wfold, carry,
           own, tgt, raw, ft, cs, ct, tidx, hub_local, hub_t, hub_s, mirror_f, mirror_t, deg, bias, mask, ws, wn,
           zs, zr, ys, yr, ls, lr, fs, fr, ms, mr, local):
    half = rings // 2
    reach = half - DIRECT
    dom, x = lax.axis_index("dom"), lax.axis_index("feat")
    z, me = dom // PLANE, dom % PLANE
    up, down = ((z + 1) % rings) * PLANE + me, ((z + rings - 1) % rings) * PLANE + me

    barrier = pltpu.get_barrier_semaphore()
    def greet(plane, dest):
        pl.semaphore_signal(barrier, inc=1, device_id=(plane * PLANE + dest, x), device_id_type=MESH)

    for o in range(PLANE):
        if o:
            greet(z, (me + o) % PLANE)
        if DIRECT > 1:
            greet((z + 1) % rings, (me + o) % PLANE)
            greet((z + rings - 1) % rings, (me + o) % PLANE)
        greet((z + rings - DIRECT + 2 * DIRECT * (me // 4)) % rings, (me + o) % PLANE)
    for o in range(1, feats):
        pl.semaphore_signal(barrier, inc=1, device_id=(dom, (x + o) % feats), device_id_type=MESH)

    loads = [pltpu.make_async_copy(src, dst, local.at[i]) for i, (src, dst) in enumerate((
        (cs_hbm, cs), (hl_hbm, hub_local), (mf_hbm, mirror_f), (mt_hbm, mirror_t), (ft_hbm, ft), (ct_hbm, ct), (ti_hbm, tidx),
        (ht_hbm, hub_t), (hs_hbm, hub_s), (deg_hbm, deg), (bias_hbm, bias), (mask_hbm, mask), (ws_hbm, ws), (wn_hbm, wn)))]
    for load in loads:
        load.start()

    def at(way, step):
        return (z + rings - step) % rings if way == 0 else (z + step) % rings

    def zcopy(way, step, piece):
        slot = at(way, step)
        if piece == PIECES:
            src, dst = own if isinstance(step, int) and step == 0 else ringi.at[slot], ringi.at[slot]
        else:
            rows = pl.ds(piece * PIECE, PIECE)
            src = ft_hbm.at[rows] if isinstance(step, int) and step == 0 else ring.at[slot, rows]
            dst = ring.at[slot, rows]
        return pltpu.make_async_remote_copy(
            src_ref=src, dst_ref=dst, send_sem=zs.at[way, step, piece], recv_sem=zr.at[slot, piece],
            device_id=(up if way == 0 else down, x), device_id_type=MESH)

    def zarrived(way, step, piece):
        slot = at(way, step)
        ref = ringi.at[slot] if piece == PIECES else ring.at[slot, pl.ds(piece * PIECE, PIECE)]
        pltpu.make_async_remote_copy(
            src_ref=ref, dst_ref=ref, send_sem=zs.at[way, 0, piece], recv_sem=zr.at[slot, piece],
            device_id=(up, x), device_id_type=MESH).wait_recv()

    order = (PIECES,) + tuple(range(PIECES))

    def forward(step, pieces):
        for piece in pieces:
            for way in (0, 1):
                zarrived(way, step, piece)
                zcopy(way, step, piece).start()

    def ycopy(step, o, rows):
        dest = (me + o) % PLANE
        return pltpu.make_async_remote_copy(
            src_ref=ysend.at[step, dest, pl.ds(0, rows)], dst_ref=yrecv.at[step, me, pl.ds(0, rows)],
            send_sem=ys.at[step, o - 1], recv_sem=yr.at[step, me],
            device_id=(z * PLANE + dest, x), device_id_type=MESH)

    def yarrived(step, rows):
        for o in range(1, PLANE):
            src = (me + o) % PLANE
            pltpu.make_async_remote_copy(
                src_ref=ysend.at[step, src, pl.ds(0, rows)], dst_ref=yrecv.at[step, src, pl.ds(0, rows)],
                send_sem=ys.at[step, o - 1], recv_sem=yr.at[step, src],
                device_id=(z * PLANE + src, x), device_id_type=MESH).wait_recv()

    kinds = [(d, way) for d in range(reach + 1, half) for way in (0, 1)] + [(half, 0)]

    def beyond(way):
        wants = []
        for d in range(reach + 1, half + 1):
            plane = (z + d - reach) % rings if way == 0 else (z + rings - d + reach) % rings
            wants.append((kinds.index((d, way)), plane, 0, 8) if d < half else (len(kinds) - 1, plane, 4 * way, 4))
        return wants

    def lcopy(kind, plane, dest):
        return pltpu.make_async_remote_copy(
            src_ref=lsend.at[kind, dest], dst_ref=lrecv.at[kind, me], send_sem=ls.at[kind, dest], recv_sem=lr.at[kind, me],
            device_id=(plane * PLANE + dest, x), device_id_type=MESH)

    def larrived(kind):
        for src in range(PLANE):
            pltpu.make_async_remote_copy(
                src_ref=lsend.at[kind, src], dst_ref=lrecv.at[kind, src], send_sem=ls.at[kind, src], recv_sem=lr.at[kind, src],
                device_id=(up, x), device_id_type=MESH).wait_recv()

    def fcopy(o):
        return pltpu.make_async_remote_copy(
            src_ref=ft_hbm, dst_ref=xf.at[x], send_sem=fs.at[o - 1], recv_sem=fr.at[x],
            device_id=(dom, (x + o) % feats), device_id_type=MESH)

    def farrived(o):
        src = (x + o) % feats
        pltpu.make_async_remote_copy(
            src_ref=ft_hbm, dst_ref=xf.at[src], send_sem=fs.at[o - 1], recv_sem=fr.at[src],
            device_id=(dom, src), device_id_type=MESH).wait_recv()

    def mcopy(src, part, o, sem):
        rows = pl.ds(384 * part, 384)
        return pltpu.make_async_remote_copy(
            src_ref=xm.at[src, rows], dst_ref=xm.at[src, rows], send_sem=ms.at[sem], recv_sem=mr.at[src, part],
            device_id=(dom, (x + o + feats) % feats), device_id_type=MESH)

    def marrived(o, part):
        mcopy((x + o + feats) % feats, part, 1, 0).wait_recv()

    def select(ref, idref, wants):
        ids = idref[0:32, :].astype(F32)
        lane = iota((32, 512), 1).astype(F32) - SHIFT
        edges = idref[32:48, :].astype(F32)
        node = (iota((512, 128), 0) - SHIFT).astype(F32)
        fro = jnp.concatenate([hot(node == edges[c:c + 1, :]) for c in range(4)], axis=1)
        picks, tos = [], []
        for plane, first, count in wants:
            here = pltpu.roll(ids, (128 - PLANE * plane) % 128, 1)
            picks += [hot(here[:, d:d + 1] == lane) for d in range(first, first + count)]
            hub = (iota((4 * count, 128), 0) + plane * 32 + 4 * first - SHIFT).astype(F32)
            tos.append(jnp.concatenate([hot(hub == edges[4 + c:5 + c, :]) for c in range(4)], axis=1))
        counts = dot_nt(jnp.concatenate(tos, axis=0), fro).astype(BF16)
        got = dot_nt(jnp.concatenate(picks + [counts], axis=0), ref[...])
        total = SLOTS * len(picks)
        out, at_row, at_sum = [], 0, total
        for _, _, count in wants:
            out.append((got[at_row:at_row + SLOTS * count, :], got[at_sum:at_sum + 4 * count, :]))
            at_row, at_sum = at_row + SLOTS * count, at_sum + 4 * count
        return out

    def spread(sums):
        count = sums.shape[0] // 4
        row, col = iota((SLOTS * count, 4 * count), 0), iota((SLOTS * count, 4 * count), 1)
        return dot(hot((row // SLOTS == col // 4) & (row % SLOTS == 28 + col % 4)), sums.astype(BF16))

    def widen(tail):
        return jnp.concatenate([tail, jnp.zeros_like(tail)], axis=1)

    low = iota((256, 128), 1) < 64

    def put(step, way, got):
        ysend[step, :, 64 * way:64 * way + 32, :] = got[:, :128].astype(BF16).reshape(PLANE, SLOTS, 128)
        tail = widen(got[:, 128:])
        if way == 1:
            tail = ysend[step, :, 32:64, :].reshape(256, 128).astype(F32) + pltpu.roll(tail, 64, 1)
        ysend[step, :, 32:64, :] = tail.astype(BF16).reshape(PLANE, SLOTS, 128)

    def pick(step, way):
        slot = at(way, step)
        (got, sums), = select(ring.at[slot], ringi.at[slot], [(z, 0, PLANE)])
        msum[:, 0:WIDTH] += sums
        put(step, way, got)

    def pick_beyond(way):
        slot, wants = at(way, reach), beyond(way)
        got = select(ring.at[slot], ringi.at[slot], [want[1:] for want in wants] + [(z, 0, PLANE)])
        for (kind, plane, first, count), (rows, sums) in zip(wants, got):
            rows = rows + spread(sums)
            lsend[kind, first:first + count, 0:32, :] = rows[:, 0:128].astype(BF16).reshape(count, SLOTS, 128)
            tail = widen(rows[:, 128:]).reshape(count, 2, 16, 128)
            tail = tail[:, 0].reshape(16 * count, 128) + pltpu.roll(tail[:, 1].reshape(16 * count, 128), 64, 1)
            lsend[kind, first:first + count, 32:48, :] = tail.astype(BF16).reshape(count, 16, 128)
            for o in range(count):
                lcopy(kind, plane, first + (me + o) % count).start()
        msum[:, 0:WIDTH] += got[-1][1]
        return got[-1][0]

    def send(step, rows):
        for o in (4, 5, 3, 2, 6, 1, 7):
            ycopy(step, o, rows).start()
        yrecv[step, me, 0:rows, :] = ysend[step, me, 0:rows, :]

    def place(zz, rows, way, sums=False):
        to = tgt[pl.ds(zz, 1), :]
        lane = iota((1, 256), 1) % SLOTS
        if sums:
            for j in range(4):
                to = jnp.where(lane == 28 + j, hub_local[0:1, j:j + 1].astype(F32), to)
        pos = iota((256, 512), 0)
        slot = pos % SLOTS
        hub = jnp.where((slot >= 24) & (slot < 28), zz * 32 + (pos // SLOTS) * 4 + slot - 24, -1)
        where = dot_nt(hub_hot[...], hot(hub == hub_s[...]))
        where = (where + jnp.where(iota((512, 256), 0).astype(F32) == to, 1.0, 0.0)).astype(BF16)
        acc = accp if way == 0 else accm
        acc[...] += dot(where, rows)

    def place_near(step, way, sums=False):
        place(at(way, step), jnp.concatenate([yrecv[step, :, 64 * way:64 * way + 32, :].reshape(256, 128),
                                              yrecv[step, :, 32:64, :].reshape(256, 128)], axis=1), way, sums)

    def place_late(kind):
        tail = lrecv[kind, :, 32:48, :].astype(F32).reshape(128, 128)
        tail = jnp.concatenate([tail.reshape(PLANE, 1, 16, 128), pltpu.roll(tail, 64, 1).reshape(PLANE, 1, 16, 128)], axis=1)
        rows = jnp.concatenate([lrecv[kind, :, 0:32, :].reshape(256, 128), tail.astype(BF16).reshape(256, 128)], axis=1)
        place(at(kinds[kind][1], kinds[kind][0]), rows, 0, True)

    def product(i):
        fold = xm[i, 512:768, :]
        carry[0:256, :] += dot(jnp.concatenate([xm[i, 0:256, :], fold], axis=1), wfold[i, 0])
        carry[256:512, :] += dot(jnp.concatenate([xm[i, 256:512, :], fold], axis=1), wfold[i, 1])

    for load in loads[:4]:
        load.wait()
    raw[0:24, :] = (cs[...] - SHIFT).astype(F32)
    row = iota((8, 128), 0)
    hubs = jnp.full((8, 128), 640, I32)
    for j in range(4):
        hubs = jnp.where(row == j, hub_local[0:1, j:j + 1], hubs)
    raw[24:32, :] = (hubs - SHIFT).astype(F32)
    raw[32:36, :] = (mirror_f[...] - SHIFT).astype(F32)
    raw[36:40, :] = (mirror_t[...] - SHIFT).astype(F32)
    raw[40:48, :] = jnp.zeros((8, 128), F32)
    own[...] = raw[...].astype(BF16)

    pl.semaphore_wait(barrier, PLANE * (2 * DIRECT) - 1 + feats - 1)
    for piece in order:
        for way in (0, 1):
            zcopy(way, 0, piece).start()
    for o in range(1, feats):
        fcopy(o).start()

    for load in loads[4:]:
        load.wait()
    accp[...] = jnp.zeros_like(accp)
    accm[...] = jnp.zeros_like(accm)
    accl[...] = jnp.zeros_like(accl)
    msum[...] = jnp.zeros_like(msum)

    ysend[0, :, 64:96, :] = jnp.zeros((PLANE, SLOTS, 128), BF16)
    (got, sums), = select(ft, own, [(z, 0, PLANE)])
    msum[:, 0:WIDTH] += sums
    put(0, 0, got)
    send(0, 96)

    raw[0:24, :] = ct[...].astype(F32)
    raw[24:48, :] = jnp.full((24, 128), -1.0, F32)
    wide = jnp.transpose(jnp.concatenate([raw[0:32, :], jnp.full((96, 128), -1.0, F32)], axis=0))
    wide = wide[0:rings * PLANE, :].reshape(rings, PLANE, 128)
    lane = iota((rings, 128), 1)
    for part in (0, 1):
        whole = jnp.full((rings, 128), -1.0, F32)
        for d in range(4):
            one = wide[:, 4 * part + d, :]
            whole = jnp.where(lane // SLOTS == d, pltpu.roll(one, SLOTS * d, 1) if d else one, whole)
        tgt[:, 128 * part:128 * part + 128] = whole
    hub_hot[...] = hot(iota((512, 512), 0) == hub_t[...])

    for t in range(12):
        is_at = [[(tidx[i:i + 1, t:t + 1] == b).astype(F32) for b in range(4)] for i in (0, 1)]
        block = sum(ft[:, 128 * b:128 * b + 128].astype(F32) * is_at[1][b] for b in range(4)).astype(BF16)
        part = dot_nt(mask[t].astype(F32).astype(BF16), block)
        for b in range(4):
            accl[128 * b:128 * b + 128, 0:WIDTH] += part * is_at[0][b]

    forward(1, order)

    for i in range(feats):
        a, b, zero = wn[192 * i:192 * i + 128, :], wn[192 * i + 128:192 * i + 192, :], jnp.zeros((64, 256), BF16)
        wfold[i, 0] = jnp.concatenate([a, b, zero], axis=0)
        wfold[i, 1] = jnp.concatenate([a, zero, b], axis=0)

    def own_columns():
        xf[x] = ft[...]
        for o in range(1, feats):
            farrived(o)
        carry[...] = jnp.zeros_like(carry) + bias[...]

        def one(i, _):
            carry[...] += dot_tn(xf[i], ws[pl.ds(pl.multiple_of(i * WIDTH, 64), WIDTH), :])
            return 0

        lax.fori_loop(0, feats, one, 0)

    def step(k, _):
        forward(k, order[:2])
        pick(k - 1, 0)
        forward(k, order[2:4])
        pick(k - 1, 1)
        forward(k, order[4:5])
        send(k - 1, 96)
        forward(k, order[5:6])
        yarrived(k - 2, 96)
        place_near(k - 2, 0)
        forward(k, order[6:7])
        place_near(k - 2, 1)

        @pl.when(k == half // 2)
        def _():
            own_columns()
        return 0

    lax.fori_loop(2, reach, step, 0)
    if not 2 <= half // 2 < reach:
        own_columns()

    k = reach
    pick(k - 1, 0)
    pick(k - 1, 1)
    send(k - 1, 96)
    yarrived(k - 2, 96)
    place_near(k - 2, 0)
    place_near(k - 2, 1)
    for piece in order:
        zarrived(0, k, piece)
    up_rows = pick_beyond(0)
    for piece in order:
        zarrived(1, k, piece)
    down_rows = pick_beyond(1)
    put(k, 0, up_rows + spread(msum[:, 0:WIDTH]))
    put(k, 1, down_rows)
    send(k, 96)
    yarrived(k - 1, 96)
    place_near(k - 1, 0)
    place_near(k - 1, 1)
    yarrived(k, 96)
    place_near(k, 0, True)
    place_near(k, 1)
    for kind in range(len(kinds)):
        larrived(kind)
        place_late(kind)

    degree = deg[...].astype(F32)
    degree = jnp.concatenate([column(degree[i:i + 1, :]) for i in range(4)], axis=0)
    lead = (accp[:, 0:128] + accm[:, 0:128] + accl[:, 0:128]) / degree
    rest = (accp[:, 128:256] + pltpu.roll(accm[:, 128:256], 64, 1) + accl[:, 128:256]) / degree
    xm[x, 0:512, :] = lead.astype(BF16)
    xm[x, 512:768, :] = jnp.where(low, rest[0:256, :], pltpu.roll(rest[256:512, :], 64, 1)).astype(BF16)
    sent = []
    if feats == 4:
        sent = [mcopy(x, 0, 1, 0), mcopy(x, 1, -1, 1), mcopy(x, 1, 1, 2), mcopy(x, 0, -1, 3)]
        for copy in sent:
            copy.start()
        product(x)
        marrived(-1, 0)
        sent.append(mcopy((x + 3) % 4, 0, 1, 4))
        sent[4].start()
        marrived(1, 1)
        sent.append(mcopy((x + 1) % 4, 1, -1, 5))
        sent[5].start()
        marrived(-1, 1)
        product((x + 3) % 4)
        marrived(1, 0)
        product((x + 1) % 4)
        marrived(2, 0)
        marrived(2, 1)
        product((x + 2) % 4)
    else:
        sent = [mcopy(x, part, o, 2 * o + part - 2) for o in range(1, feats) for part in (0, 1)]
        for copy in sent:
            copy.start()
        product(x)
        for o in range(1, feats):
            marrived(o, 0)
            marrived(o, 1)
            product((x + o) % feats)
    out[...] = jnp.maximum(carry[...], 0.0).astype(BF16)

    for way in (0, 1):
        for s in range(reach):
            for piece in order:
                zcopy(way, s, piece).wait_send()
        for kind, plane, first, count in beyond(way):
            for dest in range(first, first + count):
                lcopy(kind, plane, dest).wait_send()
    for o in range(1, PLANE):
        for s in range(reach + 1):
            ycopy(s, o, 96).wait_send()
    for o in range(1, feats):
        fcopy(o).wait_send()
    for copy in sent:
        copy.wait_send()


def on_device(rings, feats, features, w_self, w_neigh, out_bias, degrees, tile_index, tile_mask, cut_source, cut_target,
              hub_local, hub_source, hub_target, mirror_source, mirror_target):
    half = rings // 2
    reach = half - DIRECT
    parts = rings * PLANE
    anywhere = pl.BlockSpec(memory_space=pl.ANY)
    args = (features.T, cut_source[0].T, cut_target[0].T, tile_index[0].T, hub_local, hub_target, hub_source,
            mirror_source.reshape(4, 128), mirror_target.reshape(4, 128), degrees.reshape(4, 128), out_bias.reshape(1, 256),
            tile_mask[0], w_self, w_neigh)
    if parts < 128:
        args = args[:1] + tuple(jnp.pad(a, ((0, 0), (0, 128 - parts))) for a in args[1:3]) + args[3:]
    return pl.pallas_call(
        functools.partial(kernel, rings, feats),
        out_shape=jax.ShapeDtypeStruct((512, 256), BF16),
        in_specs=[anywhere] * len(args),
        out_specs=pl.BlockSpec(memory_space=pltpu.VMEM),
        scratch_shapes=[
            pltpu.VMEM((rings, WIDTH, 512), BF16),
            pltpu.VMEM((rings, IDS, 128), BF16),
            pltpu.VMEM((reach + 1, PLANE, 96, 128), BF16),
            pltpu.VMEM((reach + 1, PLANE, 96, 128), BF16),
            pltpu.VMEM((2 * DIRECT - 1, PLANE, 48, 128), BF16),
            pltpu.VMEM((2 * DIRECT - 1, PLANE, 48, 128), BF16),
            pltpu.VMEM((feats, WIDTH, 512), BF16),
            pltpu.VMEM((feats, 768, 128), BF16),
            pltpu.VMEM((512, 256), F32),
            pltpu.VMEM((512, 256), F32),
            pltpu.VMEM((512, 256), F32),
            pltpu.VMEM((32, 256), F32),
            pltpu.VMEM((512, 512), BF16),
            pltpu.VMEM((feats, 2, 256, 256), BF16),
            pltpu.VMEM((512, 256), F32),
            pltpu.VMEM((IDS, 128), BF16),
            pltpu.VMEM((rings, 256), F32),
            pltpu.VMEM((IDS, 128), F32),
        ] + [pltpu.VMEM(a.shape, a.dtype) for a in args] + [
            pltpu.SemaphoreType.DMA((2, reach, PIECES + 1)),
            pltpu.SemaphoreType.DMA((rings, PIECES + 1)),
            pltpu.SemaphoreType.DMA((reach + 1, PLANE)),
            pltpu.SemaphoreType.DMA((reach + 1, PLANE)),
            pltpu.SemaphoreType.DMA((2 * DIRECT - 1, PLANE)),
            pltpu.SemaphoreType.DMA((2 * DIRECT - 1, PLANE)),
            pltpu.SemaphoreType.DMA((4,)),
            pltpu.SemaphoreType.DMA((4,)),
            pltpu.SemaphoreType.DMA((6,)),
            pltpu.SemaphoreType.DMA((4, 2)),
            pltpu.SemaphoreType.DMA((len(args),)),
        ],
        compiler_params=pltpu.CompilerParams(
            collective_id=0, has_side_effects=True, vmem_limit_bytes=60 * 1024 * 1024),
        cost_estimate=pl.CostEstimate(flops=10**10, bytes_accessed=4 * 10**6, transcendentals=0),
    )(*args)


def solution(mesh):
    return jax.shard_map(
        functools.partial(on_device, mesh.shape["dom"] // PLANE, mesh.shape["feat"]),
        mesh=mesh,
        in_specs=(P("dom", "feat"), P(None, "feat"), P(None, "feat"), P("feat"), P("dom"), P("dom"), P("dom"), P("dom"),
                  P("dom"), P("dom"), P("dom"), P("dom"), P("dom"), P("dom")),
        out_specs=P("dom", "feat"),
        check_vma=False,
    )
```

```python
import functools

import jax
import jax.numpy as jnp
from jax import lax
from jax.experimental import pallas as pl
from jax.experimental.pallas import tpu as pltpu
from jax.sharding import PartitionSpec as P

MESH = pl.DeviceIdType.MESH
BF16, F32, I32 = jnp.bfloat16, jnp.float32, jnp.int32
PLANE = 8
SLOTS = 32
WIDTH = 192
PIECES, PIECE = 6, 32
IDS = 48
DIRECT = 2
SHIFT = 256


def dot(a, b):
    return jnp.dot(a, b, preferred_element_type=F32)


def dot_nt(a, b):
    return lax.dot_general(a, b, (((1,), (1,)), ((), ())), preferred_element_type=F32)


def iota(shape, axis):
    return lax.broadcasted_iota(I32, shape, axis)


def hot(mask):
    return jnp.where(mask, 1.0, 0.0).astype(BF16)


def column(row):
    return jnp.transpose(jnp.broadcast_to(row, (128, 128)))


def dot_tn(a, b):
    return lax.dot_general(a, b, (((0,), (0,)), ((), ())), preferred_element_type=F32)


def kernel(rings, feats, ft_hbm, cs_hbm, ct_hbm, ti_hbm, hl_hbm, ht_hbm, hs_hbm, mf_hbm, mt_hbm, deg_hbm, bias_hbm,
           mask_hbm, ws_hbm, wn_hbm, out, ring, ringi, ysend, yrecv, lsend, lrecv, xf, xm, accp, accm, accl, msum, hub_hot, farsel, places, degree, carry,
           own, tgt, raw, ft, cs, ct, tidx, hub_local, hub_t, hub_s, mirror_f, mirror_t, deg, bias, mask, ws, wn,
           zs, zr, ys, yr, ls, lr, fs, fr, ms, mr, local):
    half = rings // 2
    reach = half - DIRECT
    dom, x = lax.axis_index("dom"), lax.axis_index("feat")
    z, me = dom // PLANE, dom % PLANE
    up, down = ((z + 1) % rings) * PLANE + me, ((z + rings - 1) % rings) * PLANE + me

    barrier = pltpu.get_barrier_semaphore()
    def greet(plane, dest):
        pl.semaphore_signal(barrier, inc=1, device_id=(plane * PLANE + dest, x), device_id_type=MESH)

    for o in range(PLANE):
        if o:
            greet(z, (me + o) % PLANE)
        if DIRECT > 1:
            greet((z + 1) % rings, (me + o) % PLANE)
            greet((z + rings - 1) % rings, (me + o) % PLANE)
        greet((z + rings - DIRECT + 2 * DIRECT * (me // 4)) % rings, (me + o) % PLANE)
    for o in range(1, feats):
        pl.semaphore_signal(barrier, inc=1, device_id=(dom, (x + o) % feats), device_id_type=MESH)

    loads = [pltpu.make_async_copy(src, dst, local.at[i]) for i, (src, dst) in enumerate((
        (cs_hbm, cs), (hl_hbm, hub_local), (mf_hbm, mirror_f), (mt_hbm, mirror_t), (ft_hbm, ft), (ct_hbm, ct), (ti_hbm, tidx),
        (ht_hbm, hub_t), (hs_hbm, hub_s), (deg_hbm, deg), (bias_hbm, bias), (mask_hbm, mask), (ws_hbm, ws), (wn_hbm, wn)))]
    for load in loads:
        load.start()

    def at(way, step):
        return (z + rings - step) % rings if way == 0 else (z + step) % rings

    def zcopy(way, step, piece):
        slot = at(way, step)
        if piece == PIECES:
            src, dst = own if isinstance(step, int) and step == 0 else ringi.at[slot], ringi.at[slot]
        else:
            rows = pl.ds(piece * PIECE, PIECE)
            src = ft_hbm.at[rows] if isinstance(step, int) and step == 0 else ring.at[slot, rows]
            dst = ring.at[slot, rows]
        return pltpu.make_async_remote_copy(
            src_ref=src, dst_ref=dst, send_sem=zs.at[way, step, piece], recv_sem=zr.at[slot, piece],
            device_id=(up if way == 0 else down, x), device_id_type=MESH)

    def zarrived(way, step, piece):
        slot = at(way, step)
        ref = ringi.at[slot] if piece == PIECES else ring.at[slot, pl.ds(piece * PIECE, PIECE)]
        pltpu.make_async_remote_copy(
            src_ref=ref, dst_ref=ref, send_sem=zs.at[way, 0, piece], recv_sem=zr.at[slot, piece],
            device_id=(up, x), device_id_type=MESH).wait_recv()

    order = (PIECES,) + tuple(range(PIECES))

    def forward(step, pieces):
        for piece in pieces:
            for way in (0, 1):
                zarrived(way, step, piece)
                zcopy(way, step, piece).start()

    def ycopy(step, o, first, rows, sem):
        dest = (me + o) % PLANE
        return pltpu.make_async_remote_copy(
            src_ref=ysend.at[step, dest, pl.ds(first, rows)], dst_ref=yrecv.at[step, me, pl.ds(first, rows)],
            send_sem=ys.at[sem, o - 1], recv_sem=yr.at[sem, me],
            device_id=(z * PLANE + dest, x), device_id_type=MESH)

    def yarrived(step, first=0, rows=96, sem=None):
        for o in range(1, PLANE):
            src = (me + o) % PLANE
            ref = yrecv.at[step, src, pl.ds(first, rows)]
            pltpu.make_async_remote_copy(
                src_ref=ref, dst_ref=ref, send_sem=ys.at[step, o - 1], recv_sem=yr.at[step if sem is None else sem, src],
                device_id=(z * PLANE + src, x), device_id_type=MESH).wait_recv()

    kinds = [(d, way) for d in range(reach + 1, half) for way in (0, 1)] + [(half, 0)]

    def beyond(way):
        wants = []
        for d in range(reach + 1, half + 1):
            plane = (z + d - reach) % rings if way == 0 else (z + rings - d + reach) % rings
            wants.append((kinds.index((d, way)), plane, 0, 8) if d < half else (len(kinds) - 1, plane, 4 * way, 4))
        return wants

    late = (pl.ds(0, 32), pl.ds(32, 16))

    def lcopy(kind, plane, dest, part):
        return pltpu.make_async_remote_copy(
            src_ref=lsend.at[kind, dest, late[part]], dst_ref=lrecv.at[kind, me, late[part]],
            send_sem=ls.at[kind, dest, part], recv_sem=lr.at[kind, me, part],
            device_id=(plane * PLANE + dest, x), device_id_type=MESH)

    def larrived(part):
        for kind in range(len(kinds)):
            for src in range(PLANE):
                ref = lrecv.at[kind, src, late[part]]
                pltpu.make_async_remote_copy(
                    src_ref=ref, dst_ref=ref, send_sem=ls.at[kind, src, part], recv_sem=lr.at[kind, src, part],
                    device_id=(up, x), device_id_type=MESH).wait_recv()

    def fcopy(o):
        return pltpu.make_async_remote_copy(
            src_ref=ft_hbm, dst_ref=xf.at[x], send_sem=fs.at[o - 1], recv_sem=fr.at[x],
            device_id=(dom, (x + o) % feats), device_id_type=MESH)

    def farrived(o):
        src = (x + o) % feats
        pltpu.make_async_remote_copy(
            src_ref=ft_hbm, dst_ref=xf.at[src], send_sem=fs.at[o - 1], recv_sem=fr.at[src],
            device_id=(dom, src), device_id_type=MESH).wait_recv()

    parts = (pl.ds(0, 256), pl.ds(256, 256), pl.ds(512, 128), pl.ds(640, 128))

    def mcopy(src, part, o, sem):
        return pltpu.make_async_remote_copy(
            src_ref=xm.at[src, parts[part]], dst_ref=xm.at[src, parts[part]], send_sem=ms.at[sem], recv_sem=mr.at[src, part],
            device_id=(dom, (x + o + feats) % feats), device_id_type=MESH)

    def marrived(o, part):
        mcopy((x + o + feats) % feats, part, 1, 0).wait_recv()

    def selector(idref, wants):
        ids = idref[0:32, :].astype(F32)
        lane = iota((32, 512), 1).astype(F32) - SHIFT
        edges = idref[32:48, :].astype(F32)
        node = (iota((512, 128), 0) - SHIFT).astype(F32)
        fro = jnp.concatenate([hot(node == edges[c:c + 1, :]) for c in range(4)], axis=1)
        picks, tos = [], []
        for plane, first, count in wants:
            here = pltpu.roll(ids, (128 - PLANE * plane) % 128, 1)
            picks += [hot(here[:, d:d + 1] == lane) for d in range(first, first + count)]
            hub = (iota((4 * count, 128), 0) + plane * 32 + 4 * first - SHIFT).astype(F32)
            tos.append(jnp.concatenate([hot(hub == edges[4 + c:5 + c, :]) for c in range(4)], axis=1))
        return jnp.concatenate(picks + [dot_nt(jnp.concatenate(tos, axis=0), fro).astype(BF16)], axis=0)

    def select(ref, idref):
        got = dot_nt(selector(idref, [(z, 0, PLANE)]), ref[...])
        msum[:, 0:WIDTH] += got[256:288, :]
        return got[0:256, :]

    def spread(sums):
        count = sums.shape[0] // 4
        row, col = iota((SLOTS * count, 4 * count), 0), iota((SLOTS * count, 4 * count), 1)
        return dot(hot((row // SLOTS == col // 4) & (row % SLOTS == 28 + col % 4)), sums.astype(BF16))

    def widen(tail):
        return jnp.concatenate([tail, jnp.zeros_like(tail)], axis=1)

    low = iota((256, 128), 1) < 64

    def put(step, way, got):
        ysend[step, :, 64 * way:64 * way + 32, :] = got[:, :128].astype(BF16).reshape(PLANE, SLOTS, 128)
        tail = widen(got[:, 128:])
        if way == 1:
            tail = ysend[step, :, 32:64, :].reshape(256, 128).astype(F32) + pltpu.roll(tail, 64, 1)
        ysend[step, :, 32:64, :] = tail.astype(BF16).reshape(PLANE, SLOTS, 128)

    def pick(step, way):
        slot = at(way, step)
        put(step, way, select(ring.at[slot], ringi.at[slot]))

    def last_rows(way, columns):
        wants = beyond(way)
        got = dot_nt(farsel[way], ring[at(way, reach), columns, :])
        counts = [want[3] for want in wants] + [PLANE]
        at_row, at_sum, found = 0, SLOTS * sum(counts), []
        for count in counts:
            found.append((got[at_row:at_row + SLOTS * count, :], got[at_sum:at_sum + 4 * count, :]))
            at_row, at_sum = at_row + SLOTS * count, at_sum + 4 * count
        return wants, found[:-1], found[-1]

    def send_late(wants, found, part):
        for (kind, plane, first, count), (rows, sums) in zip(wants, found):
            rows = rows + spread(sums)
            if part == 0:
                lsend[kind, first:first + count, 0:32, :] = rows.astype(BF16).reshape(count, SLOTS, 128)
            else:
                tail = widen(rows).reshape(count, 2, 16, 128)
                tail = tail[:, 0].reshape(16 * count, 128) + pltpu.roll(tail[:, 1].reshape(16 * count, 128), 64, 1)
                lsend[kind, first:first + count, 32:48, :] = tail.astype(BF16).reshape(count, 16, 128)
            for o in range(count):
                lcopy(kind, plane, first + (me + o) % count, part).start()

    def send(step, first=0, rows=96, sem=None):
        for o in (4, 5, 3, 2, 6, 1, 7):
            ycopy(step, o, first, rows, step if sem is None else sem).start()
        yrecv[step, me, first:first + rows, :] = ysend[step, me, first:first + rows, :]

    def placement(zz, sums=False):
        to = tgt[pl.ds(zz, 1), :]
        lane = iota((1, 256), 1) % SLOTS
        if sums:
            for j in range(4):
                to = jnp.where(lane == 28 + j, hub_local[0:1, j:j + 1].astype(F32), to)
        pos = iota((256, 512), 0)
        slot = pos % SLOTS
        hub = jnp.where((slot >= 24) & (slot < 28), zz * 32 + (pos // SLOTS) * 4 + slot - 24, -1)
        where = dot_nt(hub_hot[...], hot(hub == hub_s[...]))
        return (where + jnp.where(iota((512, 256), 0).astype(F32) == to, 1.0, 0.0)).astype(BF16)

    def place(step, way):
        rows = jnp.concatenate([yrecv[step, :, 64 * way:64 * way + 32, :].reshape(256, 128),
                                yrecv[step, :, 32:64, :].reshape(256, 128)], axis=1)
        acc = accp if way == 0 else accm
        acc[...] += dot(placement(at(way, step)), rows)

    def product(i, part):
        w = pl.multiple_of(i * WIDTH, 64)
        if part == 0:
            carry[...] += dot(xm[i, 0:512, :], wn[pl.ds(w, 128), :])
        else:
            b, zero = wn[pl.ds(w + 128, 64), :], jnp.zeros((64, 256), BF16)
            carry[0:256, :] += dot(xm[i, 512:768, :], jnp.concatenate([b, zero], axis=0))
            carry[256:512, :] += dot(xm[i, 512:768, :], jnp.concatenate([zero, b], axis=0))

    for load in loads[:4]:
        load.wait()
    raw[0:24, :] = (cs[...] - SHIFT).astype(F32)
    row = iota((8, 128), 0)
    hubs = jnp.full((8, 128), 640, I32)
    for j in range(4):
        hubs = jnp.where(row == j, hub_local[0:1, j:j + 1], hubs)
    raw[24:32, :] = (hubs - SHIFT).astype(F32)
    raw[32:36, :] = (mirror_f[...] - SHIFT).astype(F32)
    raw[36:40, :] = (mirror_t[...] - SHIFT).astype(F32)
    raw[40:48, :] = jnp.zeros((8, 128), F32)
    own[...] = raw[...].astype(BF16)

    pl.semaphore_wait(barrier, PLANE * (2 * DIRECT) - 1 + feats - 1)
    for piece in order:
        for way in (0, 1):
            zcopy(way, 0, piece).start()
    for o in range(1, feats):
        fcopy(o).start()

    for load in loads[4:]:
        load.wait()
    accp[...] = jnp.zeros_like(accp)
    accm[...] = jnp.zeros_like(accm)
    accl[...] = jnp.zeros_like(accl)
    msum[...] = jnp.zeros_like(msum)

    ysend[0, :, 64:96, :] = jnp.zeros((PLANE, SLOTS, 128), BF16)
    put(0, 0, select(ft, own))
    send(0)

    raw[0:24, :] = ct[...].astype(F32)
    raw[24:48, :] = jnp.full((24, 128), -1.0, F32)
    wide = jnp.transpose(jnp.concatenate([raw[0:32, :], jnp.full((96, 128), -1.0, F32)], axis=0))
    wide = wide[0:rings * PLANE, :].reshape(rings, PLANE, 128)
    lane = iota((rings, 128), 1)
    for part in (0, 1):
        whole = jnp.full((rings, 128), -1.0, F32)
        for d in range(4):
            one = wide[:, 4 * part + d, :]
            whole = jnp.where(lane // SLOTS == d, pltpu.roll(one, SLOTS * d, 1) if d else one, whole)
        tgt[:, 128 * part:128 * part + 128] = whole
    hub_hot[...] = hot(iota((512, 512), 0) == hub_t[...])

    places[:, 0:256] = placement(at(0, reach), True)
    places[:, 256:512] = placement(at(1, reach))
    for kind, (d, way) in enumerate(kinds):
        places[:, 512 + 256 * kind:768 + 256 * kind] = placement(at(way, d), True)

    for t in range(12):
        is_at = [[(tidx[i:i + 1, t:t + 1] == b).astype(F32) for b in range(4)] for i in (0, 1)]
        block = sum(ft[:, 128 * b:128 * b + 128].astype(F32) * is_at[1][b] for b in range(4)).astype(BF16)
        part = dot_nt(mask[t].astype(F32).astype(BF16), block)
        for b in range(4):
            accl[128 * b:128 * b + 128, 0:WIDTH] += part * is_at[0][b]

    forward(1, order)

    deg_row = deg[...].astype(F32)
    for i in range(4):
        degree[128 * i:128 * i + 128, :] = column(deg_row[i:i + 1, :])

    def own_columns():
        xf[x] = ft[...]
        for o in range(1, feats):
            farrived(o)
        carry[...] = jnp.zeros_like(carry) + bias[...]

        def one(i, _):
            carry[...] += dot_tn(xf[i], ws[pl.ds(pl.multiple_of(i * WIDTH, 64), WIDTH), :])
            return 0

        lax.fori_loop(0, feats, one, 0)

    def step(k, _):
        forward(k, order[:2])
        pick(k - 1, 0)
        forward(k, order[2:4])
        pick(k - 1, 1)
        forward(k, order[4:5])
        send(k - 1)
        forward(k, order[5:6])
        yarrived(k - 2)
        place(k - 2, 0)
        forward(k, order[6:7])
        place(k - 2, 1)

        @pl.when(k == half // 2)
        def _():
            own_columns()
        return 0

    lax.fori_loop(2, reach, step, 0)
    if not 2 <= half // 2 < reach:
        own_columns()

    k = reach
    pick(k - 1, 0)
    pick(k - 1, 1)
    send(k - 1)
    for way in (0, 1):
        zarrived(way, k, PIECES)
        farsel[way] = selector(ringi.at[at(way, k)], [want[1:] for want in beyond(way)] + [(z, 0, PLANE)])
    yarrived(k - 2)
    place(k - 2, 0)
    place(k - 2, 1)
    lead, rest, split = slice(0, 128), slice(128, WIDTH), 128 // PIECE
    near = []
    for way in (0, 1):
        for piece in range(split):
            zarrived(way, k, piece)
        wants, found, own_plane = last_rows(way, lead)
        send_late(wants, found, 0)
        near.append(own_plane)
    sums = msum[:, lead] + near[0][1] + near[1][1]
    ysend[k, :, 0:32, :] = (near[0][0] + spread(sums)).astype(BF16).reshape(PLANE, SLOTS, 128)
    ysend[k, :, 32:64, :] = near[1][0].astype(BF16).reshape(PLANE, SLOTS, 128)
    send(k, 0, 64)
    near = []
    for way in (0, 1):
        for piece in range(split, PIECES):
            zarrived(way, k, piece)
        wants, found, own_plane = last_rows(way, rest)
        send_late(wants, found, 1)
        near.append(own_plane)
    sums = msum[:, rest] + near[0][1] + near[1][1]
    tail = widen(near[0][0] + spread(sums)) + pltpu.roll(widen(near[1][0]), 64, 1)
    ysend[k, :, 64:96, :] = tail.astype(BF16).reshape(PLANE, SLOTS, 128)
    send(k, 64, 32, k + 1)
    yarrived(k - 1)
    place(k - 1, 0)
    place(k - 1, 1)

    before = accp[:, lead] + accm[:, lead] + accl[:, lead]
    yarrived(k, 0, 64)
    larrived(0)
    rows = jnp.concatenate([yrecv[k, :, 0:32, :].reshape(256, 128), yrecv[k, :, 32:64, :].reshape(256, 128)]
                           + [lrecv[kind, :, 0:32, :].reshape(256, 128) for kind in range(len(kinds))], axis=0)
    xm[x, 0:512, :] = ((before + dot(places[...], rows)) / degree[...]).astype(BF16)
    sent = []

    def tell(first):
        for part, o in ((0, 1), (1, -1), (1, 1), (0, -1)) if feats == 4 else [(p, o) for o in range(1, feats) for p in (0, 1)]:
            sent.append(mcopy(x, first + part, o, len(sent)))
            sent[-1].start()

    def relay(o, part):
        marrived(-o, part)
        sent.append(mcopy((x - o + feats) % feats, part, o, len(sent)))
        sent[-1].start()

    tell(0)
    product(x, 0)

    before = accp[:, 128:256] + pltpu.roll(accm[:, 128:256], 64, 1) + accl[:, 128:256]
    yarrived(k, 64, 32, k + 1)
    larrived(1)
    both = yrecv[k, :, 64:96, :].reshape(256, 128)
    rows = [both, pltpu.roll(both.astype(F32), 64, 1).astype(BF16)]
    for kind in range(len(kinds)):
        tail = lrecv[kind, :, 32:48, :].astype(F32).reshape(128, 128)
        tail = jnp.concatenate([tail.reshape(PLANE, 1, 16, 128), pltpu.roll(tail, 64, 1).reshape(PLANE, 1, 16, 128)], axis=1)
        rows.append(tail.astype(BF16).reshape(256, 128))
    mean = (before + dot(places[...], jnp.concatenate(rows, axis=0))) / degree[...]
    xm[x, 512:768, :] = jnp.where(low, mean[0:256, :], pltpu.roll(mean[256:512, :], 64, 1)).astype(BF16)
    tell(2)
    if feats == 4:
        relay(1, 0)
        relay(-1, 1)
        relay(1, 2)
        relay(-1, 3)
        product(x, 1)
        marrived(-1, 1)
        product((x + 3) % 4, 0)
        marrived(1, 0)
        product((x + 1) % 4, 0)
        marrived(-1, 3)
        product((x + 3) % 4, 1)
        marrived(1, 2)
        product((x + 1) % 4, 1)
        marrived(2, 0)
        marrived(2, 1)
        product((x + 2) % 4, 0)
        marrived(2, 2)
        marrived(2, 3)
        product((x + 2) % 4, 1)
    else:
        product(x, 1)
        for o in range(1, feats):
            for part in range(4):
                marrived(o, part)
            product((x + o) % feats, 0)
            product((x + o) % feats, 1)
    out[...] = jnp.maximum(carry[...], 0.0).astype(BF16)

    for way in (0, 1):
        for s in range(reach):
            for piece in order:
                zcopy(way, s, piece).wait_send()
        for kind, plane, first, count in beyond(way):
            for dest in range(first, first + count):
                lcopy(kind, plane, dest, 0).wait_send()
                lcopy(kind, plane, dest, 1).wait_send()
    for o in range(1, PLANE):
        for s in range(reach):
            ycopy(s, o, 0, 96, s).wait_send()
        ycopy(reach, o, 0, 64, reach).wait_send()
        ycopy(reach, o, 64, 32, reach + 1).wait_send()
    for o in range(1, feats):
        fcopy(o).wait_send()
    for copy in sent:
        copy.wait_send()


def on_device(rings, feats, features, w_self, w_neigh, out_bias, degrees, tile_index, tile_mask, cut_source, cut_target,
              hub_local, hub_source, hub_target, mirror_source, mirror_target):
    half = rings // 2
    reach = half - DIRECT
    parts = rings * PLANE
    anywhere = pl.BlockSpec(memory_space=pl.ANY)
    args = (features.T, cut_source[0].T, cut_target[0].T, tile_index[0].T, hub_local, hub_target, hub_source,
            mirror_source.reshape(4, 128), mirror_target.reshape(4, 128), degrees.reshape(4, 128), out_bias.reshape(1, 256),
            tile_mask[0], w_self, w_neigh)
    if parts < 128:
        args = args[:1] + tuple(jnp.pad(a, ((0, 0), (0, 128 - parts))) for a in args[1:3]) + args[3:]
    return pl.pallas_call(
        functools.partial(kernel, rings, feats),
        out_shape=jax.ShapeDtypeStruct((512, 256), BF16),
        in_specs=[anywhere] * len(args),
        out_specs=pl.BlockSpec(memory_space=pltpu.VMEM),
        scratch_shapes=[
            pltpu.VMEM((rings, WIDTH, 512), BF16),
            pltpu.VMEM((rings, IDS, 128), BF16),
            pltpu.VMEM((reach + 1, PLANE, 96, 128), BF16),
            pltpu.VMEM((reach + 1, PLANE, 96, 128), BF16),
            pltpu.VMEM((2 * DIRECT - 1, PLANE, 48, 128), BF16),
            pltpu.VMEM((2 * DIRECT - 1, PLANE, 48, 128), BF16),
            pltpu.VMEM((feats, WIDTH, 512), BF16),
            pltpu.VMEM((feats, 768, 128), BF16),
            pltpu.VMEM((512, 256), F32),
            pltpu.VMEM((512, 256), F32),
            pltpu.VMEM((512, 256), F32),
            pltpu.VMEM((32, 256), F32),
            pltpu.VMEM((512, 512), BF16),
            pltpu.VMEM((2, 36 * (8 * DIRECT + 4), 512), BF16),
            pltpu.VMEM((512, 256 * (2 * DIRECT + 1)), BF16),
            pltpu.VMEM((512, 128), F32),
            pltpu.VMEM((512, 256), F32),
            pltpu.VMEM((IDS, 128), BF16),
            pltpu.VMEM((rings, 256), F32),
            pltpu.VMEM((IDS, 128), F32),
        ] + [pltpu.VMEM(a.shape, a.dtype) for a in args] + [
            pltpu.SemaphoreType.DMA((2, reach, PIECES + 1)),
            pltpu.SemaphoreType.DMA((rings, PIECES + 1)),
            pltpu.SemaphoreType.DMA((reach + 2, PLANE)),
            pltpu.SemaphoreType.DMA((reach + 2, PLANE)),
            pltpu.SemaphoreType.DMA((2 * DIRECT - 1, PLANE, 2)),
            pltpu.SemaphoreType.DMA((2 * DIRECT - 1, PLANE, 2)),
            pltpu.SemaphoreType.DMA((4,)),
            pltpu.SemaphoreType.DMA((4,)),
            pltpu.SemaphoreType.DMA((12,)),
            pltpu.SemaphoreType.DMA((4, 4)),
            pltpu.SemaphoreType.DMA((len(args),)),
        ],
        compiler_params=pltpu.CompilerParams(
            collective_id=0, has_side_effects=True, vmem_limit_bytes=60 * 1024 * 1024),
        cost_estimate=pl.CostEstimate(flops=10**10, bytes_accessed=4 * 10**6, transcendentals=0),
    )(*args)


def solution(mesh):
    return jax.shard_map(
        functools.partial(on_device, mesh.shape["dom"] // PLANE, mesh.shape["feat"]),
        mesh=mesh,
        in_specs=(P("dom", "feat"), P(None, "feat"), P(None, "feat"), P("feat"), P("dom"), P("dom"), P("dom"), P("dom"),
                  P("dom"), P("dom"), P("dom"), P("dom"), P("dom"), P("dom")),
        out_specs=P("dom", "feat"),
        check_vma=False,
    )
```

```python
import functools

import jax
import jax.numpy as jnp
from jax import lax
from jax.experimental import pallas as pl
from jax.experimental.pallas import tpu as pltpu
from jax.sharding import PartitionSpec as P

MESH = pl.DeviceIdType.MESH
BF16, F32, I32 = jnp.bfloat16, jnp.float32, jnp.int32
PLANE = 8
SLOTS = 32
WIDTH = 192
PIECES, PIECE = 6, 32
IDS = 48
DIRECT = 2
SHIFT = 256


def dot(a, b):
    return jnp.dot(a, b, preferred_element_type=F32)


def dot_nt(a, b):
    return lax.dot_general(a, b, (((1,), (1,)), ((), ())), preferred_element_type=F32)


def iota(shape, axis):
    return lax.broadcasted_iota(I32, shape, axis)


def hot(mask):
    return jnp.where(mask, 1.0, 0.0).astype(BF16)


def column(row):
    return jnp.transpose(jnp.broadcast_to(row, (128, 128)))


def dot_tn(a, b):
    return lax.dot_general(a, b, (((0,), (0,)), ((), ())), preferred_element_type=F32)


def kernel(rings, feats, ft_hbm, cs_hbm, ct_hbm, ti_hbm, hl_hbm, ht_hbm, hs_hbm, mf_hbm, mt_hbm, deg_hbm, bias_hbm,
           mask_hbm, ws_hbm, wn_hbm, out, ring, ringi, ysend, yrecv, lsend, lrecv, xf, xm, accp, accm, accl, msum, hub_hot, farsel, places, degree, carry,
           own, tgt, raw, ft, cs, ct, tidx, hub_local, hub_t, hub_s, mirror_f, mirror_t, deg, bias, mask, ws, wn,
           zs, zr, ys, yr, ls, lr, fs, fr, ms, mr, local):
    half = rings // 2
    reach = half - DIRECT
    dom, x = lax.axis_index("dom"), lax.axis_index("feat")
    z, me = dom // PLANE, dom % PLANE
    up, down = ((z + 1) % rings) * PLANE + me, ((z + rings - 1) % rings) * PLANE + me

    barrier = pltpu.get_barrier_semaphore()
    def greet(plane, dest):
        pl.semaphore_signal(barrier, inc=1, device_id=(plane * PLANE + dest, x), device_id_type=MESH)

    for o in range(PLANE):
        if o:
            greet(z, (me + o) % PLANE)
        if DIRECT > 1:
            greet((z + 1) % rings, (me + o) % PLANE)
            greet((z + rings - 1) % rings, (me + o) % PLANE)
        greet((z + rings - DIRECT + 2 * DIRECT * (me // 4)) % rings, (me + o) % PLANE)
    for o in range(1, feats):
        pl.semaphore_signal(barrier, inc=1, device_id=(dom, (x + o) % feats), device_id_type=MESH)

    loads = [pltpu.make_async_copy(src, dst, local.at[i]) for i, (src, dst) in enumerate((
        (cs_hbm, cs), (hl_hbm, hub_local), (mf_hbm, mirror_f), (mt_hbm, mirror_t), (ft_hbm, ft), (ct_hbm, ct), (ti_hbm, tidx),
        (ht_hbm, hub_t), (hs_hbm, hub_s), (deg_hbm, deg), (bias_hbm, bias), (mask_hbm, mask), (ws_hbm, ws), (wn_hbm, wn)))]
    for load in loads:
        load.start()

    def at(way, step):
        return (z + rings - step) % rings if way == 0 else (z + step) % rings

    def zcopy(way, step, piece):
        slot = at(way, step)
        if piece == PIECES:
            src, dst = own if isinstance(step, int) and step == 0 else ringi.at[slot], ringi.at[slot]
        else:
            rows = pl.ds(piece * PIECE, PIECE)
            src = ft_hbm.at[rows] if isinstance(step, int) and step == 0 else ring.at[slot, rows]
            dst = ring.at[slot, rows]
        return pltpu.make_async_remote_copy(
            src_ref=src, dst_ref=dst, send_sem=zs.at[way, step, piece // PIECES], recv_sem=zr.at[slot, piece],
            device_id=(up if way == 0 else down, x), device_id_type=MESH)

    def zarrived(way, step, piece):
        slot = at(way, step)
        ref = ringi.at[slot] if piece == PIECES else ring.at[slot, pl.ds(piece * PIECE, PIECE)]
        pltpu.make_async_remote_copy(
            src_ref=ref, dst_ref=ref, send_sem=zs.at[way, 0, piece // PIECES], recv_sem=zr.at[slot, piece],
            device_id=(up, x), device_id_type=MESH).wait_recv()

    order = (PIECES,) + tuple(range(PIECES))

    def zsent(way, step):
        slot = at(way, step)
        for ref, sem in ((ring.at[slot], 0), (ringi.at[slot], 1)):
            pltpu.make_async_remote_copy(
                src_ref=ref, dst_ref=ref, send_sem=zs.at[way, step, sem], recv_sem=zr.at[slot, 0],
                device_id=(up, x), device_id_type=MESH).wait_send()

    def forward(step, pieces):
        for piece in pieces:
            for way in (0, 1):
                zarrived(way, step, piece)
                zcopy(way, step, piece).start()

    def ycopy(step, o, first, rows, sem):
        dest = (me + o) % PLANE
        return pltpu.make_async_remote_copy(
            src_ref=ysend.at[step, dest, pl.ds(first, rows)], dst_ref=yrecv.at[step, me, pl.ds(first, rows)],
            send_sem=ys.at[sem, o - 1], recv_sem=yr.at[sem, me],
            device_id=(z * PLANE + dest, x), device_id_type=MESH)

    def yarrived(step, first=0, rows=96, sem=None):
        for o in range(1, PLANE):
            src = (me + o) % PLANE
            ref = yrecv.at[step, src, pl.ds(first, rows)]
            pltpu.make_async_remote_copy(
                src_ref=ref, dst_ref=ref, send_sem=ys.at[step, o - 1], recv_sem=yr.at[step if sem is None else sem, src],
                device_id=(z * PLANE + src, x), device_id_type=MESH).wait_recv()

    kinds = [(d, way) for d in range(reach + 1, half) for way in (0, 1)] + [(half, 0)]

    def beyond(way):
        wants = []
        for d in range(reach + 1, half + 1):
            plane = (z + d - reach) % rings if way == 0 else (z + rings - d + reach) % rings
            wants.append((kinds.index((d, way)), plane, 0, 8) if d < half else (len(kinds) - 1, plane, 4 * way, 4))
        return wants

    late = (pl.ds(0, 32), pl.ds(32, 16))

    def lcopy(kind, plane, dest, part):
        return pltpu.make_async_remote_copy(
            src_ref=lsend.at[kind, dest, late[part]], dst_ref=lrecv.at[kind, me, late[part]],
            send_sem=ls.at[part], recv_sem=lr.at[part],
            device_id=(plane * PLANE + dest, x), device_id_type=MESH)

    def lall(part):
        return pltpu.make_async_remote_copy(
            src_ref=lsend.at[:, :, late[part]], dst_ref=lrecv.at[:, :, late[part]], send_sem=ls.at[part], recv_sem=lr.at[part],
            device_id=(up, x), device_id_type=MESH)

    def fcopy(o):
        return pltpu.make_async_remote_copy(
            src_ref=ft_hbm, dst_ref=xf.at[x], send_sem=fs.at[o - 1], recv_sem=fr.at[x],
            device_id=(dom, (x + o) % feats), device_id_type=MESH)

    def farrived(o):
        src = (x + o) % feats
        pltpu.make_async_remote_copy(
            src_ref=ft_hbm, dst_ref=xf.at[src], send_sem=fs.at[o - 1], recv_sem=fr.at[src],
            device_id=(dom, src), device_id_type=MESH).wait_recv()

    parts = (pl.ds(0, 256), pl.ds(256, 256), pl.ds(512, 128), pl.ds(640, 128))

    def mcopy(src, part, o, sem):
        return pltpu.make_async_remote_copy(
            src_ref=xm.at[src, parts[part]], dst_ref=xm.at[src, parts[part]], send_sem=ms.at[sem], recv_sem=mr.at[src, part],
            device_id=(dom, (x + o + feats) % feats), device_id_type=MESH)

    def marrived(o, part):
        mcopy((x + o + feats) % feats, part, 1, 0).wait_recv()

    def selector(idref, wants):
        ids = idref[0:32, :].astype(F32)
        lane = iota((32, 512), 1).astype(F32) - SHIFT
        edges = idref[32:48, :].astype(F32)
        node = (iota((512, 128), 0) - SHIFT).astype(F32)
        fro = jnp.concatenate([hot(node == edges[c:c + 1, :]) for c in range(4)], axis=1)
        picks, tos = [], []
        for plane, first, count in wants:
            here = pltpu.roll(ids, (128 - PLANE * plane) % 128, 1)
            picks += [hot(here[:, d:d + 1] == lane) for d in range(first, first + count)]
            hub = (iota((4 * count, 128), 0) + plane * 32 + 4 * first - SHIFT).astype(F32)
            tos.append(jnp.concatenate([hot(hub == edges[4 + c:5 + c, :]) for c in range(4)], axis=1))
        return jnp.concatenate(picks + [dot_nt(jnp.concatenate(tos, axis=0), fro).astype(BF16)], axis=0)

    def select(ref, idref):
        got = dot_nt(selector(idref, [(z, 0, PLANE)]), ref[...])
        msum[:, 0:WIDTH] += got[256:288, :]
        return got[0:256, :]

    def spread(sums):
        count = sums.shape[0] // 4
        row, col = iota((SLOTS * count, 4 * count), 0), iota((SLOTS * count, 4 * count), 1)
        return dot(hot((row // SLOTS == col // 4) & (row % SLOTS == 28 + col % 4)), sums.astype(BF16))

    def widen(tail):
        return jnp.concatenate([tail, jnp.zeros_like(tail)], axis=1)

    low = iota((256, 128), 1) < 64

    def put(step, way, got):
        ysend[step, :, 64 * way:64 * way + 32, :] = got[:, :128].astype(BF16).reshape(PLANE, SLOTS, 128)
        tail = widen(got[:, 128:])
        if way == 1:
            tail = ysend[step, :, 32:64, :].reshape(256, 128).astype(F32) + pltpu.roll(tail, 64, 1)
        ysend[step, :, 32:64, :] = tail.astype(BF16).reshape(PLANE, SLOTS, 128)

    def pick(step, way):
        slot = at(way, step)
        put(step, way, select(ring.at[slot], ringi.at[slot]))

    def last_rows(way, columns):
        wants = beyond(way)
        got = dot_nt(farsel[way], ring[at(way, reach), columns, :])
        counts = [want[3] for want in wants] + [PLANE]
        at_row, at_sum, found = 0, SLOTS * sum(counts), []
        for count in counts:
            found.append((got[at_row:at_row + SLOTS * count, :], got[at_sum:at_sum + 4 * count, :]))
            at_row, at_sum = at_row + SLOTS * count, at_sum + 4 * count
        return wants, found[:-1], found[-1]

    def send_late(wants, found, part):
        for (kind, plane, first, count), (rows, sums) in zip(wants, found):
            rows = rows + spread(sums)
            if part == 0:
                lsend[kind, first:first + count, 0:32, :] = rows.astype(BF16).reshape(count, SLOTS, 128)
            else:
                tail = widen(rows).reshape(count, 2, 16, 128)
                tail = tail[:, 0].reshape(16 * count, 128) + pltpu.roll(tail[:, 1].reshape(16 * count, 128), 64, 1)
                lsend[kind, first:first + count, 32:48, :] = tail.astype(BF16).reshape(count, 16, 128)
            for o in range(count):
                lcopy(kind, plane, first + (me + o) % count, part).start()

    def send(step, first=0, rows=96, sem=None):
        for o in (4, 5, 3, 2, 6, 1, 7):
            ycopy(step, o, first, rows, step if sem is None else sem).start()
        yrecv[step, me, first:first + rows, :] = ysend[step, me, first:first + rows, :]

    def placement(zz, sums=False):
        to = tgt[pl.ds(zz, 1), :]
        lane = iota((1, 256), 1) % SLOTS
        if sums:
            for j in range(4):
                to = jnp.where(lane == 28 + j, hub_local[0:1, j:j + 1].astype(F32), to)
        pos = iota((256, 512), 0)
        slot = pos % SLOTS
        hub = jnp.where((slot >= 24) & (slot < 28), zz * 32 + (pos // SLOTS) * 4 + slot - 24, -1)
        where = dot_nt(hub_hot[...], hot(hub == hub_s[...]))
        return (where + jnp.where(iota((512, 256), 0).astype(F32) == to, 1.0, 0.0)).astype(BF16)

    def place(step, way):
        rows = jnp.concatenate([yrecv[step, :, 64 * way:64 * way + 32, :].reshape(256, 128),
                                yrecv[step, :, 32:64, :].reshape(256, 128)], axis=1)
        acc = accp if way == 0 else accm
        acc[...] += dot(placement(at(way, step)), rows)

    def product(i, part):
        w = pl.multiple_of(i * WIDTH, 64)
        if part == 0:
            carry[...] += dot(xm[i, 0:512, :], wn[pl.ds(w, 128), :])
        else:
            b, zero = wn[pl.ds(w + 128, 64), :], jnp.zeros((64, 256), BF16)
            carry[0:256, :] += dot(xm[i, 512:768, :], jnp.concatenate([b, zero], axis=0))
            carry[256:512, :] += dot(xm[i, 512:768, :], jnp.concatenate([zero, b], axis=0))

    for load in loads[:4]:
        load.wait()
    raw[0:24, :] = (cs[...] - SHIFT).astype(F32)
    row = iota((8, 128), 0)
    hubs = jnp.full((8, 128), 640, I32)
    for j in range(4):
        hubs = jnp.where(row == j, hub_local[0:1, j:j + 1], hubs)
    raw[24:32, :] = (hubs - SHIFT).astype(F32)
    raw[32:36, :] = (mirror_f[...] - SHIFT).astype(F32)
    raw[36:40, :] = (mirror_t[...] - SHIFT).astype(F32)
    raw[40:48, :] = jnp.zeros((8, 128), F32)
    own[...] = raw[...].astype(BF16)

    pl.semaphore_wait(barrier, PLANE * (2 * DIRECT) - 1 + feats - 1)
    for piece in order:
        for way in (0, 1):
            zcopy(way, 0, piece).start()
    for o in range(1, feats):
        fcopy(o).start()

    for load in loads[4:]:
        load.wait()
    accp[...] = jnp.zeros_like(accp)
    accm[...] = jnp.zeros_like(accm)
    accl[...] = jnp.zeros_like(accl)
    msum[...] = jnp.zeros_like(msum)

    ysend[0, :, 64:96, :] = jnp.zeros((PLANE, SLOTS, 128), BF16)
    put(0, 0, select(ft, own))
    send(0)

    raw[0:24, :] = ct[...].astype(F32)
    raw[24:48, :] = jnp.full((24, 128), -1.0, F32)
    wide = jnp.transpose(jnp.concatenate([raw[0:32, :], jnp.full((96, 128), -1.0, F32)], axis=0))
    wide = wide[0:rings * PLANE, :].reshape(rings, PLANE, 128)
    lane = iota((rings, 128), 1)
    for part in (0, 1):
        whole = jnp.full((rings, 128), -1.0, F32)
        for d in range(4):
            one = wide[:, 4 * part + d, :]
            whole = jnp.where(lane // SLOTS == d, pltpu.roll(one, SLOTS * d, 1) if d else one, whole)
        tgt[:, 128 * part:128 * part + 128] = whole
    hub_hot[...] = hot(iota((512, 512), 0) == hub_t[...])

    places[:, 0:256] = placement(at(0, reach), True)
    places[:, 256:512] = placement(at(1, reach))
    for kind, (d, way) in enumerate(kinds):
        places[:, 512 + 256 * kind:768 + 256 * kind] = placement(at(way, d), True)

    for t in range(12):
        is_at = [[(tidx[i:i + 1, t:t + 1] == b).astype(F32) for b in range(4)] for i in (0, 1)]
        block = sum(ft[:, 128 * b:128 * b + 128].astype(F32) * is_at[1][b] for b in range(4)).astype(BF16)
        part = dot_nt(mask[t].astype(F32).astype(BF16), block)
        for b in range(4):
            accl[128 * b:128 * b + 128, 0:WIDTH] += part * is_at[0][b]

    forward(1, order)

    deg_row = deg[...].astype(F32)
    for i in range(4):
        degree[128 * i:128 * i + 128, :] = column(deg_row[i:i + 1, :])

    def own_columns():
        xf[x] = ft[...]
        for o in range(1, feats):
            farrived(o)
        carry[...] = jnp.zeros_like(carry) + bias[...]

        def one(i, _):
            carry[...] += dot_tn(xf[i], ws[pl.ds(pl.multiple_of(i * WIDTH, 64), WIDTH), :])
            return 0

        lax.fori_loop(0, feats, one, 0)

    def step(k, _):
        forward(k, order[:2])
        pick(k - 1, 0)
        forward(k, order[2:4])
        pick(k - 1, 1)
        forward(k, order[4:5])
        send(k - 1)
        forward(k, order[5:6])
        yarrived(k - 2)
        place(k - 2, 0)
        forward(k, order[6:7])
        place(k - 2, 1)

        @pl.when(k == half // 2)
        def _():
            own_columns()
        return 0

    lax.fori_loop(2, reach, step, 0)
    if not 2 <= half // 2 < reach:
        own_columns()

    k = reach
    pick(k - 1, 0)
    pick(k - 1, 1)
    send(k - 1)
    for way in (0, 1):
        zarrived(way, k, PIECES)
        farsel[way] = selector(ringi.at[at(way, k)], [want[1:] for want in beyond(way)] + [(z, 0, PLANE)])
    yarrived(k - 2)
    place(k - 2, 0)
    place(k - 2, 1)
    lead, rest, split = slice(0, 128), slice(128, WIDTH), 128 // PIECE
    near = []
    for way in (0, 1):
        for piece in range(split):
            zarrived(way, k, piece)
        wants, found, own_plane = last_rows(way, lead)
        send_late(wants, found, 0)
        near.append(own_plane)
    sums = msum[:, lead] + near[0][1] + near[1][1]
    ysend[k, :, 0:32, :] = (near[0][0] + spread(sums)).astype(BF16).reshape(PLANE, SLOTS, 128)
    ysend[k, :, 32:64, :] = near[1][0].astype(BF16).reshape(PLANE, SLOTS, 128)
    send(k, 0, 64)
    near = []
    for way in (0, 1):
        for piece in range(split, PIECES):
            zarrived(way, k, piece)
        wants, found, own_plane = last_rows(way, rest)
        send_late(wants, found, 1)
        near.append(own_plane)
    sums = msum[:, rest] + near[0][1] + near[1][1]
    tail = widen(near[0][0] + spread(sums)) + pltpu.roll(widen(near[1][0]), 64, 1)
    ysend[k, :, 64:96, :] = tail.astype(BF16).reshape(PLANE, SLOTS, 128)
    send(k, 64, 32, k + 1)
    yarrived(k - 1)
    place(k - 1, 0)
    place(k - 1, 1)

    for s in range(reach):
        for way in (0, 1):
            zsent(way, s)
        for o in range(1, PLANE):
            ycopy(s, o, 0, 96, s).wait_send()
    for o in range(1, feats):
        fcopy(o).wait_send()

    before = accp[:, lead] + accm[:, lead] + accl[:, lead]
    yarrived(k, 0, 64)
    lall(0).wait_recv()
    rows = jnp.concatenate([yrecv[k, :, 0:32, :].reshape(256, 128), yrecv[k, :, 32:64, :].reshape(256, 128)]
                           + [lrecv[kind, :, 0:32, :].reshape(256, 128) for kind in range(len(kinds))], axis=0)
    xm[x, 0:512, :] = ((before + dot(places[...], rows)) / degree[...]).astype(BF16)
    sent = []

    def tell(first):
        for part, o in ((0, 1), (1, -1), (1, 1), (0, -1)) if feats == 4 else [(p, o) for o in range(1, feats) for p in (0, 1)]:
            sent.append(mcopy(x, first + part, o, len(sent)))
            sent[-1].start()

    def relay(o, part):
        marrived(-o, part)
        sent.append(mcopy((x - o + feats) % feats, part, o, len(sent)))
        sent[-1].start()

    def done():
        lall(0).wait_send()
        lall(1).wait_send()
        for o in range(1, PLANE):
            ycopy(k, o, 0, 64, k).wait_send()
            ycopy(k, o, 64, 32, k + 1).wait_send()

    tell(0)
    product(x, 0)

    before = accp[:, 128:256] + pltpu.roll(accm[:, 128:256], 64, 1) + accl[:, 128:256]
    yarrived(k, 64, 32, k + 1)
    lall(1).wait_recv()
    both = yrecv[k, :, 64:96, :].reshape(256, 128)
    rows = [both, pltpu.roll(both.astype(F32), 64, 1).astype(BF16)]
    for kind in range(len(kinds)):
        tail = lrecv[kind, :, 32:48, :].astype(F32).reshape(128, 128)
        tail = jnp.concatenate([tail.reshape(PLANE, 1, 16, 128), pltpu.roll(tail, 64, 1).reshape(PLANE, 1, 16, 128)], axis=1)
        rows.append(tail.astype(BF16).reshape(256, 128))
    mean = (before + dot(places[...], jnp.concatenate(rows, axis=0))) / degree[...]
    xm[x, 512:768, :] = jnp.where(low, mean[0:256, :], pltpu.roll(mean[256:512, :], 64, 1)).astype(BF16)
    tell(2)
    if feats == 4:
        relay(1, 0)
        relay(-1, 1)
        relay(1, 2)
        relay(-1, 3)
        product(x, 1)
        done()
        marrived(-1, 1)
        product((x + 3) % 4, 0)
        marrived(1, 0)
        product((x + 1) % 4, 0)
        marrived(-1, 3)
        product((x + 3) % 4, 1)
        marrived(1, 2)
        product((x + 1) % 4, 1)
        marrived(2, 0)
        marrived(2, 1)
        product((x + 2) % 4, 0)
        marrived(2, 2)
        marrived(2, 3)
        product((x + 2) % 4, 1)
    else:
        product(x, 1)
        done()
        for o in range(1, feats):
            for part in range(4):
                marrived(o, part)
            product((x + o) % feats, 0)
            product((x + o) % feats, 1)
    out[...] = jnp.maximum(carry[...], 0.0).astype(BF16)

    for copy in sent:
        copy.wait_send()


def on_device(rings, feats, features, w_self, w_neigh, out_bias, degrees, tile_index, tile_mask, cut_source, cut_target,
              hub_local, hub_source, hub_target, mirror_source, mirror_target):
    half = rings // 2
    reach = half - DIRECT
    parts = rings * PLANE
    anywhere = pl.BlockSpec(memory_space=pl.ANY)
    args = (features.T, cut_source[0].T, cut_target[0].T, tile_index[0].T, hub_local, hub_target, hub_source,
            mirror_source.reshape(4, 128), mirror_target.reshape(4, 128), degrees.reshape(4, 128), out_bias.reshape(1, 256),
            tile_mask[0], w_self, w_neigh)
    if parts < 128:
        args = args[:1] + tuple(jnp.pad(a, ((0, 0), (0, 128 - parts))) for a in args[1:3]) + args[3:]
    return pl.pallas_call(
        functools.partial(kernel, rings, feats),
        out_shape=pltpu.VMEM((512, 256), BF16),
        in_specs=[anywhere] * len(args),
        out_specs=pl.BlockSpec(memory_space=pltpu.VMEM),
        scratch_shapes=[
            pltpu.VMEM((rings, WIDTH, 512), BF16),
            pltpu.VMEM((rings, IDS, 128), BF16),
            pltpu.VMEM((reach + 1, PLANE, 96, 128), BF16),
            pltpu.VMEM((reach + 1, PLANE, 96, 128), BF16),
            pltpu.VMEM((2 * DIRECT - 1, PLANE, 48, 128), BF16),
            pltpu.VMEM((2 * DIRECT - 1, PLANE, 48, 128), BF16),
            pltpu.VMEM((feats, WIDTH, 512), BF16),
            pltpu.VMEM((feats, 768, 128), BF16),
            pltpu.VMEM((512, 256), F32),
            pltpu.VMEM((512, 256), F32),
            pltpu.VMEM((512, 256), F32),
            pltpu.VMEM((32, 256), F32),
            pltpu.VMEM((512, 512), BF16),
            pltpu.VMEM((2, 36 * (8 * DIRECT + 4), 512), BF16),
            pltpu.VMEM((512, 256 * (2 * DIRECT + 1)), BF16),
            pltpu.VMEM((512, 128), F32),
            pltpu.VMEM((512, 256), F32),
            pltpu.VMEM((IDS, 128), BF16),
            pltpu.VMEM((rings, 256), F32),
            pltpu.VMEM((IDS, 128), F32),
        ] + [pltpu.VMEM(a.shape, a.dtype) for a in args] + [
            pltpu.SemaphoreType.DMA((2, reach, 2)),
            pltpu.SemaphoreType.DMA((rings, PIECES + 1)),
            pltpu.SemaphoreType.DMA((reach + 2, PLANE)),
            pltpu.SemaphoreType.DMA((reach + 2, PLANE)),
            pltpu.SemaphoreType.DMA((2,)),
            pltpu.SemaphoreType.DMA((2,)),
            pltpu.SemaphoreType.DMA((4,)),
            pltpu.SemaphoreType.DMA((4,)),
            pltpu.SemaphoreType.DMA((12,)),
            pltpu.SemaphoreType.DMA((4, 4)),
            pltpu.SemaphoreType.DMA((len(args),)),
        ],
        compiler_params=pltpu.CompilerParams(
            collective_id=0, has_side_effects=True, vmem_limit_bytes=60 * 1024 * 1024),
        cost_estimate=pl.CostEstimate(flops=10**10, bytes_accessed=4 * 10**6, transcendentals=0),
    )(*args)


def solution(mesh):
    return jax.shard_map(
        functools.partial(on_device, mesh.shape["dom"] // PLANE, mesh.shape["feat"]),
        mesh=mesh,
        in_specs=(P("dom", "feat"), P(None, "feat"), P(None, "feat"), P("feat"), P("dom"), P("dom"), P("dom"), P("dom"),
                  P("dom"), P("dom"), P("dom"), P("dom"), P("dom"), P("dom")),
        out_specs=P("dom", "feat"),
        check_vma=False,
    )
```

```python
import functools

import jax
import jax.numpy as jnp
from jax import lax
from jax.experimental import pallas as pl
from jax.experimental.pallas import tpu as pltpu
from jax.sharding import PartitionSpec as P

MESH = pl.DeviceIdType.MESH
BF16, F32, I32 = jnp.bfloat16, jnp.float32, jnp.int32
PLANE = 8
SLOTS = 32
WIDTH = 192
PIECES, PIECE = 6, 32
IDS = 48
DIRECT = 2
SHIFT = 256


def dot(a, b):
    return jnp.dot(a, b, preferred_element_type=F32)


def dot_nt(a, b):
    return lax.dot_general(a, b, (((1,), (1,)), ((), ())), preferred_element_type=F32)


def iota(shape, axis):
    return lax.broadcasted_iota(I32, shape, axis)


def hot(mask):
    return jnp.where(mask, 1.0, 0.0).astype(BF16)


def column(row):
    return jnp.transpose(jnp.broadcast_to(row, (128, 128)))


def dot_tn(a, b):
    return lax.dot_general(a, b, (((0,), (0,)), ((), ())), preferred_element_type=F32)


def kernel(rings, feats, ft_hbm, cs_hbm, ct_hbm, ti_hbm, hl_hbm, ht_hbm, hs_hbm, mf_hbm, mt_hbm, deg_hbm, bias_hbm,
           mask_hbm, ws_hbm, wn_hbm, out, ring, ringi, ysend, yrecv, lsend, lrecv, xf, xm, accp, accm, accl, msum, hub_hot, farsel, places, degree, spot, carry,
           own, tgt, raw, ft, cs, ct, tidx, hub_local, hub_t, hub_s, mirror_f, mirror_t, deg, bias, mask, ws, wn,
           zs, zr, ys, yr, ls, lr, fs, fr, ms, mr, local):
    half = rings // 2
    reach = half - DIRECT
    dom, x = lax.axis_index("dom"), lax.axis_index("feat")
    z, me = dom // PLANE, dom % PLANE
    up, down = ((z + 1) % rings) * PLANE + me, ((z + rings - 1) % rings) * PLANE + me

    barrier = pltpu.get_barrier_semaphore()
    def greet(plane, dest):
        pl.semaphore_signal(barrier, inc=1, device_id=(plane * PLANE + dest, x), device_id_type=MESH)

    for o in range(PLANE):
        if o:
            greet(z, (me + o) % PLANE)
        if DIRECT > 1:
            greet((z + 1) % rings, (me + o) % PLANE)
            greet((z + rings - 1) % rings, (me + o) % PLANE)
        greet((z + rings - DIRECT + 2 * DIRECT * (me // 4)) % rings, (me + o) % PLANE)
    for o in range(1, feats):
        pl.semaphore_signal(barrier, inc=1, device_id=(dom, (x + o) % feats), device_id_type=MESH)

    loads = [pltpu.make_async_copy(src, dst, local.at[i]) for i, (src, dst) in enumerate((
        (cs_hbm, cs), (hl_hbm, hub_local), (mf_hbm, mirror_f), (mt_hbm, mirror_t), (ft_hbm, ft), (ct_hbm, ct), (ti_hbm, tidx),
        (ht_hbm, hub_t), (hs_hbm, hub_s), (deg_hbm, deg), (bias_hbm, bias), (mask_hbm, mask), (ws_hbm, ws), (wn_hbm, wn)))]
    for load in loads:
        load.start()

    def at(way, step):
        return (z + rings - step) % rings if way == 0 else (z + step) % rings

    def zcopy(way, step, piece):
        slot = at(way, step)
        if piece == PIECES:
            src, dst = own if isinstance(step, int) and step == 0 else ringi.at[slot], ringi.at[slot]
        else:
            rows = pl.ds(piece * PIECE, PIECE)
            src = ft_hbm.at[rows] if isinstance(step, int) and step == 0 else ring.at[slot, rows]
            dst = ring.at[slot, rows]
        return pltpu.make_async_remote_copy(
            src_ref=src, dst_ref=dst, send_sem=zs.at[way, step, piece // PIECES], recv_sem=zr.at[slot, piece],
            device_id=(up if way == 0 else down, x), device_id_type=MESH)

    def zarrived(way, step, piece):
        slot = at(way, step)
        ref = ringi.at[slot] if piece == PIECES else ring.at[slot, pl.ds(piece * PIECE, PIECE)]
        pltpu.make_async_remote_copy(
            src_ref=ref, dst_ref=ref, send_sem=zs.at[way, 0, piece // PIECES], recv_sem=zr.at[slot, piece],
            device_id=(up, x), device_id_type=MESH).wait_recv()

    order = (PIECES,) + tuple(range(PIECES))

    def zsent(way, step):
        slot = at(way, step)
        for ref, sem in ((ring.at[slot], 0), (ringi.at[slot], 1)):
            pltpu.make_async_remote_copy(
                src_ref=ref, dst_ref=ref, send_sem=zs.at[way, step, sem], recv_sem=zr.at[slot, 0],
                device_id=(up, x), device_id_type=MESH).wait_send()

    def forward(step, pieces):
        for piece in pieces:
            for way in (0, 1):
                zarrived(way, step, piece)
                zcopy(way, step, piece).start()

    def ycopy(step, o, first, rows, sem):
        dest = (me + o) % PLANE
        return pltpu.make_async_remote_copy(
            src_ref=ysend.at[step, dest, pl.ds(first, rows)], dst_ref=yrecv.at[step, me, pl.ds(first, rows)],
            send_sem=ys.at[sem, o - 1], recv_sem=yr.at[sem, me],
            device_id=(z * PLANE + dest, x), device_id_type=MESH)

    def yarrived(step, first=0, rows=96, sem=None):
        for o in range(1, PLANE):
            src = (me + o) % PLANE
            ref = yrecv.at[step, src, pl.ds(first, rows)]
            pltpu.make_async_remote_copy(
                src_ref=ref, dst_ref=ref, send_sem=ys.at[step, o - 1], recv_sem=yr.at[step if sem is None else sem, src],
                device_id=(z * PLANE + src, x), device_id_type=MESH).wait_recv()

    kinds = [(d, way) for d in range(reach + 1, half) for way in (0, 1)] + [(half, 0)]

    def beyond(way):
        wants = []
        for d in range(reach + 1, half + 1):
            plane = (z + d - reach) % rings if way == 0 else (z + rings - d + reach) % rings
            wants.append((kinds.index((d, way)), plane, 0, 8) if d < half else (len(kinds) - 1, plane, 4 * way, 4))
        return wants

    late = (pl.ds(0, 32), pl.ds(32, 16))

    def lcopy(kind, plane, dest, part):
        return pltpu.make_async_remote_copy(
            src_ref=lsend.at[kind, dest, late[part]], dst_ref=lrecv.at[kind, me, late[part]],
            send_sem=ls.at[part], recv_sem=lr.at[part],
            device_id=(plane * PLANE + dest, x), device_id_type=MESH)

    def lall(part):
        return pltpu.make_async_remote_copy(
            src_ref=lsend.at[:, :, late[part]], dst_ref=lrecv.at[:, :, late[part]], send_sem=ls.at[part], recv_sem=lr.at[part],
            device_id=(up, x), device_id_type=MESH)

    def fcopy(o):
        return pltpu.make_async_remote_copy(
            src_ref=ft_hbm, dst_ref=xf.at[x], send_sem=fs.at[o - 1], recv_sem=fr.at[x],
            device_id=(dom, (x + o) % feats), device_id_type=MESH)

    def farrived(o):
        src = (x + o) % feats
        pltpu.make_async_remote_copy(
            src_ref=ft_hbm, dst_ref=xf.at[src], send_sem=fs.at[o - 1], recv_sem=fr.at[src],
            device_id=(dom, src), device_id_type=MESH).wait_recv()

    parts = (pl.ds(0, 256), pl.ds(256, 256), pl.ds(512, 128), pl.ds(640, 128))

    def mcopy(src, part, o, sem):
        return pltpu.make_async_remote_copy(
            src_ref=xm.at[src, parts[part]], dst_ref=xm.at[src, parts[part]], send_sem=ms.at[sem], recv_sem=mr.at[src, part],
            device_id=(dom, (x + o + feats) % feats), device_id_type=MESH)

    def marrived(o, part):
        mcopy((x + o + feats) % feats, part, 1, 0).wait_recv()

    def selector(idref, wants):
        ids = idref[0:32, :].astype(F32)
        lane = iota((32, 512), 1).astype(F32) - SHIFT
        edges = idref[32:48, :].astype(F32)
        node = (iota((512, 128), 0) - SHIFT).astype(F32)
        fro = jnp.concatenate([hot(node == edges[c:c + 1, :]) for c in range(4)], axis=1)
        picks, tos = [], []
        for plane, first, count in wants:
            here = pltpu.roll(ids, (128 - PLANE * plane) % 128, 1)
            picks += [hot(here[:, d:d + 1] == lane) for d in range(first, first + count)]
            hub = (iota((4 * count, 128), 0) + plane * 32 + 4 * first - SHIFT).astype(F32)
            tos.append(jnp.concatenate([hot(hub == edges[4 + c:5 + c, :]) for c in range(4)], axis=1))
        return jnp.concatenate(picks + [dot_nt(jnp.concatenate(tos, axis=0), fro).astype(BF16)], axis=0)

    def select(ref, idref):
        got = dot_nt(selector(idref, [(z, 0, PLANE)]), ref[...])
        msum[:, 0:WIDTH] += got[256:288, :]
        return got[0:256, :]

    def spread(sums):
        count = sums.shape[0] // 4
        return dot(spot[0:SLOTS * count, 0:4 * count], sums.astype(BF16))

    def widen(tail):
        return jnp.concatenate([tail, jnp.zeros_like(tail)], axis=1)

    low = iota((256, 128), 1) < 64

    def put(step, way, got):
        ysend[step, :, 64 * way:64 * way + 32, :] = got[:, :128].astype(BF16).reshape(PLANE, SLOTS, 128)
        tail = widen(got[:, 128:])
        if way == 1:
            tail = ysend[step, :, 32:64, :].reshape(256, 128).astype(F32) + pltpu.roll(tail, 64, 1)
        ysend[step, :, 32:64, :] = tail.astype(BF16).reshape(PLANE, SLOTS, 128)

    def pick(step, way):
        slot = at(way, step)
        put(step, way, select(ring.at[slot], ringi.at[slot]))

    def last_rows(way, columns):
        wants = beyond(way)
        got = dot_nt(farsel[way], ring[at(way, reach), columns, :])
        counts = [want[3] for want in wants] + [PLANE]
        at_row, at_sum, found = 0, SLOTS * sum(counts), []
        for count in counts:
            found.append((got[at_row:at_row + SLOTS * count, :], got[at_sum:at_sum + 4 * count, :]))
            at_row, at_sum = at_row + SLOTS * count, at_sum + 4 * count
        return wants, found[:-1], found[-1]

    def send_late(wants, found, part):
        for (kind, plane, first, count), (rows, sums) in zip(wants, found):
            rows = rows + spread(sums)
            if part == 0:
                lsend[kind, first:first + count, 0:32, :] = rows.astype(BF16).reshape(count, SLOTS, 128)
            else:
                tail = widen(rows).reshape(count, 2, 16, 128)
                tail = tail[:, 0].reshape(16 * count, 128) + pltpu.roll(tail[:, 1].reshape(16 * count, 128), 64, 1)
                lsend[kind, first:first + count, 32:48, :] = tail.astype(BF16).reshape(count, 16, 128)
            for o in range(count):
                lcopy(kind, plane, first + (me + o) % count, part).start()

    def send(step, first=0, rows=96, sem=None):
        for o in (4, 5, 3, 2, 6, 1, 7):
            ycopy(step, o, first, rows, step if sem is None else sem).start()
        yrecv[step, me, first:first + rows, :] = ysend[step, me, first:first + rows, :]

    def placement(zz, sums=False):
        to = tgt[pl.ds(zz, 1), :]
        lane = iota((1, 256), 1) % SLOTS
        if sums:
            for j in range(4):
                to = jnp.where(lane == 28 + j, hub_local[0:1, j:j + 1].astype(F32), to)
        pos = iota((256, 512), 0)
        slot = pos % SLOTS
        hub = jnp.where((slot >= 24) & (slot < 28), zz * 32 + (pos // SLOTS) * 4 + slot - 24, -1)
        where = dot_nt(hub_hot[...], hot(hub == hub_s[...]))
        return (where + jnp.where(iota((512, 256), 0).astype(F32) == to, 1.0, 0.0)).astype(BF16)

    def place(step, way):
        rows = jnp.concatenate([yrecv[step, :, 64 * way:64 * way + 32, :].reshape(256, 128),
                                yrecv[step, :, 32:64, :].reshape(256, 128)], axis=1)
        acc = accp if way == 0 else accm
        acc[...] += dot(placement(at(way, step)), rows)

    def product(i, part):
        w = pl.multiple_of(i * WIDTH, 64)
        if part == 0:
            carry[...] += dot(xm[i, 0:512, :], wn[pl.ds(w, 128), :])
        else:
            b, zero = wn[pl.ds(w + 128, 64), :], jnp.zeros((64, 256), BF16)
            carry[0:256, :] += dot(xm[i, 512:768, :], jnp.concatenate([b, zero], axis=0))
            carry[256:512, :] += dot(xm[i, 512:768, :], jnp.concatenate([zero, b], axis=0))

    for load in loads[:4]:
        load.wait()
    raw[0:24, :] = (cs[...] - SHIFT).astype(F32)
    row = iota((8, 128), 0)
    hubs = jnp.full((8, 128), 640, I32)
    for j in range(4):
        hubs = jnp.where(row == j, hub_local[0:1, j:j + 1], hubs)
    raw[24:32, :] = (hubs - SHIFT).astype(F32)
    raw[32:36, :] = (mirror_f[...] - SHIFT).astype(F32)
    raw[36:40, :] = (mirror_t[...] - SHIFT).astype(F32)
    raw[40:48, :] = jnp.zeros((8, 128), F32)
    own[...] = raw[...].astype(BF16)

    pl.semaphore_wait(barrier, PLANE * (2 * DIRECT) - 1 + feats - 1)
    for piece in order:
        for way in (0, 1):
            zcopy(way, 0, piece).start()
    for o in range(1, feats):
        fcopy(o).start()

    for load in loads[4:]:
        load.wait()
    accp[...] = jnp.zeros_like(accp)
    accm[...] = jnp.zeros_like(accm)
    accl[...] = jnp.zeros_like(accl)
    msum[...] = jnp.zeros_like(msum)

    ysend[0, :, 64:96, :] = jnp.zeros((PLANE, SLOTS, 128), BF16)
    put(0, 0, select(ft, own))
    send(0)

    raw[0:24, :] = ct[...].astype(F32)
    raw[24:48, :] = jnp.full((24, 128), -1.0, F32)
    wide = jnp.transpose(jnp.concatenate([raw[0:32, :], jnp.full((96, 128), -1.0, F32)], axis=0))
    wide = wide[0:rings * PLANE, :].reshape(rings, PLANE, 128)
    lane = iota((rings, 128), 1)
    for part in (0, 1):
        whole = jnp.full((rings, 128), -1.0, F32)
        for d in range(4):
            one = wide[:, 4 * part + d, :]
            whole = jnp.where(lane // SLOTS == d, pltpu.roll(one, SLOTS * d, 1) if d else one, whole)
        tgt[:, 128 * part:128 * part + 128] = whole
    hub_hot[...] = hot(iota((512, 512), 0) == hub_t[...])
    row, col = iota((256, 32), 0), iota((256, 32), 1)
    spot[...] = hot((row // SLOTS == col // 4) & (row % SLOTS == 28 + col % 4))

    def tiles(first, last):
        for t in range(first, last):
            is_at = [[(tidx[i:i + 1, t:t + 1] == b).astype(F32) for b in range(4)] for i in (0, 1)]
            block = sum(ft[:, 128 * b:128 * b + 128].astype(F32) * is_at[1][b] for b in range(4)).astype(BF16)
            part = dot_nt(mask[t].astype(F32).astype(BF16), block)
            for b in range(4):
                accl[128 * b:128 * b + 128, 0:WIDTH] += part * is_at[0][b]

    def last_place(i):
        if i < 2:
            places[:, 256 * i:256 * i + 256] = placement(at(i, reach), i == 0)
        else:
            d, way = kinds[i - 2]
            places[:, 256 * i:256 * i + 256] = placement(at(way, d), True)

    tiles(0, 3)
    forward(1, order[0:2])
    tiles(3, 6)
    forward(1, order[2:3])
    tiles(6, 9)
    forward(1, order[3:4])
    tiles(9, 12)
    forward(1, order[4:5])
    last_place(0)
    last_place(1)
    forward(1, order[5:6])
    last_place(2)
    forward(1, order[6:7])
    for i in range(3, 2 + len(kinds)):
        last_place(i)

    deg_row = deg[...].astype(F32)
    for i in range(4):
        degree[128 * i:128 * i + 128, :] = column(deg_row[i:i + 1, :])

    def own_columns(o):
        i = (x + o) % feats
        if isinstance(o, int) and o == 0:
            xf[x] = ft[...]
            carry[...] = jnp.zeros_like(carry) + bias[...]
        else:
            farrived(o)
        carry[...] += dot_tn(xf[i], ws[pl.ds(pl.multiple_of(i * WIDTH, 64), WIDTH), :])

    own_columns(0)

    def step(k, _):
        forward(k, order[:2])
        pick(k - 1, 0)
        forward(k, order[2:4])
        pick(k - 1, 1)
        forward(k, order[4:5])
        send(k - 1)
        forward(k, order[5:6])

        @pl.when(k >= 3)
        def _():
            yarrived(k - 3)
            place(k - 3, 0)
        forward(k, order[6:7])

        @pl.when(k >= 3)
        def _():
            place(k - 3, 1)

        @pl.when(k - 1 < feats)
        def _():
            own_columns(k - 1)
        return 0

    lax.fori_loop(2, reach, step, 0)
    for o in range(max(1, reach - 1), feats):
        own_columns(o)

    k = reach
    pick(k - 1, 0)
    pick(k - 1, 1)
    send(k - 1)
    for way in (0, 1):
        zarrived(way, k, PIECES)
        farsel[way] = selector(ringi.at[at(way, k)], [want[1:] for want in beyond(way)] + [(z, 0, PLANE)])
    for s in range(max(0, k - 3), k - 1):
        yarrived(s)
        place(s, 0)
        place(s, 1)
    lead, rest, split = slice(0, 128), slice(128, WIDTH), 128 // PIECE
    near = []
    for way in (0, 1):
        for piece in range(split):
            zarrived(way, k, piece)
        wants, found, own_plane = last_rows(way, lead)
        send_late(wants, found, 0)
        near.append(own_plane)
    sums = msum[:, lead] + near[0][1] + near[1][1]
    ysend[k, :, 0:32, :] = (near[0][0] + spread(sums)).astype(BF16).reshape(PLANE, SLOTS, 128)
    ysend[k, :, 32:64, :] = near[1][0].astype(BF16).reshape(PLANE, SLOTS, 128)
    send(k, 0, 64)
    near = []
    for way in (0, 1):
        for piece in range(split, PIECES):
            zarrived(way, k, piece)
        wants, found, own_plane = last_rows(way, rest)
        send_late(wants, found, 1)
        near.append(own_plane)
    sums = msum[:, rest] + near[0][1] + near[1][1]
    tail = widen(near[0][0] + spread(sums)) + pltpu.roll(widen(near[1][0]), 64, 1)
    ysend[k, :, 64:96, :] = tail.astype(BF16).reshape(PLANE, SLOTS, 128)
    send(k, 64, 32, k + 1)
    yarrived(k - 1)
    place(k - 1, 0)
    place(k - 1, 1)

    for s in range(reach):
        for way in (0, 1):
            zsent(way, s)
        for o in range(1, PLANE):
            ycopy(s, o, 0, 96, s).wait_send()
    for o in range(1, feats):
        fcopy(o).wait_send()

    before = accp[:, lead] + accm[:, lead] + accl[:, lead]
    yarrived(k, 0, 64)
    lall(0).wait_recv()
    rows = jnp.concatenate([yrecv[k, :, 0:32, :].reshape(256, 128), yrecv[k, :, 32:64, :].reshape(256, 128)]
                           + [lrecv[kind, :, 0:32, :].reshape(256, 128) for kind in range(len(kinds))], axis=0)
    xm[x, 0:512, :] = ((before + dot(places[...], rows)) / degree[...]).astype(BF16)
    sent = []

    def tell(first):
        for part, o in ((0, 1), (1, -1), (1, 1), (0, -1)) if feats == 4 else [(p, o) for o in range(1, feats) for p in (0, 1)]:
            sent.append(mcopy(x, first + part, o, len(sent)))
            sent[-1].start()

    def relay(o, part):
        marrived(-o, part)
        sent.append(mcopy((x - o + feats) % feats, part, o, len(sent)))
        sent[-1].start()

    def done():
        lall(0).wait_send()
        lall(1).wait_send()
        for o in range(1, PLANE):
            ycopy(k, o, 0, 64, k).wait_send()
            ycopy(k, o, 64, 32, k + 1).wait_send()

    tell(0)
    product(x, 0)

    before = accp[:, 128:256] + pltpu.roll(accm[:, 128:256], 64, 1) + accl[:, 128:256]
    yarrived(k, 64, 32, k + 1)
    lall(1).wait_recv()
    both = yrecv[k, :, 64:96, :].reshape(256, 128)
    rows = [both, pltpu.roll(both.astype(F32), 64, 1).astype(BF16)]
    for kind in range(len(kinds)):
        tail = lrecv[kind, :, 32:48, :].astype(F32).reshape(128, 128)
        tail = jnp.concatenate([tail.reshape(PLANE, 1, 16, 128), pltpu.roll(tail, 64, 1).reshape(PLANE, 1, 16, 128)], axis=1)
        rows.append(tail.astype(BF16).reshape(256, 128))
    mean = (before + dot(places[...], jnp.concatenate(rows, axis=0))) / degree[...]
    xm[x, 512:768, :] = jnp.where(low, mean[0:256, :], pltpu.roll(mean[256:512, :], 64, 1)).astype(BF16)
    tell(2)
    if feats == 4:
        relay(1, 0)
        relay(-1, 1)
        relay(1, 2)
        relay(-1, 3)
        product(x, 1)
        done()
        marrived(-1, 1)
        product((x + 3) % 4, 0)
        marrived(1, 0)
        product((x + 1) % 4, 0)
        marrived(-1, 3)
        product((x + 3) % 4, 1)
        marrived(1, 2)
        product((x + 1) % 4, 1)
        marrived(2, 0)
        marrived(2, 1)
        product((x + 2) % 4, 0)
        marrived(2, 2)
        marrived(2, 3)
        product((x + 2) % 4, 1)
    else:
        product(x, 1)
        done()
        for o in range(1, feats):
            for part in range(4):
                marrived(o, part)
            product((x + o) % feats, 0)
            product((x + o) % feats, 1)
    out[...] = jnp.maximum(carry[...], 0.0).astype(BF16)

    for copy in sent:
        copy.wait_send()


def on_device(rings, feats, features, w_self, w_neigh, out_bias, degrees, tile_index, tile_mask, cut_source, cut_target,
              hub_local, hub_source, hub_target, mirror_source, mirror_target):
    half = rings // 2
    reach = half - DIRECT
    parts = rings * PLANE
    anywhere = pl.BlockSpec(memory_space=pl.ANY)
    args = (features.T, cut_source[0].T, cut_target[0].T, tile_index[0].T, hub_local, hub_target, hub_source,
            mirror_source.reshape(4, 128), mirror_target.reshape(4, 128), degrees.reshape(4, 128), out_bias.reshape(1, 256),
            tile_mask[0], w_self, w_neigh)
    if parts < 128:
        args = args[:1] + tuple(jnp.pad(a, ((0, 0), (0, 128 - parts))) for a in args[1:3]) + args[3:]
    return pl.pallas_call(
        functools.partial(kernel, rings, feats),
        out_shape=pltpu.VMEM((512, 256), BF16),
        in_specs=[anywhere] * len(args),
        out_specs=pl.BlockSpec(memory_space=pltpu.VMEM),
        scratch_shapes=[
            pltpu.VMEM((rings, WIDTH, 512), BF16),
            pltpu.VMEM((rings, IDS, 128), BF16),
            pltpu.VMEM((reach + 1, PLANE, 96, 128), BF16),
            pltpu.VMEM((reach + 1, PLANE, 96, 128), BF16),
            pltpu.VMEM((2 * DIRECT - 1, PLANE, 48, 128), BF16),
            pltpu.VMEM((2 * DIRECT - 1, PLANE, 48, 128), BF16),
            pltpu.VMEM((feats, WIDTH, 512), BF16),
            pltpu.VMEM((feats, 768, 128), BF16),
            pltpu.VMEM((512, 256), F32),
            pltpu.VMEM((512, 256), F32),
            pltpu.VMEM((512, 256), F32),
            pltpu.VMEM((32, 256), F32),
            pltpu.VMEM((512, 512), BF16),
            pltpu.VMEM((2, 36 * (8 * DIRECT + 4), 512), BF16),
            pltpu.VMEM((512, 256 * (2 * DIRECT + 1)), BF16),
            pltpu.VMEM((512, 128), F32),
            pltpu.VMEM((256, 32), BF16),
            pltpu.VMEM((512, 256), F32),
            pltpu.VMEM((IDS, 128), BF16),
            pltpu.VMEM((rings, 256), F32),
            pltpu.VMEM((IDS, 128), F32),
        ] + [pltpu.VMEM(a.shape, a.dtype) for a in args] + [
            pltpu.SemaphoreType.DMA((2, reach, 2)),
            pltpu.SemaphoreType.DMA((rings, PIECES + 1)),
            pltpu.SemaphoreType.DMA((reach + 2, PLANE)),
            pltpu.SemaphoreType.DMA((reach + 2, PLANE)),
            pltpu.SemaphoreType.DMA((2,)),
            pltpu.SemaphoreType.DMA((2,)),
            pltpu.SemaphoreType.DMA((4,)),
            pltpu.SemaphoreType.DMA((4,)),
            pltpu.SemaphoreType.DMA((12,)),
            pltpu.SemaphoreType.DMA((4, 4)),
            pltpu.SemaphoreType.DMA((len(args),)),
        ],
        compiler_params=pltpu.CompilerParams(
            collective_id=0, has_side_effects=True, vmem_limit_bytes=60 * 1024 * 1024),
        cost_estimate=pl.CostEstimate(flops=10**10, bytes_accessed=4 * 10**6, transcendentals=0),
    )(*args)


def solution(mesh):
    return jax.shard_map(
        functools.partial(on_device, mesh.shape["dom"] // PLANE, mesh.shape["feat"]),
        mesh=mesh,
        in_specs=(P("dom", "feat"), P(None, "feat"), P(None, "feat"), P("feat"), P("dom"), P("dom"), P("dom"), P("dom"),
                  P("dom"), P("dom"), P("dom"), P("dom"), P("dom"), P("dom")),
        out_specs=P("dom", "feat"),
        check_vma=False,
    )
```

```python
import functools

import jax
import jax.numpy as jnp
from jax import lax
from jax.experimental import pallas as pl
from jax.experimental.pallas import tpu as pltpu
from jax.sharding import PartitionSpec as P

MESH = pl.DeviceIdType.MESH
BF16, F32, I32 = jnp.bfloat16, jnp.float32, jnp.int32
PLANE = 8
SLOTS = 32
WIDTH = 192
PIECES, PIECE = 6, 32
IDS = 48
DIRECT = 2
SHIFT = 256


def dot(a, b):
    return jnp.dot(a, b, preferred_element_type=F32)


def dot_nt(a, b):
    return lax.dot_general(a, b, (((1,), (1,)), ((), ())), preferred_element_type=F32)


def iota(shape, axis):
    return lax.broadcasted_iota(I32, shape, axis)


def hot(mask):
    return jnp.where(mask, 1.0, 0.0).astype(BF16)


def column(row):
    return jnp.transpose(jnp.broadcast_to(row, (128, 128)))


def dot_tn(a, b):
    return lax.dot_general(a, b, (((0,), (0,)), ((), ())), preferred_element_type=F32)


def kernel(rings, feats, ft_hbm, cs_hbm, ct_hbm, ti_hbm, hl_hbm, ht_hbm, hs_hbm, mf_hbm, mt_hbm, deg_hbm, bias_hbm,
           mask_hbm, ws_hbm, wn_hbm, out, ring, ringi, ysend, yrecv, lsend, lrecv, xf, xm, accp, accm, accl, msum, hub_hot, farsel, places, degree, spot, carry,
           own, tgt, raw, ft, cs, ct, tidx, hub_local, hub_t, hub_s, mirror_f, mirror_t, deg, bias, mask, ws, wn,
           zs, zr, ys, yr, ls, lr, fs, fr, ms, mr, local):
    half = rings // 2
    reach = half - DIRECT
    dom, x = lax.axis_index("dom"), lax.axis_index("feat")
    z, me = dom // PLANE, dom % PLANE
    up, down = ((z + 1) % rings) * PLANE + me, ((z + rings - 1) % rings) * PLANE + me

    barrier = pltpu.get_barrier_semaphore()
    def greet(plane, dest):
        pl.semaphore_signal(barrier, inc=1, device_id=(plane * PLANE + dest, x), device_id_type=MESH)

    for o in range(PLANE):
        if o:
            greet(z, (me + o) % PLANE)
        if DIRECT > 1:
            greet((z + 1) % rings, (me + o) % PLANE)
            greet((z + rings - 1) % rings, (me + o) % PLANE)
        greet((z + rings - DIRECT + 2 * DIRECT * (me // 4)) % rings, (me + o) % PLANE)
    for o in range(1, feats):
        pl.semaphore_signal(barrier, inc=1, device_id=(dom, (x + o) % feats), device_id_type=MESH)

    loads = [pltpu.make_async_copy(src, dst, local.at[i]) for i, (src, dst) in enumerate((
        (cs_hbm, cs), (hl_hbm, hub_local), (mf_hbm, mirror_f), (mt_hbm, mirror_t), (ft_hbm, ft), (ct_hbm, ct), (ti_hbm, tidx),
        (ht_hbm, hub_t), (hs_hbm, hub_s), (deg_hbm, deg), (bias_hbm, bias), (mask_hbm, mask), (ws_hbm, ws), (wn_hbm, wn)))]
    for load in loads:
        load.start()

    def at(way, step):
        return (z + rings - step) % rings if way == 0 else (z + step) % rings

    def zcopy(way, step, piece):
        slot = at(way, step)
        if piece == PIECES:
            src, dst = own if isinstance(step, int) and step == 0 else ringi.at[slot], ringi.at[slot]
        else:
            rows = pl.ds(piece * PIECE, PIECE)
            src = ft_hbm.at[rows] if isinstance(step, int) and step == 0 else ring.at[slot, rows]
            dst = ring.at[slot, rows]
        return pltpu.make_async_remote_copy(
            src_ref=src, dst_ref=dst, send_sem=zs.at[piece // PIECES], recv_sem=zr.at[slot, piece],
            device_id=(up if way == 0 else down, x), device_id_type=MESH)

    def zarrived(way, step, piece):
        slot = at(way, step)
        ref = ringi.at[slot] if piece == PIECES else ring.at[slot, pl.ds(piece * PIECE, PIECE)]
        pltpu.make_async_remote_copy(
            src_ref=ref, dst_ref=ref, send_sem=zs.at[0], recv_sem=zr.at[slot, piece],
            device_id=(up, x), device_id_type=MESH).wait_recv()

    order = (PIECES,) + tuple(range(PIECES))

    def zsent():
        for buf, sem in ((ring, 0), (ringi, 1)):
            ref = buf.at[pl.ds(0, 2 * reach)]
            pltpu.make_async_remote_copy(
                src_ref=ref, dst_ref=ref, send_sem=zs.at[sem], recv_sem=zr.at[0, 0],
                device_id=(up, x), device_id_type=MESH).wait_send()

    def forward(step, pieces):
        for piece in pieces:
            for way in (0, 1):
                zarrived(way, step, piece)
                zcopy(way, step, piece).start()

    def ycopy(step, o, first, rows, sem):
        dest = (me + o) % PLANE
        return pltpu.make_async_remote_copy(
            src_ref=ysend.at[step, dest, pl.ds(first, rows)], dst_ref=yrecv.at[step, me, pl.ds(first, rows)],
            send_sem=ys.at[sem], recv_sem=yr.at[sem],
            device_id=(z * PLANE + dest, x), device_id_type=MESH)

    def yall(step, first=0, rows=96, sem=None):
        sem = step if sem is None else sem
        return pltpu.make_async_remote_copy(
            src_ref=ysend.at[step, pl.ds(0, PLANE - 1), pl.ds(first, rows)],
            dst_ref=yrecv.at[step, pl.ds(0, PLANE - 1), pl.ds(first, rows)],
            send_sem=ys.at[sem], recv_sem=yr.at[sem], device_id=(up, x), device_id_type=MESH)

    def yarrived(step, first=0, rows=96, sem=None):
        yall(step, first, rows, sem).wait_recv()

    kinds = [(d, way) for d in range(reach + 1, half) for way in (0, 1)] + [(half, 0)]

    def beyond(way):
        wants = []
        for d in range(reach + 1, half + 1):
            plane = (z + d - reach) % rings if way == 0 else (z + rings - d + reach) % rings
            wants.append((kinds.index((d, way)), plane, 0, 8) if d < half else (len(kinds) - 1, plane, 4 * way, 4))
        return wants

    late = (pl.ds(0, 32), pl.ds(32, 16))

    def lcopy(kind, plane, dest, part):
        return pltpu.make_async_remote_copy(
            src_ref=lsend.at[kind, dest, late[part]], dst_ref=lrecv.at[kind, me, late[part]],
            send_sem=ls.at[part], recv_sem=lr.at[part],
            device_id=(plane * PLANE + dest, x), device_id_type=MESH)

    def lall(part):
        return pltpu.make_async_remote_copy(
            src_ref=lsend.at[:, :, late[part]], dst_ref=lrecv.at[:, :, late[part]], send_sem=ls.at[part], recv_sem=lr.at[part],
            device_id=(up, x), device_id_type=MESH)

    def fcopy(o):
        return pltpu.make_async_remote_copy(
            src_ref=ft_hbm, dst_ref=xf.at[x], send_sem=fs.at[o - 1], recv_sem=fr.at[x],
            device_id=(dom, (x + o) % feats), device_id_type=MESH)

    def farrived(o):
        src = (x + o) % feats
        pltpu.make_async_remote_copy(
            src_ref=ft_hbm, dst_ref=xf.at[src], send_sem=fs.at[o - 1], recv_sem=fr.at[src],
            device_id=(dom, src), device_id_type=MESH).wait_recv()

    parts = (pl.ds(0, 256), pl.ds(256, 256), pl.ds(512, 128), pl.ds(640, 128))

    def mcopy(src, part, o, sem):
        return pltpu.make_async_remote_copy(
            src_ref=xm.at[src, parts[part]], dst_ref=xm.at[src, parts[part]], send_sem=ms.at[sem], recv_sem=mr.at[src, part],
            device_id=(dom, (x + o + feats) % feats), device_id_type=MESH)

    def marrived(o, part):
        mcopy((x + o + feats) % feats, part, 1, 0).wait_recv()

    def selector(idref, wants):
        ids = idref[0:32, :].astype(F32)
        lane = iota((32, 512), 1).astype(F32) - SHIFT
        edges = idref[32:48, :].astype(F32)
        node = (iota((512, 128), 0) - SHIFT).astype(F32)
        fro = jnp.concatenate([hot(node == edges[c:c + 1, :]) for c in range(4)], axis=1)
        picks, tos = [], []
        for plane, first, count in wants:
            here = pltpu.roll(ids, (128 - PLANE * plane) % 128, 1)
            picks += [hot(here[:, d:d + 1] == lane) for d in range(first, first + count)]
            hub = (iota((4 * count, 128), 0) + plane * 32 + 4 * first - SHIFT).astype(F32)
            tos.append(jnp.concatenate([hot(hub == edges[4 + c:5 + c, :]) for c in range(4)], axis=1))
        return jnp.concatenate(picks + [dot_nt(jnp.concatenate(tos, axis=0), fro).astype(BF16)], axis=0)

    def select(ref, idref):
        got = dot_nt(selector(idref, [(z, 0, PLANE)]), ref[...])
        msum[:, 0:WIDTH] += got[256:288, :]
        return got[0:256, :]

    def spread(sums):
        count = sums.shape[0] // 4
        return dot(spot[0:SLOTS * count, 0:4 * count], sums.astype(BF16))

    def widen(tail):
        return jnp.concatenate([tail, jnp.zeros_like(tail)], axis=1)

    low = iota((256, 128), 1) < 64

    def put(step, way, got):
        ysend[step, :, 64 * way:64 * way + 32, :] = got[:, :128].astype(BF16).reshape(PLANE, SLOTS, 128)
        tail = widen(got[:, 128:])
        if way == 1:
            tail = ysend[step, :, 32:64, :].reshape(256, 128).astype(F32) + pltpu.roll(tail, 64, 1)
        ysend[step, :, 32:64, :] = tail.astype(BF16).reshape(PLANE, SLOTS, 128)

    def pick(step, way):
        slot = at(way, step)
        put(step, way, select(ring.at[slot], ringi.at[slot]))

    def last_rows(way, columns):
        wants = beyond(way)
        got = dot_nt(farsel[way], ring[at(way, reach), columns, :])
        counts = [want[3] for want in wants] + [PLANE]
        at_row, at_sum, found = 0, SLOTS * sum(counts), []
        for count in counts:
            found.append((got[at_row:at_row + SLOTS * count, :], got[at_sum:at_sum + 4 * count, :]))
            at_row, at_sum = at_row + SLOTS * count, at_sum + 4 * count
        return wants, found[:-1], found[-1]

    def send_late(wants, found, part):
        for (kind, plane, first, count), (rows, sums) in zip(wants, found):
            rows = rows + spread(sums)
            if part == 0:
                lsend[kind, first:first + count, 0:32, :] = rows.astype(BF16).reshape(count, SLOTS, 128)
            else:
                tail = widen(rows).reshape(count, 2, 16, 128)
                tail = tail[:, 0].reshape(16 * count, 128) + pltpu.roll(tail[:, 1].reshape(16 * count, 128), 64, 1)
                lsend[kind, first:first + count, 32:48, :] = tail.astype(BF16).reshape(count, 16, 128)
            for o in range(count):
                lcopy(kind, plane, first + (me + o) % count, part).start()

    def send(step, first=0, rows=96, sem=None):
        for o in (4, 5, 3, 2, 6, 1, 7):
            ycopy(step, o, first, rows, step if sem is None else sem).start()
        yrecv[step, me, first:first + rows, :] = ysend[step, me, first:first + rows, :]

    def placement(zz, sums=False):
        to = tgt[pl.ds(zz, 1), :]
        lane = iota((1, 256), 1) % SLOTS
        if sums:
            for j in range(4):
                to = jnp.where(lane == 28 + j, hub_local[0:1, j:j + 1].astype(F32), to)
        pos = iota((256, 512), 0)
        slot = pos % SLOTS
        hub = jnp.where((slot >= 24) & (slot < 28), zz * 32 + (pos // SLOTS) * 4 + slot - 24, -1)
        where = dot_nt(hub_hot[...], hot(hub == hub_s[...]))
        return (where + jnp.where(iota((512, 256), 0).astype(F32) == to, 1.0, 0.0)).astype(BF16)

    def place(step, way):
        rows = jnp.concatenate([yrecv[step, :, 64 * way:64 * way + 32, :].reshape(256, 128),
                                yrecv[step, :, 32:64, :].reshape(256, 128)], axis=1)
        acc = accp if way == 0 else accm
        acc[...] += dot(placement(at(way, step)), rows)

    def product(i, part):
        w = pl.multiple_of(i * WIDTH, 64)
        if part == 0:
            carry[...] += dot(xm[i, 0:512, :], wn[pl.ds(w, 128), :])
        else:
            b, zero = wn[pl.ds(w + 128, 64), :], jnp.zeros((64, 256), BF16)
            carry[0:256, :] += dot(xm[i, 512:768, :], jnp.concatenate([b, zero], axis=0))
            carry[256:512, :] += dot(xm[i, 512:768, :], jnp.concatenate([zero, b], axis=0))

    for load in loads[:4]:
        load.wait()
    raw[0:24, :] = (cs[...] - SHIFT).astype(F32)
    row = iota((8, 128), 0)
    hubs = jnp.full((8, 128), 640, I32)
    for j in range(4):
        hubs = jnp.where(row == j, hub_local[0:1, j:j + 1], hubs)
    raw[24:32, :] = (hubs - SHIFT).astype(F32)
    raw[32:36, :] = (mirror_f[...] - SHIFT).astype(F32)
    raw[36:40, :] = (mirror_t[...] - SHIFT).astype(F32)
    raw[40:48, :] = jnp.zeros((8, 128), F32)
    own[...] = raw[...].astype(BF16)

    pl.semaphore_wait(barrier, PLANE * (2 * DIRECT) - 1 + feats - 1)
    for piece in order:
        for way in (0, 1):
            zcopy(way, 0, piece).start()
    for o in range(1, feats):
        fcopy(o).start()

    for load in loads[4:]:
        load.wait()
    accp[...] = jnp.zeros_like(accp)
    accm[...] = jnp.zeros_like(accm)
    accl[...] = jnp.zeros_like(accl)
    msum[...] = jnp.zeros_like(msum)

    ysend[0, :, 64:96, :] = jnp.zeros((PLANE, SLOTS, 128), BF16)
    put(0, 0, select(ft, own))
    send(0)

    raw[0:24, :] = ct[...].astype(F32)
    raw[24:48, :] = jnp.full((24, 128), -1.0, F32)
    wide = jnp.transpose(jnp.concatenate([raw[0:32, :], jnp.full((96, 128), -1.0, F32)], axis=0))
    wide = wide[0:rings * PLANE, :].reshape(rings, PLANE, 128)
    lane = iota((rings, 128), 1)
    for part in (0, 1):
        whole = jnp.full((rings, 128), -1.0, F32)
        for d in range(4):
            one = wide[:, 4 * part + d, :]
            whole = jnp.where(lane // SLOTS == d, pltpu.roll(one, SLOTS * d, 1) if d else one, whole)
        tgt[:, 128 * part:128 * part + 128] = whole
    hub_hot[...] = hot(iota((512, 512), 0) == hub_t[...])
    row, col = iota((256, 32), 0), iota((256, 32), 1)
    spot[...] = hot((row // SLOTS == col // 4) & (row % SLOTS == 28 + col % 4))

    def tiles(first, last):
        for t in range(first, last):
            is_at = [[(tidx[i:i + 1, t:t + 1] == b).astype(F32) for b in range(4)] for i in (0, 1)]
            block = sum(ft[:, 128 * b:128 * b + 128].astype(F32) * is_at[1][b] for b in range(4)).astype(BF16)
            part = dot_nt(mask[t].astype(F32).astype(BF16), block)
            for b in range(4):
                accl[128 * b:128 * b + 128, 0:WIDTH] += part * is_at[0][b]

    def last_place(i):
        if i < 2:
            places[:, 256 * i:256 * i + 256] = placement(at(i, reach), i == 0)
        elif i < 2 + len(kinds):
            d, way = kinds[i - 2]
            places[:, 256 * i:256 * i + 256] = placement(at(way, d), True)
        else:
            places[:, 256 * i:256 * i + 256] = placement(at(i - 2 - len(kinds), reach - 1))

    tiles(0, 3)
    forward(1, order[0:2])
    tiles(3, 6)
    forward(1, order[2:3])
    tiles(6, 9)
    forward(1, order[3:4])
    tiles(9, 12)
    forward(1, order[4:5])
    last_place(0)
    last_place(1)
    forward(1, order[5:6])
    last_place(2)
    forward(1, order[6:7])
    for i in range(3, 4 + len(kinds)):
        last_place(i)

    deg_row = deg[...].astype(F32)
    for i in range(4):
        degree[128 * i:128 * i + 128, :] = column(deg_row[i:i + 1, :])

    def own_columns(o):
        i = (x + o) % feats
        if isinstance(o, int) and o == 0:
            xf[x] = ft[...]
            carry[...] = jnp.zeros_like(carry) + bias[...]
        else:
            farrived(o)
        carry[...] += dot_tn(xf[i], ws[pl.ds(pl.multiple_of(i * WIDTH, 64), WIDTH), :])

    own_columns(0)

    def step(k, _):
        forward(k, order[:2])
        pick(k - 1, 0)
        forward(k, order[2:4])
        pick(k - 1, 1)
        forward(k, order[4:5])
        send(k - 1)
        forward(k, order[5:6])

        @pl.when(k >= 3)
        def _():
            yarrived(k - 3)
            place(k - 3, 0)
        forward(k, order[6:7])

        @pl.when(k >= 3)
        def _():
            place(k - 3, 1)

        @pl.when(k - 1 < feats)
        def _():
            own_columns(k - 1)
        return 0

    lax.fori_loop(2, reach, step, 0)
    for o in range(max(1, reach - 1), feats):
        own_columns(o)

    k = reach
    pick(k - 1, 0)
    pick(k - 1, 1)
    send(k - 1)
    for way in (0, 1):
        zarrived(way, k, PIECES)
        farsel[way] = selector(ringi.at[at(way, k)], [want[1:] for want in beyond(way)] + [(z, 0, PLANE)])
    for s in range(max(0, k - 3), k - 1):
        yarrived(s)
        place(s, 0)
        place(s, 1)
    lead, rest, split = slice(0, 128), slice(128, WIDTH), 128 // PIECE
    near = []
    for way in (0, 1):
        for piece in range(split):
            zarrived(way, k, piece)
        wants, found, own_plane = last_rows(way, lead)
        send_late(wants, found, 0)
        near.append(own_plane)
    sums = msum[:, lead] + near[0][1] + near[1][1]
    ysend[k, :, 0:32, :] = (near[0][0] + spread(sums)).astype(BF16).reshape(PLANE, SLOTS, 128)
    ysend[k, :, 32:64, :] = near[1][0].astype(BF16).reshape(PLANE, SLOTS, 128)
    send(k, 0, 64)
    near = []
    for way in (0, 1):
        for piece in range(split, PIECES):
            zarrived(way, k, piece)
        wants, found, own_plane = last_rows(way, rest)
        send_late(wants, found, 1)
        near.append(own_plane)
    sums = msum[:, rest] + near[0][1] + near[1][1]
    tail = widen(near[0][0] + spread(sums)) + pltpu.roll(widen(near[1][0]), 64, 1)
    ysend[k, :, 64:96, :] = tail.astype(BF16).reshape(PLANE, SLOTS, 128)
    send(k, 64, 32, k + 1)
    yarrived(k - 1)
    zsent()
    for s in range(reach):
        yall(s).wait_send()
    for o in range(1, feats):
        fcopy(o).wait_send()

    before = accp[:, lead] + accm[:, lead] + accl[:, lead]
    yarrived(k, 0, 64)
    lall(0).wait_recv()
    rows = jnp.concatenate([yrecv[k, :, 0:32, :].reshape(256, 128), yrecv[k, :, 32:64, :].reshape(256, 128)]
                           + [lrecv[kind, :, 0:32, :].reshape(256, 128) for kind in range(len(kinds))]
                           + [yrecv[k - 1, :, 64 * way:64 * way + 32, :].reshape(256, 128) for way in (0, 1)], axis=0)
    xm[x, 0:512, :] = ((before + dot(places[...], rows)) / degree[...]).astype(BF16)
    sent = []

    def tell(first):
        for part, o in ((0, 1), (1, -1), (1, 1), (0, -1)) if feats == 4 else [(p, o) for o in range(1, feats) for p in (0, 1)]:
            sent.append(mcopy(x, first + part, o, len(sent)))
            sent[-1].start()

    def relay(o, part):
        marrived(-o, part)
        sent.append(mcopy((x - o + feats) % feats, part, o, len(sent)))
        sent[-1].start()

    def done():
        lall(0).wait_send()
        lall(1).wait_send()
        yall(k, 0, 64, k).wait_send()
        yall(k, 64, 32, k + 1).wait_send()

    tell(0)
    product(x, 0)

    before = accp[:, 128:256] + pltpu.roll(accm[:, 128:256], 64, 1) + accl[:, 128:256]
    yarrived(k, 64, 32, k + 1)
    lall(1).wait_recv()
    both = yrecv[k, :, 64:96, :].reshape(256, 128)
    rows = [both, pltpu.roll(both.astype(F32), 64, 1).astype(BF16)]
    for kind in range(len(kinds)):
        tail = lrecv[kind, :, 32:48, :].astype(F32).reshape(128, 128)
        tail = jnp.concatenate([tail.reshape(PLANE, 1, 16, 128), pltpu.roll(tail, 64, 1).reshape(PLANE, 1, 16, 128)], axis=1)
        rows.append(tail.astype(BF16).reshape(256, 128))
    both = yrecv[k - 1, :, 32:64, :].reshape(256, 128)
    rows += [both, pltpu.roll(both.astype(F32), 64, 1).astype(BF16)]
    mean = (before + dot(places[...], jnp.concatenate(rows, axis=0))) / degree[...]
    xm[x, 512:768, :] = jnp.where(low, mean[0:256, :], pltpu.roll(mean[256:512, :], 64, 1)).astype(BF16)
    tell(2)
    if feats == 4:
        relay(1, 0)
        relay(-1, 1)
        relay(1, 2)
        relay(-1, 3)
        product(x, 1)
        done()
        marrived(-1, 1)
        product((x + 3) % 4, 0)
        marrived(1, 0)
        product((x + 1) % 4, 0)
        marrived(-1, 3)
        product((x + 3) % 4, 1)
        marrived(1, 2)
        product((x + 1) % 4, 1)
        marrived(2, 0)
        marrived(2, 1)
        product((x + 2) % 4, 0)
        marrived(2, 2)
        marrived(2, 3)
        product((x + 2) % 4, 1)
    else:
        product(x, 1)
        done()
        for o in range(1, feats):
            for part in range(4):
                marrived(o, part)
            product((x + o) % feats, 0)
            product((x + o) % feats, 1)
    out[...] = jnp.maximum(carry[...], 0.0).astype(BF16)

    for copy in sent:
        copy.wait_send()


def on_device(rings, feats, features, w_self, w_neigh, out_bias, degrees, tile_index, tile_mask, cut_source, cut_target,
              hub_local, hub_source, hub_target, mirror_source, mirror_target):
    half = rings // 2
    reach = half - DIRECT
    parts = rings * PLANE
    anywhere = pl.BlockSpec(memory_space=pl.ANY)
    args = (features.T, cut_source[0].T, cut_target[0].T, tile_index[0].T, hub_local, hub_target, hub_source,
            mirror_source.reshape(4, 128), mirror_target.reshape(4, 128), degrees.reshape(4, 128), out_bias.reshape(1, 256),
            tile_mask[0], w_self, w_neigh)
    if parts < 128:
        args = args[:1] + tuple(jnp.pad(a, ((0, 0), (0, 128 - parts))) for a in args[1:3]) + args[3:]
    return pl.pallas_call(
        functools.partial(kernel, rings, feats),
        out_shape=pltpu.VMEM((512, 256), BF16),
        in_specs=[anywhere] * len(args),
        out_specs=pl.BlockSpec(memory_space=pltpu.VMEM),
        scratch_shapes=[
            pltpu.VMEM((rings, WIDTH, 512), BF16),
            pltpu.VMEM((rings, IDS, 128), BF16),
            pltpu.VMEM((reach + 1, PLANE, 96, 128), BF16),
            pltpu.VMEM((reach + 1, PLANE, 96, 128), BF16),
            pltpu.VMEM((2 * DIRECT - 1, PLANE, 48, 128), BF16),
            pltpu.VMEM((2 * DIRECT - 1, PLANE, 48, 128), BF16),
            pltpu.VMEM((feats, WIDTH, 512), BF16),
            pltpu.VMEM((feats, 768, 128), BF16),
            pltpu.VMEM((512, 256), F32),
            pltpu.VMEM((512, 256), F32),
            pltpu.VMEM((512, 256), F32),
            pltpu.VMEM((32, 256), F32),
            pltpu.VMEM((512, 512), BF16),
            pltpu.VMEM((2, 36 * (8 * DIRECT + 4), 512), BF16),
            pltpu.VMEM((512, 256 * (2 * DIRECT + 3)), BF16),
            pltpu.VMEM((512, 128), F32),
            pltpu.VMEM((256, 32), BF16),
            pltpu.VMEM((512, 256), F32),
            pltpu.VMEM((IDS, 128), BF16),
            pltpu.VMEM((rings, 256), F32),
            pltpu.VMEM((IDS, 128), F32),
        ] + [pltpu.VMEM(a.shape, a.dtype) for a in args] + [
            pltpu.SemaphoreType.DMA((2,)),
            pltpu.SemaphoreType.DMA((rings, PIECES + 1)),
            pltpu.SemaphoreType.DMA((reach + 2,)),
            pltpu.SemaphoreType.DMA((reach + 2,)),
            pltpu.SemaphoreType.DMA((2,)),
            pltpu.SemaphoreType.DMA((2,)),
            pltpu.SemaphoreType.DMA((4,)),
            pltpu.SemaphoreType.DMA((4,)),
            pltpu.SemaphoreType.DMA((12,)),
            pltpu.SemaphoreType.DMA((4, 4)),
            pltpu.SemaphoreType.DMA((len(args),)),
        ],
        compiler_params=pltpu.CompilerParams(
            collective_id=0, has_side_effects=True, vmem_limit_bytes=60 * 1024 * 1024),
        cost_estimate=pl.CostEstimate(flops=10**10, bytes_accessed=4 * 10**6, transcendentals=0),
    )(*args)


def solution(mesh):
    return jax.shard_map(
        functools.partial(on_device, mesh.shape["dom"] // PLANE, mesh.shape["feat"]),
        mesh=mesh,
        in_specs=(P("dom", "feat"), P(None, "feat"), P(None, "feat"), P("feat"), P("dom"), P("dom"), P("dom"), P("dom"),
                  P("dom"), P("dom"), P("dom"), P("dom"), P("dom"), P("dom")),
        out_specs=P("dom", "feat"),
        check_vma=False,
    )
```

```python
import functools

import jax
import jax.numpy as jnp
from jax import lax
from jax.experimental import pallas as pl
from jax.experimental.pallas import tpu as pltpu
from jax.sharding import PartitionSpec as P

MESH = pl.DeviceIdType.MESH
BF16, F32, I32 = jnp.bfloat16, jnp.float32, jnp.int32
PLANE = 8
SLOTS = 32
WIDTH = 192
PIECES, PIECE = 6, 32
IDS = 48
DIRECT = 2
SHIFT = 256


def dot(a, b):
    return jnp.dot(a, b, preferred_element_type=F32)


def dot_nt(a, b):
    return lax.dot_general(a, b, (((1,), (1,)), ((), ())), preferred_element_type=F32)


def iota(shape, axis):
    return lax.broadcasted_iota(I32, shape, axis)


def hot(mask):
    return jnp.where(mask, 1.0, 0.0).astype(BF16)


def column(row):
    return jnp.transpose(jnp.broadcast_to(row, (128, 128)))


def dot_tn(a, b):
    return lax.dot_general(a, b, (((0,), (0,)), ((), ())), preferred_element_type=F32)


def kernel(rings, feats, ft_hbm, cs_hbm, ct_hbm, ti_hbm, hl_hbm, ht_hbm, hs_hbm, mf_hbm, mt_hbm, deg_hbm, bias_hbm,
           mask_hbm, ws_hbm, wn_hbm, out, ring, ringi, ysend, yrecv, lsend, lrecv, xf, xm, accp, accm, accl, msum, hub_hot, farsel, places, degree, spot, carry,
           own, tgt, raw, ft, cs, ct, tidx, hub_local, hub_t, hub_s, mirror_f, mirror_t, deg, bias, mask, ws, wn,
           zs, zr, ys, yr, ls, lr, fs, fr, ms, mr, local):
    half = rings // 2
    reach = half - DIRECT
    dom, x = lax.axis_index("dom"), lax.axis_index("feat")
    z, me = dom // PLANE, dom % PLANE
    up, down = ((z + 1) % rings) * PLANE + me, ((z + rings - 1) % rings) * PLANE + me

    barrier = pltpu.get_barrier_semaphore()
    def greet(plane, dest):
        pl.semaphore_signal(barrier, inc=1, device_id=(plane * PLANE + dest, x), device_id_type=MESH)

    for o in range(PLANE):
        if o:
            greet(z, (me + o) % PLANE)
        if DIRECT > 1:
            greet((z + 1) % rings, (me + o) % PLANE)
            greet((z + rings - 1) % rings, (me + o) % PLANE)
        greet((z + rings - DIRECT + 2 * DIRECT * (me // 4)) % rings, (me + o) % PLANE)
    for o in range(1, feats):
        pl.semaphore_signal(barrier, inc=1, device_id=(dom, (x + o) % feats), device_id_type=MESH)

    loads = [pltpu.make_async_copy(src, dst, local.at[i]) for i, (src, dst) in enumerate((
        (cs_hbm, cs), (hl_hbm, hub_local), (mf_hbm, mirror_f), (mt_hbm, mirror_t), (ft_hbm, ft), (ct_hbm, ct), (ti_hbm, tidx),
        (ht_hbm, hub_t), (hs_hbm, hub_s), (deg_hbm, deg), (bias_hbm, bias), (mask_hbm, mask), (ws_hbm, ws), (wn_hbm, wn)))]
    for load in loads:
        load.start()

    def at(way, step):
        return (z + rings - step) % rings if way == 0 else (z + step) % rings

    def zcopy(way, step, piece):
        slot = at(way, step)
        if piece == PIECES:
            src, dst = own if isinstance(step, int) and step == 0 else ringi.at[slot], ringi.at[slot]
        else:
            rows = pl.ds(piece * PIECE, PIECE)
            src = ft_hbm.at[rows] if isinstance(step, int) and step == 0 else ring.at[slot, rows]
            dst = ring.at[slot, rows]
        return pltpu.make_async_remote_copy(
            src_ref=src, dst_ref=dst, send_sem=zs.at[piece // PIECES], recv_sem=zr.at[slot, piece],
            device_id=(up if way == 0 else down, x), device_id_type=MESH)

    def zarrived(way, step, piece):
        slot = at(way, step)
        ref = ringi.at[slot] if piece == PIECES else ring.at[slot, pl.ds(piece * PIECE, PIECE)]
        pltpu.make_async_remote_copy(
            src_ref=ref, dst_ref=ref, send_sem=zs.at[0], recv_sem=zr.at[slot, piece],
            device_id=(up, x), device_id_type=MESH).wait_recv()

    order = (PIECES,) + tuple(range(PIECES))

    def zsent():
        for buf, sem in ((ring, 0), (ringi, 1)):
            ref = buf.at[pl.ds(0, 2 * reach)]
            pltpu.make_async_remote_copy(
                src_ref=ref, dst_ref=ref, send_sem=zs.at[sem], recv_sem=zr.at[0, 0],
                device_id=(up, x), device_id_type=MESH).wait_send()

    def forward(step, pieces):
        for piece in pieces:
            for way in (0, 1):
                zarrived(way, step, piece)
                zcopy(way, step, piece).start()

    def ycopy(step, o, first, rows, sem):
        dest = (me + o) % PLANE
        return pltpu.make_async_remote_copy(
            src_ref=ysend.at[step, dest, pl.ds(first, rows)], dst_ref=yrecv.at[step, me, pl.ds(first, rows)],
            send_sem=ys.at[sem], recv_sem=yr.at[sem],
            device_id=(z * PLANE + dest, x), device_id_type=MESH)

    def yall(step, first=0, rows=96, sem=None):
        sem = step if sem is None else sem
        return pltpu.make_async_remote_copy(
            src_ref=ysend.at[step, pl.ds(0, PLANE - 1), pl.ds(first, rows)],
            dst_ref=yrecv.at[step, pl.ds(0, PLANE - 1), pl.ds(first, rows)],
            send_sem=ys.at[sem], recv_sem=yr.at[sem], device_id=(up, x), device_id_type=MESH)

    def yarrived(step, first=0, rows=96, sem=None):
        yall(step, first, rows, sem).wait_recv()

    kinds = [(d, way) for d in range(reach + 1, half) for way in (0, 1)] + [(half, 0)]

    def beyond(way):
        wants = []
        for d in range(reach + 1, half + 1):
            plane = (z + d - reach) % rings if way == 0 else (z + rings - d + reach) % rings
            wants.append((kinds.index((d, way)), plane, 0, 8) if d < half else (len(kinds) - 1, plane, 4 * way, 4))
        return wants

    late = (pl.ds(0, 32), pl.ds(32, 16))

    def lcopy(kind, plane, dest, part):
        return pltpu.make_async_remote_copy(
            src_ref=lsend.at[kind, dest, late[part]], dst_ref=lrecv.at[kind, me, late[part]],
            send_sem=ls.at[part], recv_sem=lr.at[part],
            device_id=(plane * PLANE + dest, x), device_id_type=MESH)

    def lall(part):
        return pltpu.make_async_remote_copy(
            src_ref=lsend.at[:, :, late[part]], dst_ref=lrecv.at[:, :, late[part]], send_sem=ls.at[part], recv_sem=lr.at[part],
            device_id=(up, x), device_id_type=MESH)

    def fcopy(o):
        return pltpu.make_async_remote_copy(
            src_ref=ft_hbm, dst_ref=xf.at[x], send_sem=fs.at[o - 1], recv_sem=fr.at[x],
            device_id=(dom, (x + o) % feats), device_id_type=MESH)

    def farrived(o):
        src = (x + o) % feats
        pltpu.make_async_remote_copy(
            src_ref=ft_hbm, dst_ref=xf.at[src], send_sem=fs.at[o - 1], recv_sem=fr.at[src],
            device_id=(dom, src), device_id_type=MESH).wait_recv()

    parts = (pl.ds(0, 256), pl.ds(256, 256), pl.ds(512, 128), pl.ds(640, 128))

    def mcopy(src, part, o, sem):
        return pltpu.make_async_remote_copy(
            src_ref=xm.at[src, parts[part]], dst_ref=xm.at[src, parts[part]], send_sem=ms.at[sem], recv_sem=mr.at[src, part],
            device_id=(dom, (x + o + feats) % feats), device_id_type=MESH)

    def marrived(o, part):
        mcopy((x + o + feats) % feats, part, 1, 0).wait_recv()

    def selector(idref, wants):
        ids = idref[0:32, :].astype(F32)
        lane = iota((32, 512), 1).astype(F32) - SHIFT
        edges = idref[32:48, :].astype(F32)
        node = (iota((512, 128), 0) - SHIFT).astype(F32)
        fro = jnp.concatenate([hot(node == edges[c:c + 1, :]) for c in range(4)], axis=1)
        picks, tos = [], []
        for plane, first, count in wants:
            here = pltpu.roll(ids, (128 - PLANE * plane) % 128, 1)
            picks += [hot(here[:, d:d + 1] == lane) for d in range(first, first + count)]
            hub = (iota((4 * count, 128), 0) + plane * 32 + 4 * first - SHIFT).astype(F32)
            tos.append(jnp.concatenate([hot(hub == edges[4 + c:5 + c, :]) for c in range(4)], axis=1))
        return jnp.concatenate(picks + [dot_nt(jnp.concatenate(tos, axis=0), fro).astype(BF16)], axis=0)

    def select(ref, idref):
        got = dot_nt(selector(idref, [(z, 0, PLANE)]), ref[...])
        msum[:, 0:WIDTH] += got[256:288, :]
        return got[0:256, :]

    def spread(sums):
        count = sums.shape[0] // 4
        return dot(spot[0:SLOTS * count, 0:4 * count], sums.astype(BF16))

    def widen(tail):
        return jnp.concatenate([tail, jnp.zeros_like(tail)], axis=1)

    low = iota((256, 128), 1) < 64

    def put(step, way, got):
        ysend[step, :, 64 * way:64 * way + 32, :] = got[:, :128].astype(BF16).reshape(PLANE, SLOTS, 128)
        tail = widen(got[:, 128:])
        if way == 1:
            tail = ysend[step, :, 32:64, :].reshape(256, 128).astype(F32) + pltpu.roll(tail, 64, 1)
        ysend[step, :, 32:64, :] = tail.astype(BF16).reshape(PLANE, SLOTS, 128)

    def pick(step, way):
        slot = at(way, step)
        put(step, way, select(ring.at[slot], ringi.at[slot]))

    def last_rows(way, columns):
        wants = beyond(way)
        got = dot_nt(farsel[way], ring[at(way, reach), columns, :])
        counts = [want[3] for want in wants] + [PLANE]
        at_row, at_sum, found = 0, SLOTS * sum(counts), []
        for count in counts:
            found.append((got[at_row:at_row + SLOTS * count, :], got[at_sum:at_sum + 4 * count, :]))
            at_row, at_sum = at_row + SLOTS * count, at_sum + 4 * count
        return wants, found[:-1], found[-1]

    def send_late(wants, found, part):
        for (kind, plane, first, count), (rows, sums) in zip(wants, found):
            rows = rows + spread(sums)
            if part == 0:
                lsend[kind, first:first + count, 0:32, :] = rows.astype(BF16).reshape(count, SLOTS, 128)
            else:
                tail = widen(rows).reshape(count, 2, 16, 128)
                tail = tail[:, 0].reshape(16 * count, 128) + pltpu.roll(tail[:, 1].reshape(16 * count, 128), 64, 1)
                lsend[kind, first:first + count, 32:48, :] = tail.astype(BF16).reshape(count, 16, 128)
            for o in range(count):
                lcopy(kind, plane, first + (me + o) % count, part).start()

    def send(step, first=0, rows=96, sem=None):
        for o in (4, 5, 3, 2, 6, 1, 7):
            ycopy(step, o, first, rows, step if sem is None else sem).start()
        yrecv[step, me, first:first + rows, :] = ysend[step, me, first:first + rows, :]

    def placement(zz, sums=False):
        to = tgt[pl.ds(zz, 1), :]
        lane = iota((1, 256), 1) % SLOTS
        if sums:
            for j in range(4):
                to = jnp.where(lane == 28 + j, hub_local[0:1, j:j + 1].astype(F32), to)
        pos = iota((256, 512), 0)
        slot = pos % SLOTS
        hub = jnp.where((slot >= 24) & (slot < 28), zz * 32 + (pos // SLOTS) * 4 + slot - 24, -1)
        where = dot_nt(hub_hot[...], hot(hub == hub_s[...]))
        return (where + jnp.where(iota((512, 256), 0).astype(F32) == to, 1.0, 0.0)).astype(BF16)

    def place(step, way):
        rows = jnp.concatenate([yrecv[step, :, 64 * way:64 * way + 32, :].reshape(256, 128),
                                yrecv[step, :, 32:64, :].reshape(256, 128)], axis=1)
        acc = accp if way == 0 else accm
        acc[...] += dot(placement(at(way, step)), rows)

    def product(i, part):
        w = pl.multiple_of(i * WIDTH, 64)
        if part == 0:
            carry[...] += dot(xm[i, 0:512, :], wn[pl.ds(w, 128), :])
        else:
            b, zero = wn[pl.ds(w + 128, 64), :], jnp.zeros((64, 256), BF16)
            carry[0:256, :] += dot(xm[i, 512:768, :], jnp.concatenate([b, zero], axis=0))
            carry[256:512, :] += dot(xm[i, 512:768, :], jnp.concatenate([zero, b], axis=0))

    for load in loads[:4]:
        load.wait()
    raw[0:24, :] = (cs[...] - SHIFT).astype(F32)
    row = iota((8, 128), 0)
    hubs = jnp.full((8, 128), 640, I32)
    for j in range(4):
        hubs = jnp.where(row == j, hub_local[0:1, j:j + 1], hubs)
    raw[24:32, :] = (hubs - SHIFT).astype(F32)
    raw[32:36, :] = (mirror_f[...] - SHIFT).astype(F32)
    raw[36:40, :] = (mirror_t[...] - SHIFT).astype(F32)
    raw[40:48, :] = jnp.zeros((8, 128), F32)
    own[...] = raw[...].astype(BF16)

    pl.semaphore_wait(barrier, PLANE * (2 * DIRECT) - 1 + feats - 1)
    for piece in order:
        for way in (0, 1):
            zcopy(way, 0, piece).start()
    for o in range(1, feats):
        fcopy(o).start()

    for load in loads[4:]:
        load.wait()
    accp[...] = jnp.zeros_like(accp)
    accm[...] = jnp.zeros_like(accm)
    accl[...] = jnp.zeros_like(accl)
    msum[...] = jnp.zeros_like(msum)

    ysend[0, :, 64:96, :] = jnp.zeros((PLANE, SLOTS, 128), BF16)
    put(0, 0, select(ft, own))
    send(0)

    raw[0:24, :] = ct[...].astype(F32)
    raw[24:48, :] = jnp.full((24, 128), -1.0, F32)
    wide = jnp.transpose(jnp.concatenate([raw[0:32, :], jnp.full((96, 128), -1.0, F32)], axis=0))
    wide = wide[0:rings * PLANE, :].reshape(rings, PLANE, 128)
    lane = iota((rings, 128), 1)
    for part in (0, 1):
        whole = jnp.full((rings, 128), -1.0, F32)
        for d in range(4):
            one = wide[:, 4 * part + d, :]
            whole = jnp.where(lane // SLOTS == d, pltpu.roll(one, SLOTS * d, 1) if d else one, whole)
        tgt[:, 128 * part:128 * part + 128] = whole
    hub_hot[...] = hot(iota((512, 512), 0) == hub_t[...])
    row, col = iota((256, 32), 0), iota((256, 32), 1)
    spot[...] = hot((row // SLOTS == col // 4) & (row % SLOTS == 28 + col % 4))

    def tiles(first, last):
        for t in range(first, last):
            is_at = [[(tidx[i:i + 1, t:t + 1] == b).astype(F32) for b in range(4)] for i in (0, 1)]
            block = sum(ft[:, 128 * b:128 * b + 128].astype(F32) * is_at[1][b] for b in range(4)).astype(BF16)
            part = dot_nt(mask[t].astype(F32).astype(BF16), block)
            for b in range(4):
                accl[128 * b:128 * b + 128, 0:WIDTH] += part * is_at[0][b]

    def last_place(i):
        if i < 2:
            places[:, 256 * i:256 * i + 256] = placement(at(i, reach), i == 0)
        elif i < 2 + len(kinds):
            d, way = kinds[i - 2]
            places[:, 256 * i:256 * i + 256] = placement(at(way, d), True)
        else:
            places[:, 256 * i:256 * i + 256] = placement(at(i - 2 - len(kinds), reach - 1))

    tiles(0, 3)
    forward(1, order[0:2])
    tiles(3, 6)
    forward(1, order[2:3])
    tiles(6, 9)
    forward(1, order[3:4])
    tiles(9, 12)
    forward(1, order[4:5])
    last_place(0)
    last_place(1)
    forward(1, order[5:6])
    last_place(2)
    forward(1, order[6:7])
    for i in range(3, 4 + len(kinds)):
        last_place(i)

    deg_row = deg[...].astype(F32)
    for i in range(4):
        degree[128 * i:128 * i + 128, :] = column(deg_row[i:i + 1, :])

    def own_columns(o):
        i = (x + o) % feats
        if isinstance(o, int) and o == 0:
            xf[x] = ft[...]
            carry[...] = jnp.zeros_like(carry) + bias[...]
        else:
            farrived(o)
        carry[...] += dot_tn(xf[i], ws[pl.ds(pl.multiple_of(i * WIDTH, 64), WIDTH), :])

    own_columns(0)

    def step(k, _):
        forward(k, order[:2])
        pick(k - 1, 0)
        forward(k, order[2:4])
        pick(k - 1, 1)
        forward(k, order[4:5])
        send(k - 1)
        forward(k, order[5:6])

        @pl.when(k >= 3)
        def _():
            yarrived(k - 3)
            place(k - 3, 0)
        forward(k, order[6:7])

        @pl.when(k >= 3)
        def _():
            place(k - 3, 1)

        @pl.when(k - 1 < feats)
        def _():
            own_columns(k - 1)
        return 0

    lax.fori_loop(2, reach, step, 0)
    for o in range(max(1, reach - 1), feats):
        own_columns(o)

    k = reach
    pick(k - 1, 0)
    pick(k - 1, 1)
    send(k - 1)
    for way in (0, 1):
        zarrived(way, k, PIECES)
        farsel[way] = selector(ringi.at[at(way, k)], [want[1:] for want in beyond(way)] + [(z, 0, PLANE)])
    lead, rest, split = slice(0, 128), slice(128, WIDTH), 128 // PIECE
    near = []
    for way in (0, 1):
        for piece in range(split):
            zarrived(way, k, piece)
        wants, found, own_plane = last_rows(way, lead)
        send_late(wants, found, 0)
        near.append(own_plane)
    sums = msum[:, lead] + near[0][1] + near[1][1]
    ysend[k, :, 0:32, :] = (near[0][0] + spread(sums)).astype(BF16).reshape(PLANE, SLOTS, 128)
    ysend[k, :, 32:64, :] = near[1][0].astype(BF16).reshape(PLANE, SLOTS, 128)
    send(k, 0, 64)
    near = []
    for way in (0, 1):
        for piece in range(split, PIECES):
            zarrived(way, k, piece)
        wants, found, own_plane = last_rows(way, rest)
        send_late(wants, found, 1)
        near.append(own_plane)
    sums = msum[:, rest] + near[0][1] + near[1][1]
    tail = widen(near[0][0] + spread(sums)) + pltpu.roll(widen(near[1][0]), 64, 1)
    ysend[k, :, 64:96, :] = tail.astype(BF16).reshape(PLANE, SLOTS, 128)
    send(k, 64, 32, k + 1)
    for s in range(max(0, k - 3), k - 1):
        yarrived(s)
        place(s, 0)
        place(s, 1)
    yarrived(k - 1)
    zsent()
    for s in range(reach):
        yall(s).wait_send()
    for o in range(1, feats):
        fcopy(o).wait_send()

    before = accp[:, lead] + accm[:, lead] + accl[:, lead]
    yarrived(k, 0, 64)
    lall(0).wait_recv()
    rows = jnp.concatenate([yrecv[k, :, 0:32, :].reshape(256, 128), yrecv[k, :, 32:64, :].reshape(256, 128)]
                           + [lrecv[kind, :, 0:32, :].reshape(256, 128) for kind in range(len(kinds))]
                           + [yrecv[k - 1, :, 64 * way:64 * way + 32, :].reshape(256, 128) for way in (0, 1)], axis=0)
    xm[x, 0:512, :] = ((before + dot(places[...], rows)) / degree[...]).astype(BF16)
    sent = []

    def tell(first):
        for part, o in ((0, 1), (1, -1), (1, 1), (0, -1)) if feats == 4 else [(p, o) for o in range(1, feats) for p in (0, 1)]:
            sent.append(mcopy(x, first + part, o, len(sent)))
            sent[-1].start()

    def relay(o, part):
        marrived(-o, part)
        sent.append(mcopy((x - o + feats) % feats, part, o, len(sent)))
        sent[-1].start()

    def done():
        lall(0).wait_send()
        lall(1).wait_send()
        yall(k, 0, 64, k).wait_send()
        yall(k, 64, 32, k + 1).wait_send()

    tell(0)
    product(x, 0)

    before = accp[:, 128:256] + pltpu.roll(accm[:, 128:256], 64, 1) + accl[:, 128:256]
    yarrived(k, 64, 32, k + 1)
    lall(1).wait_recv()
    both = yrecv[k, :, 64:96, :].reshape(256, 128)
    rows = [both, pltpu.roll(both.astype(F32), 64, 1).astype(BF16)]
    for kind in range(len(kinds)):
        tail = lrecv[kind, :, 32:48, :].astype(F32).reshape(128, 128)
        tail = jnp.concatenate([tail.reshape(PLANE, 1, 16, 128), pltpu.roll(tail, 64, 1).reshape(PLANE, 1, 16, 128)], axis=1)
        rows.append(tail.astype(BF16).reshape(256, 128))
    both = yrecv[k - 1, :, 32:64, :].reshape(256, 128)
    rows += [both, pltpu.roll(both.astype(F32), 64, 1).astype(BF16)]
    mean = (before + dot(places[...], jnp.concatenate(rows, axis=0))) / degree[...]
    xm[x, 512:768, :] = jnp.where(low, mean[0:256, :], pltpu.roll(mean[256:512, :], 64, 1)).astype(BF16)
    tell(2)
    if feats == 4:
        relay(1, 0)
        relay(-1, 1)
        relay(1, 2)
        relay(-1, 3)
        product(x, 1)
        done()
        marrived(-1, 1)
        product((x + 3) % 4, 0)
        marrived(1, 0)
        product((x + 1) % 4, 0)
        marrived(-1, 3)
        product((x + 3) % 4, 1)
        marrived(1, 2)
        product((x + 1) % 4, 1)
        marrived(2, 0)
        marrived(2, 1)
        product((x + 2) % 4, 0)
        marrived(2, 2)
        marrived(2, 3)
        product((x + 2) % 4, 1)
    else:
        product(x, 1)
        done()
        for o in range(1, feats):
            for part in range(4):
                marrived(o, part)
            product((x + o) % feats, 0)
            product((x + o) % feats, 1)
    out[...] = jnp.maximum(carry[...], 0.0).astype(BF16)

    for copy in sent:
        copy.wait_send()


def on_device(rings, feats, features, w_self, w_neigh, out_bias, degrees, tile_index, tile_mask, cut_source, cut_target,
              hub_local, hub_source, hub_target, mirror_source, mirror_target):
    half = rings // 2
    reach = half - DIRECT
    parts = rings * PLANE
    anywhere = pl.BlockSpec(memory_space=pl.ANY)
    args = (features.T, cut_source[0].T, cut_target[0].T, tile_index[0].T, hub_local, hub_target, hub_source,
            mirror_source.reshape(4, 128), mirror_target.reshape(4, 128), degrees.reshape(4, 128), out_bias.reshape(1, 256),
            tile_mask[0], w_self, w_neigh)
    if parts < 128:
        args = args[:1] + tuple(jnp.pad(a, ((0, 0), (0, 128 - parts))) for a in args[1:3]) + args[3:]
    return pl.pallas_call(
        functools.partial(kernel, rings, feats),
        out_shape=pltpu.VMEM((512, 256), BF16),
        in_specs=[anywhere] * len(args),
        out_specs=pl.BlockSpec(memory_space=pltpu.VMEM),
        scratch_shapes=[
            pltpu.VMEM((rings, WIDTH, 512), BF16),
            pltpu.VMEM((rings, IDS, 128), BF16),
            pltpu.VMEM((reach + 1, PLANE, 96, 128), BF16),
            pltpu.VMEM((reach + 1, PLANE, 96, 128), BF16),
            pltpu.VMEM((2 * DIRECT - 1, PLANE, 48, 128), BF16),
            pltpu.VMEM((2 * DIRECT - 1, PLANE, 48, 128), BF16),
            pltpu.VMEM((feats, WIDTH, 512), BF16),
            pltpu.VMEM((feats, 768, 128), BF16),
            pltpu.VMEM((512, 256), F32),
            pltpu.VMEM((512, 256), F32),
            pltpu.VMEM((512, 256), F32),
            pltpu.VMEM((32, 256), F32),
            pltpu.VMEM((512, 512), BF16),
            pltpu.VMEM((2, 36 * (8 * DIRECT + 4), 512), BF16),
            pltpu.VMEM((512, 256 * (2 * DIRECT + 3)), BF16),
            pltpu.VMEM((512, 128), F32),
            pltpu.VMEM((256, 32), BF16),
            pltpu.VMEM((512, 256), F32),
            pltpu.VMEM((IDS, 128), BF16),
            pltpu.VMEM((rings, 256), F32),
            pltpu.VMEM((IDS, 128), F32),
        ] + [pltpu.VMEM(a.shape, a.dtype) for a in args] + [
            pltpu.SemaphoreType.DMA((2,)),
            pltpu.SemaphoreType.DMA((rings, PIECES + 1)),
            pltpu.SemaphoreType.DMA((reach + 2,)),
            pltpu.SemaphoreType.DMA((reach + 2,)),
            pltpu.SemaphoreType.DMA((2,)),
            pltpu.SemaphoreType.DMA((2,)),
            pltpu.SemaphoreType.DMA((4,)),
            pltpu.SemaphoreType.DMA((4,)),
            pltpu.SemaphoreType.DMA((12,)),
            pltpu.SemaphoreType.DMA((4, 4)),
            pltpu.SemaphoreType.DMA((len(args),)),
        ],
        compiler_params=pltpu.CompilerParams(
            collective_id=0, has_side_effects=True, vmem_limit_bytes=60 * 1024 * 1024),
        cost_estimate=pl.CostEstimate(flops=10**10, bytes_accessed=4 * 10**6, transcendentals=0),
    )(*args)


def solution(mesh):
    return jax.shard_map(
        functools.partial(on_device, mesh.shape["dom"] // PLANE, mesh.shape["feat"]),
        mesh=mesh,
        in_specs=(P("dom", "feat"), P(None, "feat"), P(None, "feat"), P("feat"), P("dom"), P("dom"), P("dom"), P("dom"),
                  P("dom"), P("dom"), P("dom"), P("dom"), P("dom"), P("dom")),
        out_specs=P("dom", "feat"),
        check_vma=False,
    )
```
